32 devices in a mesh: section: 2 (over core), seq: 4 (over z), wshard: 4 (over y, x).
Axes of the slice: x: 2, y: 2, z: 4, core: 2. Of those that a mesh axis runs over, the one named last changes fastest.
Arguments:
- ends_in: bfloat16 [2, 2, 4, 1024, 1024], P('section', None, 'wshard', 'seq'), may hold values from -6 to 6
- seq_lengths: int32 [2, 4, 4], P(None, 'wshard'), may hold values from 1 to 512, 1024 in all within a row
- deal_order: int32 [2, 4, 1024], P(None, 'wshard'), may hold values from 0 to 1023, each once within a row
- norm_w: float32 [2, 1024], P('section'), may hold values from 0.1 to 1.9
- in_w: bfloat16 [2, 1024, 4384], P('section', 'wshard'), may hold values from -0.1875 to 0.1875
- conv_w: float32 [2, 4, 2304], P('section'), may hold values from -3 to 3
- conv_b: float32 [2, 2304], P('section'), may hold values from -3 to 3
- dt_bias: float32 [2, 32], P('section'), may hold values from -5 to -3
- a_log: float32 [2, 32], P('section'), may hold values from -6 to 2
- d_skip: float32 [2, 32], P('section'), may hold values from 0.1 to 1.9
- gnorm_w: float32 [2, 2048], P('section'), may hold values from 0.1 to 1.9
- out_w: bfloat16 [2, 2048, 1024], P('section', 'wshard'), may hold values from -0.125 to 0.125
Outputs:
- ends_out: float32 [2, 2, 4, 1024, 1024], P('section', None, 'wshard', 'seq')
- g_norm_w: float32 [2, 1024], P('section')
- g_in_w: float32 [2, 1024, 4384], P('section', ('seq', 'wshard'))
- g_conv_w: float32 [2, 4, 2304], P('section')
- g_conv_b: float32 [2, 2304], P('section')
- g_dt_bias: float32 [2, 32], P('section')
- g_a_log: float32 [2, 32], P('section')
- g_d_skip: float32 [2, 32], P('section')
- g_gnorm_w: float32 [2, 2048], P('section')
- g_out_w: float32 [2, 2048, 1024], P('section', ('seq', 'wshard'))
The draws below stay inside these ranges and needn't reach their ends.
Inputs may be any that keep to these rules, and one draw needn't show every extreme that they name: `seq_lengths`: the 4 lengths of a micro-batch and group add up to 1024, and the largest is exactly 512. `deal_order`: each row of a micro-batch and group is a permutation of the positions 0 to 1023.
All inputs are finite; a program needn't handle non-finite values.
Results may differ from the reference program's by a relative error of at most 0.015.
The reference program's roundings to bfloat16 on the way (of `normed`, `mixing`, `mixed` and `normed_out`) count: a program that leaves them out, or rounds other values in their place, can miss the bound.
Values may be sent and summed in bfloat16 or wider, within the bound.
No kernel may reach another device: no remote copies, remote signals or barrier semaphores. Data moves between devices by JAX's collectives and lax.ppermute only.
A program may use at most 320 MiB of HBM per device.

```python
import math
import jax
import jax.numpy as jnp
import numpy as np
from jax import lax

D = 1024
HEADDIM = 64
STATE = 128
KCONV = 4
BLOCK = 256
MB = 2
NSEQ = 4
INNER = 2048
HEADS = 32
CONVDIM = 2304
PROJ = 4384
GROUPS = 4
GTOK = 1024
MOSTLEN = 512


def block_scale(stream_key, dims, cuts, low, largest):
    def one(axis_at, parts):
        draws = jax.random.uniform(jax.random.fold_in(jax.random.fold_in(stream_key, 6), axis_at), (parts,), jnp.float32, low / len(cuts), largest / len(cuts))
        return jnp.repeat(jnp.exp(draws), dims[axis_at] // parts).reshape((-1,) + (1,) * (len(dims) - axis_at - 1))

    level = one(*cuts[0])
    for cut in cuts[1:]:
        level = level * one(*cut)
    return level


def profile(amount, total, most, skew):
    portions = [(1 << 20) // math.isqrt(rank ** skew) + 1 for rank in range(2, amount + 1)]
    surplus, counts = total - most - (amount - 1), [1] * (amount - 1)
    while surplus > 0:
        free = [i for i in range(amount - 1) if counts[i] < most]
        mass, remaining = sum([portions[i] for i in free]), surplus
        for i in free:
            extra = min(most - counts[i], max(1, remaining * portions[i] // mass), surplus)
            counts[i] = counts[i] + extra
            surplus = surplus - extra
    return np.array([most] + counts)


def ragged(own_key, count, total, most, lean):
    if count == 2:
        one = jax.random.randint(own_key, (), max(1, total - most), min(most, total - 1) + 1)
        return jnp.stack([one, total - one])
    tallies = jnp.asarray(profile(count, total, most, lean), jnp.int32)
    couples = (count - 1) // 2
    giver, sink = tallies[1:1 + 2 * couples:2], tallies[2:2 + 2 * couples:2]
    margin = jnp.minimum(giver - 1, most - sink)
    moved = jax.random.randint(jax.random.fold_in(own_key, 1), (couples,), 0, 1 << 20) % (margin + 1)
    tallies = tallies.at[1:1 + 2 * couples:2].set(giver - moved).at[2:2 + 2 * couples:2].set(sink + moved)
    return tallies[jax.random.permutation(jax.random.fold_in(own_key, 2), count)]


def noise(rng, shape, width, limit, split=(), dtype=jnp.bfloat16):
    values = width * jax.random.normal(rng, shape, jnp.float32)
    if split:
        values = values * block_scale(rng, shape, split, -0.22, 0.18)
    return jnp.clip(values, -limit, limit).astype(dtype)


def setup_inputs(seed: int = 0) -> dict:
    keys = jax.random.split(jax.random.key(seed), 13)
    ends_in = noise(keys[0], (2, MB, GROUPS, GTOK, D), 1.0, 6.0, ((0, 2), (2, 4), (3, 4)))
    seq_lengths = jax.vmap(lambda own: ragged(own, NSEQ, GTOK, MOSTLEN, 2))(jax.random.split(keys[1], MB * GROUPS)).reshape((MB, GROUPS, NSEQ)).astype(jnp.int32)
    deal_order = jax.vmap(lambda own: jax.random.permutation(own, GTOK))(jax.random.split(keys[2], MB * GROUPS)).reshape((MB, GROUPS, GTOK)).astype(jnp.int32)
    norm_w = jnp.clip(1.0 + 0.18 * jax.random.normal(keys[3], (2, D), jnp.float32), 0.1, 1.9)
    in_w = noise(keys[4], (2, D, PROJ), D ** -0.5, 0.1875, ((0, 2), (1, 4)))
    conv_w = noise(keys[5], (2, KCONV, CONVDIM), KCONV ** -0.5, 3.0, ((0, 2),), jnp.float32)
    conv_b = noise(keys[6], (2, CONVDIM), 0.5, 3.0, ((0, 2),), jnp.float32)
    dt_bias = jnp.clip(-5.0 + 2.0 * jax.random.uniform(keys[7], (2, HEADS), jnp.float32) ** block_scale(keys[7], (2, HEADS), ((0, 2),), -0.2, 0.2), -5.0, -3.0)
    a_log = jnp.clip(-6.0 + 8.0 * jax.random.uniform(keys[8], (2, HEADS), jnp.float32) ** block_scale(keys[8], (2, HEADS), ((0, 2),), -0.2, 0.2), -6.0, 2.0)
    d_skip = jnp.clip(1.0 + 0.18 * jax.random.normal(keys[9], (2, HEADS), jnp.float32), 0.1, 1.9)
    gnorm_w = jnp.clip(1.0 + 0.18 * jax.random.normal(keys[10], (2, INNER), jnp.float32), 0.1, 1.9)
    out_w = noise(keys[11], (2, INNER, D), INNER ** -0.5, 0.125, ((0, 2), (1, 4)))
    return {"ends_in": ends_in, "seq_lengths": seq_lengths, "deal_order": deal_order, "norm_w": norm_w, "in_w": in_w, "conv_w": conv_w, "conv_b": conv_b, "dt_bias": dt_bias, "a_log": a_log, "d_skip": d_skip, "gnorm_w": gnorm_w, "out_w": out_w}


EPS = 1e-05
HIGH = lax.Precision.HIGHEST

@jax.custom_vjp
def low(v):
    return lax.optimization_barrier(v.astype(jnp.bfloat16)).astype(jnp.float32)

@jax.custom_vjp
def low_back(v):
    return v

def low_keep(v):
    return (low(v), None)

def low_pass(kept, grad):
    return (grad,)

def back_keep(v):
    return (v, None)

def back_low(kept, grad):
    return (low(grad),)
low.defvjp(low_keep, low_pass)
low_back.defvjp(back_keep, back_low)

def prenorm(tokens, gain):
    return tokens * lax.rsqrt(lax.optimization_barrier(jnp.mean(tokens * tokens, axis=-1, keepdims=True)) + EPS) * gain[None, :]

def gated(values, gate, gain):
    mixed = values * jax.nn.silu(gate)
    return mixed * lax.rsqrt(lax.optimization_barrier(jnp.mean(mixed * mixed, axis=-1, keepdims=True)) + EPS) * gain[None, :]

def segments(lengths, total):
    ends = jnp.cumsum(lengths).astype(jnp.int32)
    place = lax.broadcasted_iota(jnp.int32, (total,), 0)
    passed = place[:, None] >= ends[None, :]
    label = lax.optimization_barrier(jnp.sum(passed.astype(jnp.int32), axis=1)).astype(jnp.int32)
    begin = lax.optimization_barrier(jnp.max(jnp.where(passed, ends[None, :], 0), axis=1)).astype(jnp.int32)
    return (label, place - begin)

def invert(order):
    total = order.shape[0]
    return jnp.zeros((total,), jnp.int32).at[order].set(lax.broadcasted_iota(jnp.int32, (total,), 0))

def convolve(values, kernel, shift, offset):
    count = values.shape[0]
    taps = kernel.shape[0]
    total = jnp.zeros(values.shape, jnp.float32) + shift[None, :]
    for index in range(taps):
        delay = taps - 1 - index
        moved = jnp.pad(values, ((delay, 0), (0, 0)))[:count]
        inside = (offset >= delay).astype(jnp.float32)
        total = total + kernel[index][None, :] * moved * inside[:, None]
    return jax.nn.silu(total)

def decays(raw, bias, log_rate, label, before):
    rate = jax.nn.softplus(raw + bias[None, :])
    level = jnp.cumsum(rate * (-jnp.exp(log_rate))[None, :], axis=0)
    length = raw.shape[0]
    rows = lax.broadcasted_iota(jnp.int32, (length, length), 0)
    column = lax.broadcasted_iota(jnp.int32, (length, length), 1)
    inside = (label[:, None] == label[None, :]) & (column <= rows)
    gap = level.T[:, :, None] - level.T[:, None, :]
    weight = jnp.exp(jnp.where(inside[None], gap, 0.0)) * inside[None].astype(jnp.float32) * rate.T[:, None, :]
    final = label[length - 1]
    tail = jnp.exp(level[length - 1][None, :] - level) * (label == final).astype(jnp.float32)[:, None] * rate
    head = jnp.exp(level) * (label == before).astype(jnp.float32)[:, None]
    carry = jnp.exp(level[length - 1]) * (final == before).astype(jnp.float32)
    return (weight, tail, head, carry)

def block_step(bias, log_rate, skip, state, piece):
    inputs, pair, raw, label, before = piece
    weight, tail, head, carry = decays(raw, bias, log_rate, label, before)
    write_part = pair[:, :STATE]
    read_part = pair[:, STATE:]
    gram = jnp.dot(read_part, write_part.T, precision=HIGH)
    mixing = low(gram[None] * weight)
    output = jnp.einsum('hij,jhp->ihp', mixing, inputs, precision=HIGH)
    output = output + head[:, :, None] * jnp.einsum('in,hnp->ihp', read_part, state, precision=HIGH)
    output = output + skip[None, :, None] * inputs
    fresh = carry[:, None, None] * state + jnp.einsum('jn,jhp->hnp', write_part, tail[:, :, None] * inputs, precision=HIGH)
    return (fresh, output)

def scan_heads(input_conv, pair_conv, raw, label, bias, log_rate, skip):
    total = input_conv.shape[0]
    count = total // BLOCK
    label_parts = label.reshape(count, BLOCK)
    before = jnp.concatenate([jnp.full((1,), -1, jnp.int32), label_parts[:-1, BLOCK - 1]])

    def advance(state, piece):
        return block_step(bias, log_rate, skip, state, piece)
    start = jnp.zeros((HEADS, STATE, HEADDIM), jnp.float32)
    pieces = (input_conv.reshape(count, BLOCK, HEADS, HEADDIM), pair_conv.reshape(count, BLOCK, 2 * STATE), raw.reshape(count, BLOCK, HEADS), label_parts, before)
    _, outputs = lax.scan(jax.checkpoint(advance), start, pieces)
    return outputs.reshape(total, INNER)

def layer(weights, tokens, order, lengths):
    norm_gain, in_proj, kernel, conv_bias, rate_bias, log_rate, skip, gated_gain, out_proj = weights
    normed = low(prenorm(tokens, norm_gain))
    projected = low_back(jnp.dot(normed, in_proj, precision=HIGH))
    gate = projected[:, :INNER]
    conv_rows = low(projected[:, INNER:INNER + CONVDIM])
    raw_rows = low(projected[:, INNER + CONVDIM:])
    total = tokens.shape[0]
    label, offset = segments(lengths, total)
    inverse = invert(order)
    conv_out = convolve(conv_rows[inverse], kernel, conv_bias, offset)
    input_conv = low(conv_out[:, :INNER])
    pair_conv = low(conv_out[:, INNER:])
    mixed = scan_heads(input_conv, pair_conv, raw_rows[inverse], label, rate_bias, log_rate, skip)
    mixed = low_back(low(mixed[order]))
    normed_out = low(gated(mixed, gate, gated_gain))
    output = low_back(jnp.dot(normed_out, out_proj, precision=HIGH))
    return tokens + output

def reference(ends_in, seq_lengths, deal_order, norm_w, in_w, conv_w, conv_b, dt_bias, a_log, d_skip, gnorm_w, out_w):
    start = ends_in[0].astype(jnp.float32)
    cotangent = ends_in[1].astype(jnp.float32)
    weights = tuple((item.astype(jnp.float32) for item in (norm_w, in_w, conv_w, conv_b, dt_bias, a_log, d_skip, gnorm_w, out_w)))
    count = MB * GROUPS
    orders = deal_order.reshape(count, GTOK)
    lens = seq_lengths.reshape(count, NSEQ)

    def forward(weights, start):
        first = tuple((item[0] for item in weights))
        second = tuple((item[1] for item in weights))

        def through(piece):
            tokens, order, lengths = piece
            middle = layer(first, tokens, order, lengths)
            middle = low_back(low(middle))
            return layer(second, middle, order, lengths)
        result = lax.map(through, (start.reshape(count, GTOK, D), orders, lens))
        return result.reshape(MB, GROUPS, GTOK, D)
    final, pullback = jax.vjp(forward, weights, start)
    grads, grad_start = pullback(cotangent)
    ends_out = jnp.stack([grad_start, final])
    return (ends_out, grads[0], grads[1], grads[2], grads[3], grads[4], grads[5], grads[6], grads[7], grads[8])
```

```python
import functools

import jax
import jax.numpy as jnp
from jax import lax
from jax.experimental import pallas as pl
from jax.experimental.pallas import tpu as pltpu
from jax.sharding import PartitionSpec as P

D = 1024
HEADDIM = 64
STATE = 128
KCONV = 4
BLOCK = 256
INNER = 2048
HEADS = 32
PAIR = 2 * STATE
LANES = 128
EPS = 1e-05
NEG = -1e30
BF = jnp.bfloat16
F32 = jnp.float32
HIGH = lax.Precision.HIGHEST
AXES = ("section", "seq", "wshard")
VMEM_LIMIT = 58 << 20


def params():
    return pltpu.CompilerParams(
        dimension_semantics=("arbitrary",), vmem_limit_bytes=VMEM_LIMIT
    )


def cost(flops, nbytes, trans=0):
    return pl.CostEstimate(flops=flops, bytes_accessed=nbytes, transcendentals=trans)


def nn(a, b, precision=None):
    return lax.dot_general(
        a, b, (((1,), (0,)), ((), ())), preferred_element_type=F32, precision=precision
    )


def nt(a, b):
    return lax.dot_general(a, b, (((1,), (1,)), ((), ())), preferred_element_type=F32)


def tn(a, b):
    return lax.dot_general(a, b, (((0,), (0,)), ((), ())), preferred_element_type=F32)


def two(x):
    hi = x.astype(BF)
    lo = (x - hi.astype(F32)).astype(BF)
    return jnp.concatenate([hi, lo], axis=1)


def iota(shape, dim):
    return lax.broadcasted_iota(jnp.int32, shape, dim)


def column(row):
    return jnp.broadcast_to(row, (LANES, row.shape[1])).T[:, :1]


def as_row(col):
    return jnp.broadcast_to(col, (col.shape[0], LANES)).T[:1]


def sigmoid(x):
    return 1.0 / (1.0 + jnp.exp(-x))


def softplus(x):
    return jnp.maximum(x, 0.0) + jnp.log1p(jnp.exp(-jnp.abs(x)))


def full(shape):
    return pl.BlockSpec(shape, lambda i: (0,) * len(shape))


def place_kernel(with_norm, order_ref, x_ref, gain_ref, *outs):
    base = pl.program_id(0) * BLOCK
    total = x_ref.shape[0]
    hot = (order_ref[...] == base + iota((BLOCK, total), 0)).astype(BF)
    tokens = nn(hot, x_ref[...])
    outs[0][...] = tokens.astype(BF)
    if with_norm:
        scale = lax.rsqrt(jnp.mean(tokens * tokens, axis=1, keepdims=True) + EPS)
        outs[1][...] = (tokens * scale * gain_ref[...]).astype(BF)


def place(order_row, x, gain, with_norm):
    total = x.shape[0]
    count = total // BLOCK
    out = jax.ShapeDtypeStruct((total, D), BF)
    number = 2 if with_norm else 1
    return pl.pallas_call(
        functools.partial(place_kernel, with_norm),
        grid=(count,),
        in_specs=[full((1, total)), full((total, D)), full((1, D))],
        out_specs=[pl.BlockSpec((BLOCK, D), lambda i: (i, 0))] * number,
        out_shape=[out] * number,
        compiler_params=params(),
        cost_estimate=cost(2 * total * total * D, 6 * total * D),
        name="place",
    )(order_row, x, gain)


def unplace_kernel(order_ref, x_ref, out_ref):
    total = x_ref.shape[0]
    hot = (order_ref[...] == iota((BLOCK, total), 1)).astype(BF)
    out_ref[...] = nn(hot, x_ref[...]).astype(BF)


def unplace(order_col, x):
    total = x.shape[0]
    return pl.pallas_call(
        unplace_kernel,
        grid=(total // BLOCK,),
        in_specs=[pl.BlockSpec((BLOCK, 1), lambda i: (i, 0)), full((total, D))],
        out_specs=pl.BlockSpec((BLOCK, D), lambda i: (i, 0)),
        out_shape=jax.ShapeDtypeStruct((total, D), BF),
        compiler_params=params(),
        cost_estimate=cost(2 * total * total * D, 4 * total * D),
        name="unplace",
    )(order_col, x)


def block_terms(raw, dtb, rate_sign, label_col, offset):
    rate = softplus(raw + dtb)
    rows = iota((BLOCK, BLOCK), 0)
    cols = iota((BLOCK, BLOCK), 1)
    lower = (cols <= rows).astype(F32)
    level = nn(lower, rate * rate_sign, HIGH)
    local = iota((BLOCK, 1), 0)
    end = level[BLOCK - 1 :]
    end_offset = offset[BLOCK - 1 :]
    head = jnp.where(offset > local, jnp.exp(level), 0.0)
    fade = jnp.where(local >= BLOCK - 1 - end_offset, jnp.exp(end - level), 0.0)
    carry = jnp.where(end_offset > BLOCK - 1, jnp.exp(end), 0.0)
    return rate, level, head, fade, carry


def forward_kernel(
    heads,
    normed_ref,
    wg_ref,
    wc_ref,
    wr_ref,
    taps_ref,
    bias_ref,
    dtb_ref,
    sign_ref,
    skip_ref,
    spread_ref,
    pos_ref,
    label_ref,
    gate_ref,
    pre_ref,
    cin_ref,
    raw_ref,
    mixed_ref,
    states_ref,
    square_ref,
    state_ref,
    halo_ref,
):
    width = heads * HEADDIM

    @pl.when(pl.program_id(0) == 0)
    def _():
        state_ref[...] = jnp.zeros_like(state_ref)
        halo_ref[...] = jnp.zeros_like(halo_ref)

    x = normed_ref[...]
    gate = nn(x, wg_ref[...])
    gate_ref[...] = gate
    cin_low = nn(x, wc_ref[...]).astype(BF)
    cin_ref[...] = cin_low
    raw_low = nn(x, wr_ref[...]).astype(BF)
    raw_ref[...] = raw_low
    pos = pos_ref[...]
    label_col = pos[:, 0:1]
    offset = pos[:, 1:2]
    cin = cin_low.astype(F32)
    longer = jnp.concatenate([halo_ref[...], cin], axis=0)
    halo_ref[...] = cin[BLOCK - 8 :]
    taps = taps_ref[...]
    pre = bias_ref[...] + taps[KCONV - 1 : KCONV] * cin
    for index in range(KCONV - 1):
        delay = KCONV - 1 - index
        moved = longer[8 - delay : 8 - delay + BLOCK]
        pre = pre + jnp.where(offset >= delay, taps[index : index + 1] * moved, 0.0)
    pre_ref[...] = pre
    conv = (pre * sigmoid(pre)).astype(BF)
    write = conv[:, :STATE]
    read = conv[:, STATE:PAIR]
    xs = conv[:, PAIR:]
    xs_float = xs.astype(F32)
    rate, level, head, fade, carry = block_terms(
        raw_low.astype(F32), dtb_ref[...], sign_ref[...], label_col, offset
    )
    tail = fade * rate
    level_rows = level.T
    rate_rows = rate.T
    spread = spread_ref[...]
    state = state_ref[...]
    states_ref[0] = state
    mixed = nn(two(head), spread) * nn(read, state.astype(BF)) + skip_ref[...] * xs_float
    gram = nt(read, write)
    inside = (label_col == label_ref[0]) & (iota((BLOCK, BLOCK), 1) <= iota((BLOCK, BLOCK), 0))
    closed = jnp.where(inside, 0.0, NEG)
    step = 2 if heads % 2 == 0 else 1
    parts = []
    for first in range(0, heads, step):
        span = xs[:, first * HEADDIM : (first + step) * HEADDIM]
        mixing = []
        values = []
        for h in range(first, first + step):
            weight = jnp.exp(level[:, h : h + 1] - level_rows[h : h + 1] + closed)
            mixing.append((gram * (weight * rate_rows[h : h + 1])).astype(BF))
            if step == 1:
                values.append(span)
            else:
                own = iota(span.shape, 1) // HEADDIM == h - first
                values.append(jnp.where(own, span, jnp.zeros_like(span)))
        parts.append(nn(jnp.concatenate(mixing, axis=1), jnp.concatenate(values, axis=0)))
    mixed = mixed + jnp.concatenate(parts, axis=1)
    mixed_low = mixed.astype(BF)
    mixed_ref[...] = mixed_low
    gv = mixed_low.astype(F32) * (gate * sigmoid(gate))
    square_ref[0] = as_row(jnp.sum(gv * gv, axis=1, keepdims=True))
    carry_rows = jnp.broadcast_to(carry, (8, LANES))
    carry_wide = nn(two(carry_rows), spread)[:1]
    written = (nn(two(tail), spread) * xs_float).astype(BF)
    state_ref[...] = carry_wide * state + tn(write, written)


def forward(heads, normed, weights, vectors, spread, pos, label_row):
    total = normed.shape[0]
    count = total // BLOCK
    width = heads * HEADDIM
    conv = PAIR + width
    wg, wc, wr = weights
    block = lambda n: pl.BlockSpec((BLOCK, n), lambda i: (i, 0))
    row = pl.BlockSpec((1, 1, BLOCK), lambda i: (i, 0, 0))
    return pl.pallas_call(
        functools.partial(forward_kernel, heads),
        grid=(count,),
        in_specs=[
            block(D),
            full((D, width)),
            full((D, conv)),
            full((D, LANES)),
            full((KCONV, conv)),
            full((1, conv)),
            full((1, LANES)),
            full((1, LANES)),
            full((1, width)),
            full((2 * LANES, width)),
            block(3),
            row,
        ],
        out_specs=[
            block(width),
            block(conv),
            block(conv),
            block(LANES),
            block(width),
            pl.BlockSpec((1, STATE, width), lambda i: (i, 0, 0)),
            row,
        ],
        out_shape=[
            jax.ShapeDtypeStruct((total, width), F32),
            jax.ShapeDtypeStruct((total, conv), F32),
            jax.ShapeDtypeStruct((total, conv), BF),
            jax.ShapeDtypeStruct((total, LANES), BF),
            jax.ShapeDtypeStruct((total, width), BF),
            jax.ShapeDtypeStruct((count, STATE, width), F32),
            jax.ShapeDtypeStruct((count, 1, BLOCK), F32),
        ],
        scratch_shapes=[pltpu.VMEM((STATE, width), F32), pltpu.VMEM((8, conv), F32)],
        compiler_params=params(),
        cost_estimate=cost(
            2 * total * D * (width + conv + LANES) * 2, total * D * 12, total * BLOCK * heads
        ),
        name="forward",
    )(
        normed,
        wg,
        wc,
        wr,
        vectors["taps"],
        vectors["bias"],
        vectors["dtb"],
        vectors["sign"],
        vectors["skip"],
        spread,
        pos,
        label_row,
    )


def project_kernel(with_rest, own_ref, mixed_ref, gate_ref, square_ref, gain_ref, w_ref, rest_ref, out_ref):
    gate = gate_ref[...]
    gv = mixed_ref[...].astype(F32) * (gate * sigmoid(gate))
    scale = lax.rsqrt(column(square_ref[0]) / INNER + EPS)
    normed_out = (gv * scale * gain_ref[...]).astype(BF)
    out = nn(normed_out, w_ref[...])
    if with_rest:
        own = (own_ref[0] == pl.program_id(0)).astype(F32)
        out = out + own * rest_ref[...].astype(F32)
    out_ref[...] = out.astype(BF)


def project(mixed, gate, square, gain, w, own, rest, with_rest):
    total, width = mixed.shape
    block = lambda n: pl.BlockSpec((BLOCK, n), lambda i: (i, 0))
    return pl.pallas_call(
        functools.partial(project_kernel, with_rest),
        grid=(total // BLOCK,),
        in_specs=[
            pl.BlockSpec(memory_space=pltpu.SMEM),
            block(width),
            block(width),
            pl.BlockSpec((1, 1, BLOCK), lambda i: (i, 0, 0)),
            full((1, width)),
            full((width, D)),
            full((BLOCK, D)),
        ],
        out_specs=block(D),
        out_shape=jax.ShapeDtypeStruct((total, D), BF),
        compiler_params=params(),
        cost_estimate=cost(2 * total * D * width, total * (width * 6 + D * 2)),
        name="project",
    )(own, mixed, gate, square, gain, w, rest)


def dots_kernel(dout_ref, w_ref, mixed_ref, gate_ref, gain_ref, out_ref):
    gate = gate_ref[...]
    gv = mixed_ref[...].astype(F32) * (gate * sigmoid(gate))
    grad = nt(dout_ref[...], w_ref[...]) * gain_ref[...]
    out_ref[0] = as_row(jnp.sum(grad * gv, axis=1, keepdims=True))


def dots(dout, w, mixed, gate, gain):
    total, width = mixed.shape
    block = lambda n: pl.BlockSpec((BLOCK, n), lambda i: (i, 0))
    row = pl.BlockSpec((1, 1, BLOCK), lambda i: (i, 0, 0))
    return pl.pallas_call(
        dots_kernel,
        grid=(total // BLOCK,),
        in_specs=[block(D), full((width, D)), block(width), block(width), full((1, width))],
        out_specs=row,
        out_shape=jax.ShapeDtypeStruct((total // BLOCK, 1, BLOCK), F32),
        compiler_params=params(),
        cost_estimate=cost(2 * total * D * width, total * (width * 6 + D * 2)),
        name="dots",
    )(dout, w, mixed, gate, gain)


def ungate_kernel(
    dout_ref,
    w_ref,
    mixed_ref,
    gate_ref,
    gain_ref,
    square_ref,
    dot_ref,
    normed_ref,
    dmixed_ref,
    dgate_ref,
    ggain_ref,
    gout_ref,
    gin_ref,
    out_total,
    in_total,
):
    step = pl.program_id(0)

    @pl.when(step == 0)
    def _():
        ggain_ref[...] = jnp.zeros_like(ggain_ref)
        out_total[...] = jnp.zeros_like(out_total)
        in_total[...] = jnp.zeros_like(in_total)

    gate = gate_ref[...]
    gain = gain_ref[...]
    mixed = mixed_ref[...].astype(F32)
    sig = sigmoid(gate)
    act = gate * sig
    scale = lax.rsqrt(column(square_ref[0]) / INNER + EPS)
    normal = mixed * act * scale
    dout = dout_ref[...]
    grad_out = nt(dout, w_ref[...])
    grad_normal = grad_out * gain
    shared = column(dot_ref[0]) * scale / INNER
    grad_gv = scale * (grad_normal - normal * shared)
    dmixed_ref[...] = (grad_gv * act).astype(BF)
    dgate = (grad_gv * mixed * (sig * (1.0 + gate * (1.0 - sig)))).astype(BF)
    dgate_ref[...] = dgate
    ggain_ref[...] += jnp.sum(grad_out * normal, axis=0, keepdims=True)
    out_total[...] += tn((normal * gain).astype(BF), dout)
    in_total[...] += tn(normed_ref[...], dgate)

    @pl.when(step == pl.num_programs(0) - 1)
    def _():
        gout_ref[...] = out_total[...].astype(BF)
        gin_ref[...] = in_total[...].astype(BF)


def ungate(dout, w, mixed, gate, gain, square, dot, normed):
    total, width = mixed.shape
    block = lambda n: pl.BlockSpec((BLOCK, n), lambda i: (i, 0))
    row = pl.BlockSpec((1, 1, BLOCK), lambda i: (i, 0, 0))
    return pl.pallas_call(
        ungate_kernel,
        grid=(total // BLOCK,),
        in_specs=[
            block(D),
            full((width, D)),
            block(width),
            block(width),
            full((1, width)),
            row,
            row,
            block(D),
        ],
        out_specs=[
            block(width),
            block(width),
            full((1, width)),
            full((width, D)),
            full((D, width)),
        ],
        out_shape=[
            jax.ShapeDtypeStruct((total, width), BF),
            jax.ShapeDtypeStruct((total, width), BF),
            jax.ShapeDtypeStruct((1, width), F32),
            jax.ShapeDtypeStruct((width, D), BF),
            jax.ShapeDtypeStruct((D, width), BF),
        ],
        scratch_shapes=[pltpu.VMEM((width, D), F32), pltpu.VMEM((D, width), F32)],
        compiler_params=params(),
        cost_estimate=cost(6 * total * D * width, total * (width * 10 + D * 4)),
        name="ungate",
    )(dout, w, mixed, gate, gain, square, dot, normed)


def backward_kernel(
    heads,
    normed_ref,
    wg_ref,
    wc_ref,
    wr_ref,
    taps_ref,
    dtb_ref,
    sign_ref,
    skip_ref,
    spread_ref,
    fold_ref,
    pos_ref,
    label_ref,
    pre_ref,
    cin_ref,
    raw_ref,
    states_ref,
    dmixed_ref,
    dgate_ref,
    dnormed_ref,
    gconv_ref,
    graw_ref,
    gtaps_ref,
    gheads_ref,
    gskip_ref,
    dstate_ref,
    halo_ref,
    conv_total,
    raw_total,
):
    step = pl.program_id(0)

    @pl.when(step == 0)
    def _():
        dstate_ref[...] = jnp.zeros_like(dstate_ref)
        halo_ref[...] = jnp.zeros_like(halo_ref)
        conv_total[...] = jnp.zeros_like(conv_total)
        raw_total[...] = jnp.zeros_like(raw_total)
        gtaps_ref[...] = jnp.zeros_like(gtaps_ref)
        gheads_ref[...] = jnp.zeros_like(gheads_ref)
        gskip_ref[...] = jnp.zeros_like(gskip_ref)

    pos = pos_ref[...]
    label_col = pos[:, 0:1]
    offset = pos[:, 1:2]
    remain = pos[:, 2:3]
    pre = pre_ref[...]
    sig = sigmoid(pre)
    conv = (pre * sig).astype(BF)
    write = conv[:, :STATE]
    read = conv[:, STATE:PAIR]
    xs = conv[:, PAIR:]
    xs_float = xs.astype(F32)
    raw = raw_ref[...].astype(F32)
    sign = sign_ref[...]
    rate, level, head, fade, carry = block_terms(raw, dtb_ref[...], sign, label_col, offset)
    tail = fade * rate
    level_rows = level.T
    spread = spread_ref[...]
    fold = fold_ref[...]
    skip = skip_ref[...]
    dy = dmixed_ref[...]
    dy_float = dy.astype(F32)
    state = states_ref[0]
    state_low = state.astype(BF)
    dstate = dstate_ref[...]
    dstate_low = dstate.astype(BF)
    from_state = nn(read, state_low)
    dhead = nn(two(dy_float * from_state), fold)
    tail_wide = nn(two(tail), spread)
    scaled = (nn(two(head), spread) * dy_float).astype(BF)
    written = (tail_wide * xs_float).astype(BF)
    through = nn(write, dstate_low)
    dtail = nn(two(xs_float * through), fold)
    gskip_ref[...] += jnp.sum(dy_float * xs_float, axis=0, keepdims=True)
    carry_rows = jnp.broadcast_to(carry, (8, LANES))
    carry_wide = nn(two(carry_rows), spread)[:1]
    held = jnp.broadcast_to(jnp.sum(state * dstate, axis=0, keepdims=True), (8, heads * HEADDIM))
    dcarry = nn(two(held), fold)[:1]

    gram = nt(write, read)
    inside = (label_col == label_ref[0]) & (iota((BLOCK, BLOCK), 0) <= iota((BLOCK, BLOCK), 1))
    closed = jnp.where(inside, 0.0, NEG)
    pair_size = 2 if heads % 2 == 0 else 1
    lane = iota((1, LANES), 1)
    drate = jnp.zeros((BLOCK, LANES), F32)
    level_sums = []
    parts = []
    dgram = jnp.zeros((BLOCK, BLOCK), F32)
    for first in range(0, heads, pair_size):
        cut = slice(first * HEADDIM, (first + pair_size) * HEADDIM)
        xs_span = xs[:, cut]
        dy_span = dy[:, cut]
        mixing = []
        values = []
        for h in range(first, first + pair_size):
            if pair_size == 1:
                xs_own = xs_span
                dy_own = dy_span
            else:
                own = iota(xs_span.shape, 1) // HEADDIM == h - first
                xs_own = jnp.where(own, xs_span, jnp.zeros_like(xs_span))
                dy_own = jnp.where(own, dy_span, jnp.zeros_like(dy_span))
            decay = jnp.exp(level_rows[h : h + 1] - level[:, h : h + 1] + closed)
            rate_col = rate[:, h : h + 1]
            weight = decay * rate_col
            mixing.append((gram * weight).astype(BF))
            values.append(dy_own)
            dmix = nt(xs_own, dy_span)
            dgram = dgram + dmix * weight
            bare = dmix * gram * decay
            drate = drate + jnp.sum(bare, axis=1, keepdims=True) * (lane == h).astype(F32)
            level_sums.append(jnp.sum(bare * rate_col, axis=0, keepdims=True))
        parts.append(nn(jnp.concatenate(mixing, axis=1), jnp.concatenate(values, axis=0)))
    dxs = jnp.concatenate(parts, axis=1) + skip * dy_float + tail_wide * through
    dgram_low = dgram.astype(BF)
    dread = tn(dgram_low, write) + nt(scaled, state_low)
    dwrite = nn(dgram_low, read) + nt(written, dstate_low)
    dstate_ref[...] = carry_wide * dstate + tn(read, scaled)

    level_sums.append(jnp.zeros((LANES - heads, BLOCK), F32))
    tail_flow = dtail * tail
    local = iota((BLOCK, 1), 0)
    last = jnp.sum(tail_flow, axis=0, keepdims=True) + dcarry * carry
    dlevel = jnp.concatenate(level_sums, axis=0).T - rate * drate + dhead * head - tail_flow
    dlevel = dlevel + jnp.where(local == BLOCK - 1, last, 0.0)
    upper = (iota((BLOCK, BLOCK), 0) <= iota((BLOCK, BLOCK), 1)).astype(F32)
    dsum = nn(upper, dlevel, HIGH)
    drate = drate + dtail * fade + sign * dsum
    draw = drate * sigmoid(raw + dtb_ref[...])
    gheads_ref[0:1] += jnp.sum(draw, axis=0, keepdims=True)
    gheads_ref[1:2] += jnp.sum(rate * dsum, axis=0, keepdims=True) * sign

    dpre = jnp.concatenate([dwrite, dread, dxs], axis=1) * (sig * (1.0 + pre * (1.0 - sig)))
    longer = jnp.concatenate([dpre, halo_ref[...]], axis=0)
    halo_ref[...] = dpre[:8]
    cin = cin_ref[...].astype(F32)
    taps = taps_ref[...]
    gtaps_ref[KCONV : KCONV + 1] += jnp.sum(dpre, axis=0, keepdims=True)
    gtaps_ref[KCONV - 1 : KCONV] += jnp.sum(dpre * cin, axis=0, keepdims=True)
    dcin = taps[KCONV - 1 : KCONV] * dpre
    for index in range(KCONV - 1):
        delay = KCONV - 1 - index
        moved = jnp.where(remain >= delay, longer[delay : delay + BLOCK], 0.0)
        dcin = dcin + taps[index : index + 1] * moved
        gtaps_ref[index : index + 1] += jnp.sum(moved * cin, axis=0, keepdims=True)
    dcin_low = dcin.astype(BF)
    draw_low = draw.astype(BF)
    dnormed = (
        nt(dgate_ref[...], wg_ref[...]) + nt(dcin_low, wc_ref[...]) + nt(draw_low, wr_ref[...])
    )
    dnormed_ref[...] = dnormed.astype(BF)
    x = normed_ref[...]
    conv_total[...] += tn(x, dcin_low)
    raw_total[...] += tn(x, draw_low)

    @pl.when(step == pl.num_programs(0) - 1)
    def _():
        gconv_ref[...] = conv_total[...].astype(BF)
        graw_ref[...] = raw_total[...].astype(BF)


def backward(heads, normed, weights, vectors, spread, fold, pos, label_row, kept, dmixed, dgate):
    total = normed.shape[0]
    count = total // BLOCK
    width = heads * HEADDIM
    conv = PAIR + width
    wg, wc, wr = weights
    pre, cin, raw, states = kept
    block = lambda n: pl.BlockSpec((BLOCK, n), lambda i: (count - 1 - i, 0))
    return pl.pallas_call(
        functools.partial(backward_kernel, heads),
        grid=(count,),
        in_specs=[
            block(D),
            full((D, width)),
            full((D, conv)),
            full((D, LANES)),
            full((KCONV, conv)),
            full((1, LANES)),
            full((1, LANES)),
            full((1, width)),
            full((2 * LANES, width)),
            full((2 * width, LANES)),
            block(3),
            pl.BlockSpec((1, 1, BLOCK), lambda i: (count - 1 - i, 0, 0)),
            block(conv),
            block(conv),
            block(LANES),
            pl.BlockSpec((1, STATE, width), lambda i: (count - 1 - i, 0, 0)),
            block(width),
            block(width),
        ],
        out_specs=[
            block(D),
            full((D, conv)),
            full((D, LANES)),
            full((8, conv)),
            full((8, LANES)),
            full((1, width)),
        ],
        out_shape=[
            jax.ShapeDtypeStruct((total, D), BF),
            jax.ShapeDtypeStruct((D, conv), BF),
            jax.ShapeDtypeStruct((D, LANES), BF),
            jax.ShapeDtypeStruct((8, conv), F32),
            jax.ShapeDtypeStruct((8, LANES), F32),
            jax.ShapeDtypeStruct((1, width), F32),
        ],
        scratch_shapes=[
            pltpu.VMEM((STATE, width), F32),
            pltpu.VMEM((8, conv), F32),
            pltpu.VMEM((D, conv), F32),
            pltpu.VMEM((D, LANES), F32),
        ],
        compiler_params=params(),
        cost_estimate=cost(
            4 * total * D * (width + conv + LANES) * 2, total * D * 16, total * BLOCK * heads
        ),
        name="backward",
    )(
        normed,
        wg,
        wc,
        wr,
        vectors["taps"],
        vectors["dtb"],
        vectors["sign"],
        vectors["skip"],
        spread,
        fold,
        pos,
        label_row,
        pre,
        cin,
        raw,
        states,
        dmixed,
        dgate,
    )


class Plan:
    def __init__(self):
        self.seq = lax.axis_size("seq")
        self.shards = lax.axis_size("wshard")
        self.half = self.seq // 2
        self.core = lax.axis_index("section")
        self.z = lax.axis_index("seq")
        self.w = lax.axis_index("wshard")
        self.batch = self.z // self.half
        self.place = self.z % self.half
        self.rank = 2 * self.place + self.core

    def send(self, value, route, cores=(0, 1)):
        pairs = []
        for c in range(2):
            for z in range(self.seq):
                for w in range(self.shards):
                    target = route(c, z, w)
                    if c in cores and target is not None:
                        source = (c * self.seq + z) * self.shards + w
                        tc, tz, tw = target
                        pairs.append((source, (tc * self.seq + tz) * self.shards + tw))
        return lax.ppermute(value, AXES, pairs)

    def swap(self, value, cores=(0, 1)):
        return self.send(value, lambda c, z, w: (1 - c, z, w), cores)

    def turn(self, value, k, cores=(0, 1)):
        half = self.half
        return self.send(
            value, lambda c, z, w: (c, z // half * half + (z % half + k) % half, w), cores
        )

    def across(self, value, cores=(0, 1)):
        return self.send(value, lambda c, z, w: (c, (z + self.half) % self.seq, w), cores)

    def beside(self, value, bit, cores=(0, 1)):
        return self.send(value, lambda c, z, w: (c, z, w ^ bit), cores)

    def along(self, value, k):
        return self.send(value, lambda c, z, w: (c, z ^ k, w))

    def gather(self, value):
        rows, width = value.shape
        half = self.half
        whole = jnp.zeros((half, 2, rows, width), value.dtype)

        def put(whole, piece, place, core):
            return lax.dynamic_update_slice(whole, piece[None, None], (place, core, 0, 0))

        zero = jnp.int32(0)
        whole = put(whole, value, self.place, self.core)
        whole = put(whole, self.swap(value), self.place, 1 - self.core)
        for k in range(1, half):
            piece = self.turn(value, k)
            source = (self.place - k + half) % half + zero
            whole = put(whole, piece, source, self.core)
            whole = put(whole, self.swap(piece), source, 1 - self.core)
        return whole.reshape(half * 2 * rows, width)

    def scatter(self, value):
        half = self.half
        rows = value.shape[0] // (2 * half)
        parts = value.reshape(half, 2, rows, value.shape[1])

        def chip_sum(place):
            mine = pick(pick(parts, place), self.core)
            theirs = pick(pick(parts, place), 1 - self.core)
            return mine.astype(F32) + self.swap(theirs).astype(F32)

        arrived = []
        for k in range(1, half):
            term = chip_sum((self.place + k) % half).astype(BF)
            arrived.append(self.turn(term, k))
        total = chip_sum(self.place)
        for term in arrived:
            total = total + term.astype(F32)
        return total

    def total(self, value):
        chip = value + self.swap(value)
        whole = chip
        for k in range(1, self.half):
            whole = whole + self.turn(chip, k)
        return whole

    def shards_of(self, chunk, core):
        rows, width = chunk.shape
        low, high = chunk[: rows // 2], chunk[rows // 2 :]
        low_x = self.beside(low, 1, (core,))
        high_y = self.beside(high, 2, (core,))
        low_y = self.beside(jnp.stack([low, low_x]), 2, (core,))
        high_x = self.beside(jnp.stack([high, high_y]), 1, (core,))
        whole = jnp.zeros((self.shards, 2, rows // 2, width), chunk.dtype)

        def put(whole, piece, shard, part):
            return lax.dynamic_update_slice(whole, piece[None, None], (shard, part, 0, 0))

        w = self.w
        whole = put(whole, low, w, 0)
        whole = put(whole, low_x, w ^ 1, 0)
        whole = put(whole, low_y[0], w ^ 2, 0)
        whole = put(whole, low_y[1], w ^ 3, 0)
        whole = put(whole, high, w, 1)
        whole = put(whole, high_y, w ^ 2, 1)
        whole = put(whole, high_x[0], w ^ 1, 1)
        whole = put(whole, high_x[1], w ^ 3, 1)
        return whole.reshape(self.shards * rows, width)

    def reduce_shards(self, low, high):
        results = []
        firsts = []
        for value, bit in ((low, 1), (high, 2)):
            keep = jnp.stack([pick(value, self.w, 1), pick(value, self.w ^ (3 - bit), 1)])
            away = jnp.stack([pick(value, self.w ^ bit, 1), pick(value, self.w ^ 3, 1)])
            firsts.append((keep, self.beside(away, bit)))
        for (keep, came), bit in zip(firsts, (1, 2)):
            total = keep.astype(F32) + came.astype(F32)
            other = self.beside(total[1].astype(BF), 3 - bit)
            results.append((total[0] + other.astype(F32)).astype(BF))
        return results

    def spread_rows(self, value):
        pieces = [pick(value, self.z)]
        for k in range(1, self.seq):
            pieces.append(self.along(pick(value, self.z ^ k), k))
        half = self.half
        whole = jnp.zeros((half,) + value.shape[1:], BF)
        for k in range(half):
            term = (pieces[k].astype(F32) + pieces[k + half].astype(F32)).astype(BF)
            place = (self.place ^ k) if half > 1 else self.place
            whole = lax.dynamic_update_slice(whole, term[None], (place, 0, 0))
        return whole

    def home(self, value, batch, layer):
        half = self.half

        def route(c, z, w):
            if z // half != batch:
                return None
            return (layer, 2 * (z % half) + c, w)

        return self.send(value, route)


def pick(value, index, axis=0):
    return lax.dynamic_index_in_dim(value, index, axis, keepdims=False)


def cut(value, start, size, axis):
    return lax.dynamic_slice_in_dim(value, start, size, axis)


def prenorm(tokens, gain):
    scale = lax.rsqrt(jnp.mean(tokens * tokens, axis=-1, keepdims=True) + EPS)
    return tokens * scale * gain[None, :]


def on_device(
    ends_in,
    seq_lengths,
    deal_order,
    norm_w,
    in_w,
    conv_w,
    conv_b,
    dt_bias,
    a_log,
    d_skip,
    gnorm_w,
    out_w,
):
    plan = Plan()
    core = plan.core
    half = plan.half
    rank = plan.rank
    rows = ends_in.shape[3]
    total = rows * plan.seq
    count = total // BLOCK
    heads = HEADS // plan.seq
    width = heads * HEADDIM
    conv = PAIR + width

    order = pick(deal_order[:, 0], plan.batch)
    lengths = pick(seq_lengths[:, 0], plan.batch)
    ends = jnp.cumsum(lengths)
    at = iota((total,), 0)
    passed = at[:, None] >= ends[None, :]
    label = jnp.sum(passed.astype(jnp.int32), axis=1)
    begin = jnp.max(jnp.where(passed, ends[None, :], 0), axis=1)
    finish = jnp.min(jnp.where(passed, total, ends[None, :]), axis=1)
    pos = jnp.stack([label, at - begin, finish - 1 - at], axis=1)
    label_row = label.reshape(count, 1, BLOCK)
    order_row = order.reshape(1, total)
    order_col = order.reshape(total, 1)

    def collect(held, slot):
        only = (slot,)
        own = pick(held, plan.batch)
        far = plan.across(pick(held, 1 - plan.batch), only)
        whole = jnp.zeros((2, half, rows, D), BF)

        def put(whole, piece, batch, place):
            return lax.dynamic_update_slice(whole, piece[None, None], (batch, place, 0, 0))

        whole = put(whole, own, plan.batch, plan.place)
        whole = put(whole, far, 1 - plan.batch, plan.place)
        for k in range(1, half):
            source = (plan.place - k + half) % half
            whole = put(whole, plan.turn(own, k, only), plan.batch, source)
            whole = put(whole, plan.turn(far, k, only), 1 - plan.batch, source)
        whole = whole.reshape(total, D)
        return jnp.where(core == slot, whole, plan.swap(whole, only))

    held = ends_in[0, :, 0]
    started = collect(held, 0)
    held_later, _ = lax.optimization_barrier((held, started))
    cotangent = collect(held_later, 1)

    own_small = jnp.concatenate(
        [
            norm_w[0],
            conv_w[0].reshape(-1),
            conv_b[0],
            dt_bias[0],
            a_log[0],
            d_skip[0],
            gnorm_w[0],
        ]
    )
    other_small = plan.swap(own_small)

    def vectors_of(layer):
        flat = jnp.where(core == layer, own_small, other_small)
        sizes = (D, KCONV * (INNER + PAIR), INNER + PAIR, HEADS, HEADS, HEADS, INNER)
        pieces = []
        start = 0
        for size in sizes:
            pieces.append(flat[start : start + size])
            start += size
        gain, taps, bias, dtb, log_rate, skip, gated = pieces
        taps = taps.reshape(KCONV, INNER + PAIR)
        bias = bias.reshape(1, INNER + PAIR)

        def channels(value):
            return jnp.concatenate(
                [value[:, INNER:], cut(value, rank * width, width, 1)], axis=1
            )

        def lanes(value):
            own = cut(value, rank * heads, heads, 0)
            return jnp.pad(own, (0, LANES - heads)).reshape(1, LANES)

        return {
            "gain": gain,
            "taps": channels(taps),
            "bias": channels(bias),
            "dtb": lanes(dtb),
            "sign": lanes(-jnp.exp(log_rate)),
            "skip": jnp.repeat(cut(skip, rank * heads, heads, 0), HEADDIM).reshape(1, width),
            "gated": cut(gated, rank * width, width, 0).reshape(1, width),
        }

    vectors = [vectors_of(0), vectors_of(1)]

    first = 2 * width * plan.place
    gate_cols = cut(in_w[0], first, 2 * width, 1)
    input_cols = cut(in_w[0], INNER + first, 2 * width, 1)
    pair_cols = in_w[0][:, 2 * INNER : 2 * INNER + PAIR]
    raw_cols = cut(in_w[0], 2 * INNER + PAIR + 2 * heads * plan.place, 2 * heads, 1)
    raw_cols = jnp.pad(raw_cols, ((0, 0), (0, LANES - 2 * heads)))
    chunk = jnp.concatenate(
        [
            gate_cols[:, :width],
            input_cols[:, :width],
            gate_cols[:, width:],
            input_cols[:, width:],
            pair_cols,
            raw_cols,
        ],
        axis=1,
    )
    out_chunk = out_w[0]

    def in_weights(chunk, layer):
        whole = plan.shards_of(chunk, layer)
        shared = whole[:, 4 * width :]
        mine = whole[:, 2 * width * layer : 2 * width * (layer + 1)]
        theirs = whole[:, 2 * width * (1 - layer) : 2 * width * (2 - layer)]
        came = plan.swap(jnp.concatenate([theirs, shared], axis=1), (layer,))
        got = jnp.where(core == layer, jnp.concatenate([mine, shared], axis=1), came)
        raw = cut(got[:, 2 * width + PAIR :], core * heads, heads, 1)
        return (
            got[:, :width],
            jnp.concatenate([got[:, 2 * width : 2 * width + PAIR], got[:, width : 2 * width]], axis=1),
            jnp.pad(raw, ((0, 0), (0, LANES - heads))),
        )

    def out_weights(chunk, layer):
        whole = plan.shards_of(chunk, layer)
        mine = cut(whole, width * rank, width, 0)
        theirs = cut(whole, width * (rank ^ 1), width, 0)
        return jnp.where(core == layer, mine, plan.swap(theirs, (layer,)))

    in_first = in_weights(chunk, 0)
    out_chunk_0, _ = lax.optimization_barrier((out_chunk, in_first))
    out_first = out_weights(out_chunk_0, 0)
    chunk_1, _ = lax.optimization_barrier((chunk, out_first))
    in_second = in_weights(chunk_1, 1)
    out_chunk_1, _ = lax.optimization_barrier((out_chunk, in_second))
    out_second = out_weights(out_chunk_1, 1)
    in_parts = [in_first, in_second]
    out_parts = [out_first, out_second]

    channel_head = iota((LANES, width), 1) // HEADDIM
    hot = (channel_head == iota((LANES, width), 0)).astype(BF)
    spread = jnp.concatenate([hot, hot], axis=0)
    fold = jnp.concatenate([hot.T, hot.T], axis=0)

    own_rank = rank.reshape(1).astype(jnp.int32)
    tokens, normed = place(order_row, started, vectors[0]["gain"][None], True)
    saved = []
    unused = jnp.zeros((BLOCK, D), BF)
    own_tokens = cut(tokens, rank * rows, rows, 0)
    rank_tokens = [own_tokens]
    result = None
    for layer in range(2):
        gate, pre, cin, raw, mixed, states, square = forward(
            heads, normed, in_parts[layer], vectors[layer], spread, pos, label_row
        )
        square = plan.total(square)
        saved.append((normed, gate, pre, cin, raw, mixed, states, square))
        rest = unused if layer == 0 else own_tokens
        partial = project(
            mixed, gate, square, vectors[layer]["gated"], out_parts[layer], own_rank, rest, layer == 1
        )
        if layer == 0:
            summed = plan.scatter(partial) + own_tokens.astype(F32)
            own_tokens = summed.astype(BF)
            rank_tokens.append(own_tokens)
            mine = prenorm(own_tokens.astype(F32), vectors[1]["gain"]).astype(BF)
            normed = plan.gather(mine)
        else:
            result = plan.scatter(unplace(order_col, partial)).astype(BF)

    small_terms = []
    weight_terms = []
    (dout,) = place(order_row, cotangent, vectors[0]["gain"][None], False)
    own_dout = cut(dout, rank * rows, rows, 0)
    start_grad = None
    for layer in (1, 0):
        normed, gate, pre, cin, raw, mixed, states, square = saved[layer]
        gated = vectors[layer]["gated"]
        w = out_parts[layer]
        dot = plan.total(dots(dout, w, mixed, gate, gated))
        dmixed, dgate, ggated, gout, ggate = ungate(
            dout, w, mixed, gate, gated, square, dot, normed
        )
        dnormed, gconv, graw, gtaps, gheads, gskip = backward(
            heads,
            normed,
            in_parts[layer],
            vectors[layer],
            spread,
            fold,
            pos,
            label_row,
            (pre, cin, raw, states),
            dmixed,
            dgate,
        )
        if layer == 0:
            dnormed = unplace(order_col, dnormed)
            dout_rows = unplace(order_col, dout)
            own_dout = cut(dout_rows, rank * rows, rows, 0)
            own_in = cut(started, rank * rows, rows, 0)
        else:
            own_in = rank_tokens[1]
        grad = plan.scatter(dnormed)
        _, pull = jax.vjp(prenorm, own_in.astype(F32), vectors[layer]["gain"])
        dtokens, ggain = pull(grad)
        dtokens = (own_dout.astype(F32) + dtokens).astype(BF)
        if layer == 1:
            own_dout = dtokens
            dout = plan.gather(dtokens)
        else:
            start_grad = dtokens
        small_terms.append((ggain, gtaps, gheads, gskip, ggated))
        weight_terms.append((gout, ggate, gconv, graw))
    small_terms.reverse()
    weight_terms.reverse()

    def reduced_in(value):
        share = value.shape[0] // (plan.seq * plan.shards)
        parts = value.reshape(plan.seq, plan.shards, share, value.shape[1])
        cut_at = plan.seq // 2
        low, high = plan.reduce_shards(parts[:cut_at], parts[cut_at:])
        return plan.spread_rows(jnp.concatenate([low, high], axis=0))

    def reduced_out(value):
        share = value.shape[0] // plan.shards
        parts = value.reshape(1, plan.shards, share, D)
        low, high = plan.reduce_shards(parts[..., : D // 2], parts[..., D // 2 :])
        return jnp.concatenate([low[0], high[0]], axis=1)

    in_grads = []
    out_grads = []
    for layer in range(2):
        gout, ggate, gconv, graw = weight_terms[layer]
        gout = reduced_out(gout)
        out_grads.append(
            plan.home(gout, 0, layer).astype(F32) + plan.home(gout, 1, layer).astype(F32)
        )

        def both(value):
            came = plan.swap(value, (1 - layer,))
            return (value, came) if layer == 0 else (came, value)

        gate_even, gate_odd = both(reduced_in(ggate))
        rest_even, rest_odd = both(reduced_in(jnp.concatenate([gconv, graw], axis=1)))
        ranks = [(even, odd) for even, odd in zip(range(half), range(half))]
        gates = []
        inputs = []
        raws = []
        pair = None
        for even, odd in ranks:
            gates += [gate_even[even], gate_odd[odd]]
            for part in (rest_even[even], rest_odd[odd]):
                term = part[:, :PAIR].astype(F32)
                pair = term if pair is None else pair + term
                inputs.append(part[:, PAIR:conv])
                raws.append(part[:, conv : conv + heads])
        in_grads.append(
            jnp.concatenate(
                [item.astype(F32) for item in gates + inputs] + [pair] + [item.astype(F32) for item in raws],
                axis=1,
            )
        )
    g_in = jnp.where(core == 0, in_grads[0], in_grads[1])
    g_out = jnp.where(core == 0, out_grads[0], out_grads[1])

    def flat_of(terms):
        ggain, gtaps, gheads, gskip, ggated = terms
        zeros = lambda *shape: jnp.zeros(shape, F32)

        def channels(value):
            whole = zeros(value.shape[0], INNER)
            whole = lax.dynamic_update_slice_in_dim(whole, value[:, PAIR:], rank * width, 1)
            return jnp.concatenate([whole, value[:, :PAIR]], axis=1)

        def per_head(value):
            return lax.dynamic_update_slice_in_dim(zeros(HEADS), value, rank * heads, 0)

        spread_gated = lax.dynamic_update_slice_in_dim(zeros(INNER), ggated[0], rank * width, 0)
        return jnp.concatenate(
            [
                ggain,
                channels(gtaps[: KCONV + 1]).reshape(-1),
                per_head(gheads[0, :heads]),
                per_head(gheads[1, :heads]),
                per_head(jnp.sum(gskip.reshape(heads, HEADDIM), axis=1)),
                spread_gated,
            ]
        )

    flat = [flat_of(terms) for terms in small_terms]
    sums = jnp.where(core == 0, flat[0], flat[1]) + plan.swap(jnp.where(core == 0, flat[1], flat[0]))
    for bit in (1, 2):
        sums = sums + plan.beside(sums, bit)
    hop = 1
    while hop < plan.seq:
        sums = sums + plan.along(sums, hop)
        hop *= 2
    sizes = (D, (KCONV + 1) * (INNER + PAIR), HEADS, HEADS, HEADS, INNER)
    pieces = []
    start = 0
    for size in sizes:
        pieces.append(sums[start : start + size])
        start += size
    g_norm, g_taps, g_dt, g_log, g_skip, g_gated = pieces
    g_taps = g_taps.reshape(KCONV + 1, INNER + PAIR)

    outs = []
    for batch in range(2):
        last = plan.home(result, batch, 1)
        first_grad = plan.home(start_grad, batch, 0)
        outs.append(jnp.where(core == 1, last, first_grad).astype(F32))
    ends_out = jnp.stack(outs)[None, :, None]
    return (
        ends_out,
        g_norm[None],
        g_in[None],
        g_taps[None, :KCONV],
        g_taps[KCONV][None],
        g_dt[None],
        g_log[None],
        g_skip[None],
        g_gated[None],
        g_out[None],
    )


def solution(mesh):
    placed = (
        P("section", None, "wshard", "seq", None),
        P(None, "wshard", None),
        P(None, "wshard", None),
        P("section", None),
        P("section", "wshard", None),
        P("section", None, None),
        P("section", None),
        P("section", None),
        P("section", None),
        P("section", None),
        P("section", None),
        P("section", "wshard", None),
    )
    return jax.shard_map(
        on_device,
        mesh=mesh,
        in_specs=placed,
        out_specs=(
            P("section", None, "wshard", "seq", None),
            P("section", None),
            P("section", ("seq", "wshard"), None),
            P("section", None, None),
            P("section", None),
            P("section", None),
            P("section", None),
            P("section", None),
            P("section", None),
            P("section", ("seq", "wshard"), None),
        ),
        check_vma=False,
    )
```

```python
import functools
import types

import jax
import jax.numpy as jnp
from jax import lax
from jax.experimental import pallas as pl
from jax.experimental.pallas import tpu as pltpu
from jax.sharding import PartitionSpec as P

D = 1024
HEADDIM = 64
STATE = 128
KCONV = 4
BLOCK = 256
INNER = 2048
HEADS = 32
PAIR = 2 * STATE
LANES = 128
EPS = 1e-05
NEG = -1e30
BF = jnp.bfloat16
F32 = jnp.float32
HIGH = lax.Precision.HIGHEST
AXES = ("section", "seq", "wshard")
VMEM_LIMIT = 58 << 20


def nn(a, b, precision=None):
    return lax.dot_general(
        a, b, (((1,), (0,)), ((), ())), preferred_element_type=F32, precision=precision
    )


def nt(a, b):
    return lax.dot_general(a, b, (((1,), (1,)), ((), ())), preferred_element_type=F32)


def tn(a, b):
    return lax.dot_general(a, b, (((0,), (0,)), ((), ())), preferred_element_type=F32)


def two(x):
    hi = x.astype(BF)
    lo = (x - hi.astype(F32)).astype(BF)
    return jnp.concatenate([hi, lo], axis=1)


def iota(shape, dim):
    return lax.broadcasted_iota(jnp.int32, shape, dim)


def column(row):
    return jnp.broadcast_to(row, (LANES, row.shape[1])).T[:, :1]


def as_row(col):
    return jnp.broadcast_to(col, (col.shape[0], LANES)).T[:1]


def sigmoid(x):
    return 1.0 / (1.0 + jnp.exp(-x))


def softplus(x):
    return jnp.maximum(x, 0.0) + jnp.log1p(jnp.exp(-jnp.abs(x)))


def full(shape):
    return pl.BlockSpec(shape, lambda i: (0,) * len(shape))


def launch(name, body, grid, ins, outs, scratch=(), flops=0, nbytes=0):
    names = [item[0] for item in ins] + [item[0] for item in outs] + [item[0] for item in scratch]

    def kernel(*refs):
        body(types.SimpleNamespace(**dict(zip(names, refs))))

    results = pl.pallas_call(
        kernel,
        grid=grid,
        in_specs=[item[2] for item in ins],
        out_specs=[item[3] for item in outs],
        out_shape=[jax.ShapeDtypeStruct(item[1], item[2]) for item in outs],
        scratch_shapes=[item[1] for item in scratch],
        compiler_params=pltpu.CompilerParams(
            dimension_semantics=("arbitrary",) * len(grid), vmem_limit_bytes=VMEM_LIMIT
        ),
        cost_estimate=pl.CostEstimate(flops=flops, bytes_accessed=nbytes, transcendentals=0),
        name=name,
    )(*[item[1] for item in ins])
    return types.SimpleNamespace(**dict(zip([item[0] for item in outs], results)))


def small():
    return pl.BlockSpec(memory_space=pltpu.SMEM)


def rows_of(width, first=0):
    return pl.BlockSpec((BLOCK, width), lambda i: (first + i, 0))


def turned(width, last):
    return pl.BlockSpec((BLOCK, width), lambda i: (last - i, 0))


def place(orders, halves):
    mine, theirs = halves
    total = 2 * mine.shape[0]

    def body(r):
        at = pl.program_id(0) * BLOCK + iota((BLOCK, total // 2), 0)
        first = (r.mine_order[...] == at).astype(BF)
        second = (r.their_order[...] == at).astype(BF)
        r.out[...] = (nn(first, r.mine[...]) + nn(second, r.theirs[...])).astype(BF)

    return launch(
        "place",
        body,
        (total // BLOCK,),
        [
            ("mine_order", orders[0], full((1, total // 2))),
            ("their_order", orders[1], full((1, total // 2))),
            ("mine", mine, full((total // 2, D))),
            ("theirs", theirs, full((total // 2, D))),
        ],
        [("out", (total, D), BF, rows_of(D))],
        flops=2 * total * total * D,
        nbytes=4 * total * D,
    ).out


def assemble(spot, part, near, far, theirs, wide):
    rows = part.shape[0]
    side = 2 * wide + LANES
    total = PAIR + side

    def body(r):
        w = r.spot[1]

        def move(source, row, base, pair):
            place_at = pl.ds(pl.multiple_of(row, rows), rows)
            r.out[place_at, :wide] = source[:, base : base + wide]
            r.out[place_at, wide : wide + PAIR] = source[:, pair : pair + PAIR]
            r.out[place_at, wide + PAIR :] = source[:, base + wide : base + side]

        for core in range(2):

            @pl.when(r.spot[0] == core)
            def _():
                own = core * (side + PAIR)
                shards = (w, w ^ (1 + core), w ^ (2 - core), w ^ 3)
                sources = (r.part, r.near, r.far.at[0], r.far.at[1])
                for source, shard in zip(sources, shards):
                    move(source, (2 * shard + core) * rows, own, side)
                shards = (w, w ^ (2 - core), w ^ (1 + core), w ^ 3)
                for index, shard in enumerate(shards):
                    source = r.theirs.at[index]
                    move(source, (2 * shard + 1 - core) * rows, core * PAIR, (1 - core) * side)

    return launch(
        "assemble",
        body,
        (1,),
        [
            ("spot", spot, small()),
            ("part", part, full(part.shape)),
            ("near", near, full(near.shape)),
            ("far", far, full(far.shape)),
            ("theirs", theirs, full(theirs.shape)),
        ],
        [("out", (8 * rows, total), BF, full((8 * rows, total)))],
        nbytes=32 * rows * total,
    ).out


def block_terms(raw, dtb, rate_sign, offset):
    rate = softplus(raw + dtb)
    lower = (iota((BLOCK, BLOCK), 1) <= iota((BLOCK, BLOCK), 0)).astype(F32)
    level = nn(lower, rate * rate_sign, HIGH)
    local = iota((BLOCK, 1), 0)
    end = level[BLOCK - 1 :]
    end_offset = offset[BLOCK - 1 :]
    head = jnp.where(offset > local, jnp.exp(level), 0.0)
    fade = jnp.where(local >= BLOCK - 1 - end_offset, jnp.exp(end - level), 0.0)
    carry = jnp.where(end_offset > BLOCK - 1, jnp.exp(end), 0.0)
    return rate, level, head, fade, carry


def either(flag, first, second):
    chosen = flag.astype(F32)
    return chosen * first.astype(F32) + (1.0 - chosen) * second.astype(F32)


def keep_or_give(r, core, block, split, value):
    slot = pl.ds(pl.multiple_of(block % split * BLOCK, BLOCK), BLOCK)

    @pl.when(block // split == core)
    def _():
        r.keep[slot] = value

    @pl.when(block // split != core)
    def _():
        r.away[slot] = value


def forward_body(layer, begin, wide, split, r):
    heads = wide // HEADDIM
    conv = PAIR + wide
    step = pl.program_id(0)
    core = r.spot[0]

    @pl.when(step == 0)
    def _():
        if begin:
            r.state[...] = jnp.zeros_like(r.state)
            r.halo[...] = jnp.zeros_like(r.halo)
        else:
            r.state[...] = r.state_in[...]
            r.halo[...] = r.halo_in[...]

    tokens = r.tokens[...].astype(F32)
    if layer == 1:
        scale = lax.rsqrt(column(r.last_rows[0][0:1]) / INNER + EPS)
        summed = either(step // split == core, r.mine[...], r.theirs[...])
        low = (tokens + summed * scale).astype(BF)
        r.next[...] = low
        tokens = low.astype(F32)
    scale = lax.rsqrt(jnp.mean(tokens * tokens, axis=1, keepdims=True) + EPS)
    x = (tokens * scale * r.gain[...]).astype(BF)
    r.normed[...] = x
    projected = nn(x, r.w[...])
    gate = projected[:, :wide]
    r.gate[...] = gate
    cin_low = projected[:, wide : wide + conv].astype(BF)
    r.cin[...] = cin_low
    raw_low = projected[:, wide + conv :].astype(BF)
    r.raw[...] = raw_low
    pos = r.pos[...]
    label_col = pos[:, 0:1]
    offset = pos[:, 1:2]
    cin = cin_low.astype(F32)
    longer = jnp.concatenate([r.halo[...], cin], axis=0)
    r.halo[...] = cin[BLOCK - 8 :]
    taps = r.taps[...]
    pre = taps[KCONV : KCONV + 1] + taps[KCONV - 1 : KCONV] * cin
    for index in range(KCONV - 1):
        delay = KCONV - 1 - index
        moved = longer[8 - delay : 8 - delay + BLOCK]
        pre = pre + jnp.where(offset >= delay, taps[index : index + 1] * moved, 0.0)
    r.pre[...] = pre
    mixed_conv = (pre * sigmoid(pre)).astype(BF)
    write = mixed_conv[:, :STATE]
    read = mixed_conv[:, STATE:PAIR]
    xs = mixed_conv[:, PAIR:]
    xs_float = xs.astype(F32)
    terms = r.terms[...]
    rate, level, head, fade, carry = block_terms(
        raw_low.astype(F32), terms[0:1], terms[1:2], offset
    )
    level_rows = level.T
    rate_rows = rate.T
    spread = r.spread[...]
    state = r.state[...]
    r.states[0] = state
    wides = r.wides[...]
    mixed = nn(two(head), spread) * nn(read, state.astype(BF)) + wides[0:1] * xs_float
    gram = nt(read, write)
    inside = (label_col == r.label[0]) & (iota((BLOCK, BLOCK), 1) <= iota((BLOCK, BLOCK), 0))
    closed = jnp.where(inside, 0.0, NEG)
    parts = []
    for first in range(0, heads, 2):
        span = xs[:, first * HEADDIM : (first + 2) * HEADDIM]
        mixing = []
        values = []
        for h in range(first, first + 2):
            weight = jnp.exp(level[:, h : h + 1] - level_rows[h : h + 1] + closed)
            mixing.append((gram * (weight * rate_rows[h : h + 1])).astype(BF))
            own = iota(span.shape, 1) // HEADDIM == h - first
            values.append(jnp.where(own, span, jnp.zeros_like(span)))
        parts.append(nn(jnp.concatenate(mixing, axis=1), jnp.concatenate(values, axis=0)))
    mixed = mixed + jnp.concatenate(parts, axis=1)
    mixed_low = mixed.astype(BF)
    r.mixed[...] = mixed_low
    carry_wide = nn(two(jnp.broadcast_to(carry, (8, LANES))), spread)[:1]
    written = (nn(two(fade * rate), spread) * xs_float).astype(BF)
    r.state[...] = carry_wide * state + tn(write, written)
    gv = mixed_low.astype(F32) * (gate * sigmoid(gate))
    r.rows[0, 0:1] = as_row(jnp.sum(gv * gv, axis=1, keepdims=True))
    scaled = gv * wides[1:2]
    if layer == 1:
        dotted = nt(r.dout[...], r.w_out[...]) * scaled
        r.rows[0, 1:2] = as_row(jnp.sum(dotted, axis=1, keepdims=True))
    else:
        r.rows[0, 1:2] = jnp.zeros((1, BLOCK), F32)
    keep_or_give(r, core, step, split, nn(scaled.astype(BF), r.w_out[...]).astype(BF))


def forward(layer, part, spot, env, tokens, before, weights, vectors, carried, dout):
    w, w_out = weights
    wide = w_out.shape[0]
    conv = PAIR + wide
    count = tokens.shape[0] // BLOCK // 2
    split = count // 2
    first = part * count
    total = count * BLOCK
    row = pl.BlockSpec((1, 2, BLOCK), lambda i: (i, 0, 0))
    ins = [
        ("spot", spot, small()),
        ("tokens", tokens, rows_of(D, first)),
        ("gain", vectors["gain"], full((1, D))),
        ("w", w, full(w.shape)),
        ("w_out", w_out, full(w_out.shape)),
        ("taps", vectors["taps"], full((8, conv))),
        ("terms", vectors["terms"], full((8, LANES))),
        ("wides", vectors["wides"], full((8, wide))),
        ("spread", env.spread, full(env.spread.shape)),
        ("pos", env.pos, rows_of(3, first)),
        ("label", env.label_row, pl.BlockSpec((1, 1, BLOCK), lambda i: (first + i, 0, 0))),
    ]
    outs = [
        ("normed", (total, D), BF, rows_of(D)),
        ("gate", (total, wide), F32, rows_of(wide)),
        ("pre", (total, conv), F32, rows_of(conv)),
        ("cin", (total, conv), BF, rows_of(conv)),
        ("raw", (total, LANES), BF, rows_of(LANES)),
        ("mixed", (total, wide), BF, rows_of(wide)),
        ("states", (count, STATE, wide), F32, pl.BlockSpec((1, STATE, wide), lambda i: (i, 0, 0))),
        ("rows", (count, 2, BLOCK), F32, row),
        ("keep", (total // 2, D), BF, full((total // 2, D))),
        ("away", (total // 2, D), BF, full((total // 2, D))),
        ("state", (STATE, wide), F32, full((STATE, wide))),
        ("halo", (8, conv), F32, full((8, conv))),
    ]
    if part == 1:
        ins += [
            ("state_in", carried.state, full((STATE, wide))),
            ("halo_in", carried.halo, full((8, conv))),
        ]
    if layer == 1:
        block = pl.BlockSpec((BLOCK, D), lambda i: (i % split, 0))
        mine, theirs, last_rows = before
        ins += [
            ("mine", mine, block),
            ("theirs", theirs, block),
            ("last_rows", last_rows, row),
            ("dout", dout, rows_of(D, first)),
        ]
        outs.append(("next", (total, D), BF, rows_of(D)))
    return launch(
        "forward",
        functools.partial(forward_body, layer, part == 0, wide, split),
        (count,),
        ins,
        outs,
        flops=4 * total * D * (2 * wide + conv),
        nbytes=total * D * 16,
    )


def ungate_body(layer, wide, count, split, r):
    step = pl.program_id(0)
    block = count - 1 - step
    core = r.spot[0]

    @pl.when(step == 0)
    def _():
        r.ggated[...] = jnp.zeros_like(r.ggated)
        if layer == 0:
            r.ggain[...] = jnp.zeros_like(r.ggain)

    scale = lax.rsqrt(column(r.rows[0][0:1]) / INNER + EPS)
    if layer == 1:
        dout = r.dout[...]
        dots = column(r.rows[0][1:2])
    else:
        flag = block // split == core
        grad = either(flag, r.grad_mine[...], r.grad_theirs[...])
        dtokens, dgain = unnorm(r.tokens[...].astype(F32), r.gain[...], grad)
        r.ggain[...] += dgain
        dout = (r.dlater[...].astype(F32) + dtokens).astype(BF)
        r.dout[...] = dout
        summed = either(flag, r.mine[...], r.theirs[...])
        dots = jnp.sum(dout.astype(F32) * summed, axis=1, keepdims=True)
    gate = r.gate[...]
    gain = r.wides[1:2]
    mixed = r.mixed[...].astype(F32)
    sig = sigmoid(gate)
    act = gate * sig
    normal = mixed * act * scale
    grad_out = nt(dout, r.w_out[...])
    shared = dots * scale / INNER
    grad_gv = scale * (grad_out * gain - normal * shared)
    r.dmixed[...] = (grad_gv * act).astype(BF)
    r.dgate[...] = (grad_gv * mixed * (sig * (1.0 + gate * (1.0 - sig)))).astype(BF)
    r.ggated[...] += jnp.sum(grad_out * normal, axis=0, keepdims=True)
    r.normed_out[...] = (normal * gain).astype(BF)


def unnorm(tokens, gain, grad):
    scale = lax.rsqrt(jnp.mean(tokens * tokens, axis=1, keepdims=True) + EPS)
    normal = tokens * scale
    inner = grad * gain
    dtokens = scale * (inner - normal * jnp.mean(inner * normal, axis=1, keepdims=True))
    return dtokens, jnp.sum(grad * normal, axis=0, keepdims=True)


def ungate(layer, part, spot, kept, rows, w_out, vectors, above):
    total, wide = kept.mixed.shape
    count = total // BLOCK
    split = count // 2
    last = count - 1
    row = pl.BlockSpec((1, 2, BLOCK), lambda i: (last - i, 0, 0))
    ins = [
        ("spot", spot, small()),
        ("rows", rows, row),
        ("gate", kept.gate, turned(wide, last)),
        ("mixed", kept.mixed, turned(wide, last)),
        ("wides", vectors["wides"], full((8, wide))),
        ("w_out", w_out, full((wide, D))),
    ]
    outs = [
        ("dmixed", (total, wide), BF, turned(wide, last)),
        ("dgate", (total, wide), BF, turned(wide, last)),
        ("normed_out", (total, wide), BF, turned(wide, last)),
        ("ggated", (1, wide), F32, full((1, wide))),
    ]
    if layer == 1:
        ins.append(("dout", above.dout, turned(D, part * count + last)))
    else:
        block = pl.BlockSpec((BLOCK, D), lambda i: ((last - i) % split, 0))
        ins += [
            ("grad_mine", above.grad[0], block),
            ("grad_theirs", above.grad[1], block),
            ("mine", above.summed[0], block),
            ("theirs", above.summed[1], block),
            ("tokens", above.tokens, turned(D, last)),
            ("gain", above.gain, full((1, D))),
            ("dlater", above.dout, turned(D, part * count + last)),
        ]
        outs += [("dout", (total, D), BF, turned(D, last)), ("ggain", (1, D), F32, full((1, D)))]
    return launch(
        "ungate",
        functools.partial(ungate_body, layer, wide, count, split),
        (count,),
        ins,
        outs,
        flops=2 * total * D * wide,
        nbytes=total * (wide * 10 + D * 4),
    )


def backward_body(begin, wide, count, split, r):
    heads = wide // HEADDIM
    conv = PAIR + wide
    step = pl.program_id(0)
    block = count - 1 - step
    core = r.spot[0]

    @pl.when(step == 0)
    def _():
        if begin:
            r.dstate[...] = jnp.zeros_like(r.dstate)
            r.halo[...] = jnp.zeros_like(r.halo)
        else:
            r.dstate[...] = r.dstate_in[...]
            r.halo[...] = r.halo_in[...]
        r.gtaps[...] = jnp.zeros_like(r.gtaps)
        r.gheads[...] = jnp.zeros_like(r.gheads)
        r.gskip[...] = jnp.zeros_like(r.gskip)

    pos = r.pos[...]
    label_col = pos[:, 0:1]
    offset = pos[:, 1:2]
    remain = pos[:, 2:3]
    pre = r.pre[...]
    sig = sigmoid(pre)
    mixed_conv = (pre * sig).astype(BF)
    write = mixed_conv[:, :STATE]
    read = mixed_conv[:, STATE:PAIR]
    xs = mixed_conv[:, PAIR:]
    xs_float = xs.astype(F32)
    raw = r.raw[...].astype(F32)
    terms = r.terms[...]
    dtb = terms[0:1]
    sign = terms[1:2]
    rate, level, head, fade, carry = block_terms(raw, dtb, sign, offset)
    tail = fade * rate
    level_rows = level.T
    spread = r.spread[...]
    fold = r.fold[...]
    dy = r.dmixed[...]
    dy_float = dy.astype(F32)
    state = r.states[0]
    state_low = state.astype(BF)
    dstate = r.dstate[...]
    dstate_low = dstate.astype(BF)
    dhead = nn(two(dy_float * nn(read, state_low)), fold)
    tail_wide = nn(two(tail), spread)
    scaled = (nn(two(head), spread) * dy_float).astype(BF)
    written = (tail_wide * xs_float).astype(BF)
    through = nn(write, dstate_low)
    dtail = nn(two(xs_float * through), fold)
    r.gskip[...] += jnp.sum(dy_float * xs_float, axis=0, keepdims=True)
    carry_wide = nn(two(jnp.broadcast_to(carry, (8, LANES))), spread)[:1]
    held = jnp.broadcast_to(jnp.sum(state * dstate, axis=0, keepdims=True), (8, wide))
    dcarry = nn(two(held), fold)[:1]

    gram = nt(write, read)
    inside = (label_col == r.label[0]) & (iota((BLOCK, BLOCK), 0) <= iota((BLOCK, BLOCK), 1))
    closed = jnp.where(inside, 0.0, NEG)
    lane = iota((1, LANES), 1)
    drate = jnp.zeros((BLOCK, LANES), F32)
    level_sums = []
    parts = []
    dgram = jnp.zeros((BLOCK, BLOCK), F32)
    for first in range(0, heads, 2):
        cut_at = slice(first * HEADDIM, (first + 2) * HEADDIM)
        xs_span = xs[:, cut_at]
        dy_span = dy[:, cut_at]
        mixing = []
        values = []
        for h in range(first, first + 2):
            own = iota(xs_span.shape, 1) // HEADDIM == h - first
            xs_own = jnp.where(own, xs_span, jnp.zeros_like(xs_span))
            values.append(jnp.where(own, dy_span, jnp.zeros_like(dy_span)))
            decay = jnp.exp(level_rows[h : h + 1] - level[:, h : h + 1] + closed)
            rate_col = rate[:, h : h + 1]
            weight = decay * rate_col
            mixing.append((gram * weight).astype(BF))
            dmix = nt(xs_own, dy_span)
            dgram = dgram + dmix * weight
            bare = dmix * gram * decay
            drate = drate + jnp.sum(bare, axis=1, keepdims=True) * (lane == h).astype(F32)
            level_sums.append(jnp.sum(bare * rate_col, axis=0, keepdims=True))
        parts.append(nn(jnp.concatenate(mixing, axis=1), jnp.concatenate(values, axis=0)))
    dxs = jnp.concatenate(parts, axis=1) + r.wides[0:1] * dy_float + tail_wide * through
    dgram_low = dgram.astype(BF)
    dread = tn(dgram_low, write) + nt(scaled, state_low)
    dwrite = nn(dgram_low, read) + nt(written, dstate_low)
    r.dstate[...] = carry_wide * dstate + tn(read, scaled)

    level_sums.append(jnp.zeros((LANES - heads, BLOCK), F32))
    tail_flow = dtail * tail
    local = iota((BLOCK, 1), 0)
    last = jnp.sum(tail_flow, axis=0, keepdims=True) + dcarry * carry
    dlevel = jnp.concatenate(level_sums, axis=0).T - rate * drate + dhead * head - tail_flow
    dlevel = dlevel + jnp.where(local == BLOCK - 1, last, 0.0)
    upper = (iota((BLOCK, BLOCK), 0) <= iota((BLOCK, BLOCK), 1)).astype(F32)
    dsum = nn(upper, dlevel, HIGH)
    drate = drate + dtail * fade + sign * dsum
    draw = drate * sigmoid(raw + dtb)
    r.gheads[0:1] += jnp.sum(draw, axis=0, keepdims=True)
    r.gheads[1:2] += jnp.sum(rate * dsum, axis=0, keepdims=True) * sign

    dpre = jnp.concatenate([dwrite, dread, dxs], axis=1) * (sig * (1.0 + pre * (1.0 - sig)))
    longer = jnp.concatenate([dpre, r.halo[...]], axis=0)
    r.halo[...] = dpre[:8]
    cin = r.cin[...].astype(F32)
    taps = r.taps[...]
    r.gtaps[KCONV : KCONV + 1] += jnp.sum(dpre, axis=0, keepdims=True)
    r.gtaps[KCONV - 1 : KCONV] += jnp.sum(dpre * cin, axis=0, keepdims=True)
    dcin = taps[KCONV - 1 : KCONV] * dpre
    for index in range(KCONV - 1):
        delay = KCONV - 1 - index
        moved = jnp.where(remain >= delay, longer[delay : delay + BLOCK], 0.0)
        dcin = dcin + taps[index : index + 1] * moved
        r.gtaps[index : index + 1] += jnp.sum(moved * cin, axis=0, keepdims=True)
    rest = jnp.concatenate([dcin, draw], axis=1).astype(BF)
    r.rest[...] = rest
    w = r.w[...]
    dnormed = nt(r.dgate[...], w[:, :wide]) + nt(rest, w[:, wide:])
    keep_or_give(r, core, block, split, dnormed.astype(BF))


def backward(part, spot, env, kept, grads, w, vectors, carried):
    total, wide = kept.mixed.shape
    conv = PAIR + wide
    count = total // BLOCK
    split = count // 2
    last = count - 1
    top = part * count + last
    ins = [
        ("spot", spot, small()),
        ("w", w, full(w.shape)),
        ("taps", vectors["taps"], full((8, conv))),
        ("terms", vectors["terms"], full((8, LANES))),
        ("wides", vectors["wides"], full((8, wide))),
        ("spread", env.spread, full(env.spread.shape)),
        ("fold", env.fold, full(env.fold.shape)),
        ("pos", env.pos, turned(3, top)),
        ("label", env.label_row, pl.BlockSpec((1, 1, BLOCK), lambda i: (top - i, 0, 0))),
        ("pre", kept.pre, turned(conv, last)),
        ("cin", kept.cin, turned(conv, last)),
        ("raw", kept.raw, turned(LANES, last)),
        ("states", kept.states, pl.BlockSpec((1, STATE, wide), lambda i: (last - i, 0, 0))),
        ("dmixed", grads.dmixed, turned(wide, last)),
        ("dgate", grads.dgate, turned(wide, last)),
    ]
    if part == 0:
        ins += [
            ("dstate_in", carried.dstate, full((STATE, wide))),
            ("halo_in", carried.halo, full((8, conv))),
        ]
    outs = [
        ("keep", (total // 2, D), BF, full((total // 2, D))),
        ("away", (total // 2, D), BF, full((total // 2, D))),
        ("rest", (total, conv + LANES), BF, turned(conv + LANES, last)),
        ("gtaps", (8, conv), F32, full((8, conv))),
        ("gheads", (8, LANES), F32, full((8, LANES))),
        ("gskip", (1, wide), F32, full((1, wide))),
        ("dstate", (STATE, wide), F32, full((STATE, wide))),
        ("halo", (8, conv), F32, full((8, conv))),
    ]
    return launch(
        "backward",
        functools.partial(backward_body, part == 1, wide, count, split),
        (count,),
        ins,
        outs,
        flops=6 * total * D * (2 * wide + conv),
        nbytes=total * D * 16,
    )


def weight_grads(spot, lefts, rights, seq, outer=None, size=0):
    depth = lefts[0].shape[1]
    wide = rights[0].shape[1]
    share = depth // (4 * seq)
    rows = depth // 4
    extra = size * (D // wide)

    def body(r):
        w = r.spot[1]
        z = r.spot[2]
        sides = ((r.keep, (0, r.spot[5])), (r.away, (r.spot[4], 3)))
        r.total[...] = tn(r.left0[...], r.right0[...]) + tn(r.left1[...], r.right1[...])
        for ref, shards in sides:
            for index, shard in enumerate(shards):
                for turn in range(seq):
                    start = ((z ^ turn) * 4 + (w ^ shard)) * share
                    piece = r.total[pl.ds(pl.multiple_of(start, share), share)]
                    ref[index, turn * share : (turn + 1) * share] = piece.astype(BF)
        if outer is None:
            return
        for part in range(D // wide):
            cols = slice(part * wide, (part + 1) * wide)
            r.outer[...] = tn(r.out0[...], r.dout0[...][:, cols]) + tn(
                r.out1[...], r.dout1[...][:, cols]
            )
            for ref, shards in sides:
                for index, shard in enumerate(shards):
                    start = pl.multiple_of((w ^ shard) * size, size)
                    begin = rows + part * size
                    ref[index, begin : begin + size] = r.outer[pl.ds(start, size)].astype(BF)

    ins = [("spot", spot, small())]
    for name, pair in (("left", lefts), ("right", rights)):
        for index in range(2):
            ins.append((name + str(index), pair[index], full(pair[index].shape)))
    scratch = [("total", pltpu.VMEM((depth, wide), F32))]
    if outer is not None:
        outs, douts = outer
        height = outs[0].shape[0]
        for index in range(2):
            ins.append(("out" + str(index), outs[index], full(outs[index].shape)))
            array, at = douts[index]
            spec = pl.BlockSpec((height, D), functools.partial(lambda at, i: (at, 0), at))
            ins.append(("dout" + str(index), array, spec))
        scratch.append(("outer", pltpu.VMEM((outs[0].shape[1], wide), F32)))
    height = rows + extra
    return launch(
        "weight_grads",
        body,
        (1,),
        ins,
        [
            ("keep", (2, height, wide), BF, full((2, height, wide))),
            ("away", (2, height, wide), BF, full((2, height, wide))),
        ],
        scratch=scratch,
        flops=4 * lefts[0].shape[0] * depth * wide,
        nbytes=4 * depth * wide,
    )


def finish(kind, part, spot, orders, values, before):
    count = values.count
    split = count // 2
    total = count * BLOCK

    def body(r):
        step = pl.program_id(0)
        core = r.spot[0]

        @pl.when(step == 0)
        def _():
            if before is None:
                r.own[...] = jnp.zeros_like(r.own)
                r.across[...] = jnp.zeros_like(r.across)
            else:
                r.own[...] = r.own_in[...]
                r.across[...] = r.across_in[...]
            if kind == "grad":
                r.ggain[...] = jnp.zeros_like(r.ggain)

        summed = either(step // split == core, r.mine[...], r.theirs[...])
        if kind == "grad":
            dtokens, dgain = unnorm(r.tokens[...].astype(F32), r.gain[...], summed)
            r.ggain[...] += dgain
            value = r.rest[...].astype(F32) + dtokens
        else:
            scale = lax.rsqrt(column(r.rows[0][0:1]) / INNER + EPS)
            value = r.rest[...].astype(F32) + summed * scale
        low = value.astype(BF)
        at = (part * count + step) * BLOCK + iota((BLOCK, BLOCK), 1)
        r.own[...] += nn((r.own_order[...] == at).astype(BF), low)
        r.across[...] += nn((r.far_order[...] == at).astype(BF), low)

    block = pl.BlockSpec((BLOCK, D), lambda i: (i % split, 0))
    ins = [
        ("spot", spot, small()),
        ("own_order", orders[0], full((BLOCK, 1))),
        ("far_order", orders[1], full((BLOCK, 1))),
        ("mine", values.summed[0], block),
        ("theirs", values.summed[1], block),
        ("rest", values.rest, rows_of(D)),
    ]
    outs = [
        ("own", (BLOCK, D), F32, full((BLOCK, D))),
        ("across", (BLOCK, D), F32, full((BLOCK, D))),
    ]
    if kind == "grad":
        ins += [
            ("tokens", values.tokens, rows_of(D, part * count)),
            ("gain", values.gain, full((1, D))),
        ]
        outs.append(("ggain", (1, D), F32, full((1, D))))
    else:
        ins.append(("rows", values.rows, pl.BlockSpec((1, 2, BLOCK), lambda i: (i, 0, 0))))
    if before is not None:
        ins += [
            ("own_in", before.own, full((BLOCK, D))),
            ("across_in", before.across, full((BLOCK, D))),
        ]
    return launch(
        "finish", body, (count,), ins, outs, flops=4 * total * BLOCK * D, nbytes=total * D * 8
    )


class Plan:
    def __init__(self):
        self.seq = lax.axis_size("seq")
        self.shards = lax.axis_size("wshard")
        self.half = self.seq // 2
        self.core = lax.axis_index("section")
        self.z = lax.axis_index("seq")
        self.w = lax.axis_index("wshard")
        self.batch = self.z // self.half
        self.place = self.z % self.half
        self.rank = 2 * self.place + self.core

    def send(self, value, route, cores=(0, 1)):
        pairs = []
        for c in range(2):
            for z in range(self.seq):
                for w in range(self.shards):
                    target = route(c, z, w)
                    if c in cores and target is not None:
                        source = (c * self.seq + z) * self.shards + w
                        tc, tz, tw = target
                        pairs.append((source, (tc * self.seq + tz) * self.shards + tw))
        return lax.ppermute(value, AXES, pairs)

    def swap(self, value, cores=(0, 1)):
        return self.send(value, lambda c, z, w: (1 - c, z, w), cores)

    def along(self, value, k, cores=(0, 1)):
        return self.send(value, lambda c, z, w: (c, z ^ k, w), cores)

    def first_side(self, value):
        return self.send(value, lambda c, z, w: (c, z, w ^ (1 + c)))

    def second_side(self, value):
        return self.send(value, lambda c, z, w: (c, z, w ^ (2 - c)))

    def own(self, first, second):
        return jnp.where(self.core == 0, first, second)

    def collect(self, near, far):
        pieces = [near]
        came = self.along(far, self.half)
        for k in range(1, self.half):
            pieces.append(self.along(near, k))
        pieces.append(came)
        for k in range(1, self.half):
            pieces.append(self.along(came, k))
        mine = jnp.concatenate(pieces, axis=0)
        return mine, self.swap(mine)

    def fold(self, terms):
        return add(terms.keep, self.swap(terms.away))

    def reduce(self, total):
        hop = 1
        while hop < self.half:
            total = add(total, self.along(total, hop))
            hop *= 2
        return total, self.swap(total)

    def total(self, value):
        value = value + self.swap(value)
        hop = 1
        while hop < self.half:
            value = value + self.along(value, hop)
            hop *= 2
        return value

    def home(self, value, batch, layer):
        half = self.half

        def route(c, z, w):
            if z // half != batch:
                return None
            return (layer, 2 * (z % half) + c, w)

        return self.send(value, route)

    def gather_chips(self, value, share):
        pieces = [value[:share]]
        for k in range(1, self.seq):
            pieces.append(self.along(value[k * share : (k + 1) * share], k))
        half = self.half
        terms = [add(pieces[k], pieces[k + half]) for k in range(half)]
        if half == 2:
            even = self.place == 0
            ordered = [jnp.where(even, terms[0], terms[1]), jnp.where(even, terms[1], terms[0])]
            return jnp.stack(ordered)
        stacked = jnp.stack(terms)
        return stacked[self.place ^ jnp.arange(half)]


def add(first, second):
    return (first.astype(F32) + second.astype(F32)).astype(BF)


def after(value, *others):
    return lax.optimization_barrier((value,) + others)[0]


def pick(value, index, axis=0):
    return lax.dynamic_index_in_dim(value, index, axis, keepdims=False)


def cut(value, start, size, axis):
    return lax.dynamic_slice_in_dim(value, start, size, axis)


def on_device(
    ends_in,
    seq_lengths,
    deal_order,
    norm_w,
    in_w,
    conv_w,
    conv_b,
    dt_bias,
    a_log,
    d_skip,
    gnorm_w,
    out_w,
):
    plan = Plan()
    core = plan.core
    half = plan.half
    rank = plan.rank
    seq = plan.seq
    rows = ends_in.shape[3]
    total = rows * seq
    count = total // BLOCK
    heads = HEADS // seq
    width = heads * HEADDIM
    wide = max(width, LANES)
    side = 2 * wide + LANES
    first = 1 + core
    second = 2 - core
    spot = jnp.stack([core, plan.w, plan.z, plan.place, first, second, rank, 0 * rank])
    spot = spot.astype(jnp.int32)

    start = 2 * width * plan.place
    gate_cols = cut(in_w[0], start, 2 * width, 1)
    input_cols = cut(in_w[0], INNER + start, 2 * width, 1)
    pair_cols = in_w[0][:, 2 * INNER : 2 * INNER + PAIR]
    raw_cols = cut(in_w[0], 2 * INNER + PAIR + 2 * heads * plan.place, 2 * heads, 1)

    def padded(value, size):
        return jnp.pad(value, ((0, 0), (0, size - value.shape[1])))

    chunk = jnp.concatenate(
        [
            padded(gate_cols[:, :width], wide),
            padded(input_cols[:, :width], wide),
            padded(raw_cols[:, :heads], LANES),
            pair_cols,
            padded(gate_cols[:, width:], wide),
            padded(input_cols[:, width:], wide),
            padded(raw_cols[:, heads:], LANES),
        ],
        axis=1,
    )
    split_rows = chunk.shape[0] // 2
    chunk_keep = cut(chunk, core * split_rows, split_rows, 0)
    chunk_came = plan.swap(cut(chunk, (1 - core) * split_rows, split_rows, 0))
    chunk_parts = [plan.own(chunk_keep, chunk_came), plan.own(chunk_came, chunk_keep)]

    half_rows = rows // 2
    ends_keep = cut(ends_in[0, :, 0], core * half_rows, half_rows, 1)
    ends_came = plan.swap(cut(ends_in[0, :, 0], (1 - core) * half_rows, half_rows, 1))
    end_parts = [plan.own(ends_keep, ends_came), plan.own(ends_came, ends_keep)]

    order = pick(deal_order[:, 0], plan.batch)
    by_chip = order.reshape(seq, 2, half_rows)[plan.z ^ jnp.arange(seq)]
    orders = (
        pick(by_chip, core, 1).reshape(1, total // 2),
        pick(by_chip, 1 - core, 1).reshape(1, total // 2),
    )
    end_orders = (
        cut(order, rows * plan.z, rows, 0).reshape(rows, 1),
        cut(order, rows * (plan.z ^ half), rows, 0).reshape(rows, 1),
    )

    def collect(part):
        return plan.collect(pick(part, plan.batch), pick(part, 1 - plan.batch))

    started = collect(end_parts[0])

    def in_weights(part):
        near = plan.first_side(part)
        far = plan.second_side(jnp.stack([part, near]))
        give = jnp.stack([part, near, far[0], far[1]])
        theirs = plan.swap(cut(give, (1 - core) * side, side + PAIR, 2))
        return assemble(spot, part, near, far, theirs, wide), near

    def out_weights(part):
        if half == 2:
            low_shard = plan.w // 2

            def route(c, z, w):
                return (c, z, w ^ 2) if w // 2 == z % half else None

            came = plan.send(part, route)
            here = jnp.where(low_shard == plan.place, part, came)
            beside = plan.send(here, lambda c, z, w: (c, z, w ^ 1))
            same = plan.w % 2 == core
            mine = jnp.where(same, here, beside)
            theirs = plan.swap(jnp.where(same, beside, here))
            return jnp.concatenate([plan.own(mine, theirs), plan.own(theirs, mine)], axis=0)
        half_part = part.shape[0]
        near = plan.first_side(part)
        far = plan.second_side(jnp.stack([part, near]))
        pieces = jnp.stack([part, near, far[0], far[1]])
        shards = jnp.arange(4) ^ plan.w
        ordered = pieces[jnp.where((shards == 0) | (shards == 3), shards, jnp.where(core == 0, shards, 3 - shards))]
        other = plan.swap(ordered)
        whole = jnp.stack([plan.own(ordered, other), plan.own(other, ordered)], axis=1)
        whole = whole.reshape(8 * half_part, D)
        return jnp.pad(cut(whole, width * rank, width, 0), ((0, wide - width), (0, 0)))

    out_rows = out_w.shape[1] // 2
    out_keep = cut(out_w[0], core * out_rows, out_rows, 0)
    out_came = plan.swap(cut(out_w[0], (1 - core) * out_rows, out_rows, 0))
    out_parts = [plan.own(out_keep, out_came), plan.own(out_came, out_keep)]

    w_first, in_sent = in_weights(chunk_parts[0])
    w_out_first = out_weights(after(out_parts[0], in_sent))
    w_second, in_sent = in_weights(after(chunk_parts[1], w_first, w_out_first))
    w_out_second = out_weights(after(out_parts[1], in_sent))
    weights = [(w_first, w_out_first), (w_second, w_out_second)]

    tokens = place(orders, started)
    cotangent = place(orders, collect(after(end_parts[1], *started)))

    lengths = pick(seq_lengths[:, 0], plan.batch)
    ends = jnp.cumsum(lengths)
    at = iota((total,), 0)
    passed = at[:, None] >= ends[None, :]
    label = jnp.sum(passed.astype(jnp.int32), axis=1)
    begin = jnp.max(jnp.where(passed, ends[None, :], 0), axis=1)
    finished = jnp.min(jnp.where(passed, total, ends[None, :]), axis=1)
    channel_head = iota((LANES, wide), 1) // HEADDIM
    hot = (channel_head == iota((LANES, wide), 0)).astype(BF)
    env = types.SimpleNamespace(
        pos=jnp.stack([label, at - begin, finished - 1 - at], axis=1),
        label_row=label.reshape(count, 1, BLOCK),
        spread=jnp.concatenate([hot, hot], axis=0),
        fold=jnp.concatenate([hot.T, hot.T], axis=0),
    )

    own_small = jnp.concatenate(
        [
            norm_w[0],
            conv_w[0].reshape(-1),
            conv_b[0],
            dt_bias[0],
            a_log[0],
            d_skip[0],
            gnorm_w[0],
        ]
    )
    other_small = plan.swap(own_small)
    sizes = (D, (KCONV + 1) * (INNER + PAIR), HEADS, HEADS, HEADS, INNER)

    def pieces_of(flat):
        pieces = []
        begin = 0
        for size in sizes:
            pieces.append(flat[begin : begin + size])
            begin += size
        return pieces

    def vectors_of(layer):
        flat = jnp.where(core == layer, own_small, other_small)
        gain, taps, dtb, log_rate, skip, gated = pieces_of(flat)
        taps = taps.reshape(KCONV + 1, INNER + PAIR)
        channels = jnp.concatenate(
            [taps[:, INNER:], padded(cut(taps, rank * width, width, 1), wide)], axis=1
        )

        def lanes(value):
            return padded(cut(value, rank * heads, heads, 0)[None], LANES)

        terms = jnp.concatenate([lanes(dtb), lanes(-jnp.exp(log_rate))], axis=0)
        skips = jnp.repeat(cut(skip, rank * heads, heads, 0), HEADDIM)[None]
        wides = jnp.concatenate([skips, cut(gated, rank * width, width, 0)[None]], axis=0)
        return {
            "gain": gain[None],
            "taps": jnp.pad(channels, ((0, 8 - KCONV - 1), (0, 0))),
            "terms": jnp.pad(terms, ((0, 6), (0, 0))),
            "wides": jnp.pad(wides, ((0, 6), (0, wide - width))),
        }

    vectors = [vectors_of(0), vectors_of(1)]

    kept = [[], []]
    rows_summed = [[], []]
    summed = [[], []]
    turn = spot
    for layer in range(2):
        carried = None
        for part in range(2):
            before = None
            if layer == 1:
                before = summed[0][part] + (rows_summed[0][part],)
            carried = forward(
                layer, part, turn, env, tokens, before, weights[layer], vectors[layer], carried, cotangent
            )
            kept[layer].append(carried)
            rows_summed[layer].append(plan.total(carried.rows))
            folded = plan.fold(carried)
            if layer == 0:
                turn = after(spot, folded)
            summed[layer].append(plan.reduce(folded))

    grads_summed = [[None, None], [None, None]]
    turn = spot
    small_terms = [None, None]
    weight_terms = [None, None]
    douts = [None, None]
    for layer in (1, 0):
        carried = None
        gated = [None, None]
        scans = [None, None]
        for part in (1, 0):
            above = types.SimpleNamespace(dout=cotangent)
            if layer == 0:
                above.grad = grads_summed[1][part]
                above.summed = summed[0][part]
                above.tokens = kept[1][part].next
                above.gain = vectors[1]["gain"]
            gated[part] = ungate(
                layer,
                part,
                turn if part == 1 else spot,
                kept[layer][part],
                rows_summed[layer][part],
                weights[layer][1],
                vectors[layer],
                above,
            )
            carried = backward(
                part, turn, env, kept[layer][part], gated[part], weights[layer][0], vectors[layer], carried
            )
            scans[part] = carried
            folded = plan.fold(carried)
            turn = after(spot, folded)
            grads_summed[layer][part] = plan.reduce(folded)
        normed = [item.normed for item in kept[layer]]
        if layer == 1:
            dout_parts = ((cotangent, 0), (cotangent, 1))
        else:
            dout_parts = ((gated[0].dout, 0), (gated[1].dout, 0))
            douts = [item.dout for item in gated]
            gain_terms = gated[0].ggain + gated[1].ggain
        weight_terms[layer] = (
            weight_grads(
                spot,
                normed,
                [item.dgate for item in gated],
                seq,
                ([item.normed_out for item in gated], dout_parts),
                width // 4,
            ),
            weight_grads(spot, normed, [item.rest for item in scans], seq),
        )
        small_terms[layer] = (
            scans[0].gtaps + scans[1].gtaps,
            scans[0].gheads + scans[1].gheads,
            scans[0].gskip + scans[1].gskip,
            gated[0].ggated + gated[1].ggated,
        )

    result = None
    for part in (0, 1):
        values = types.SimpleNamespace(
            count=count // 2, summed=summed[1][part], rest=kept[1][part].next, rows=rows_summed[1][part]
        )
        result = finish("result", part, spot, end_orders, values, result)
    start_grad = None
    first_gain = None
    for part in (1, 0):
        values = types.SimpleNamespace(
            count=count // 2,
            summed=grads_summed[0][part],
            rest=douts[part],
            tokens=tokens,
            gain=vectors[0]["gain"],
        )
        start_grad = finish("grad", part, spot, end_orders, values, start_grad)
        gain = start_grad.ggain
        first_gain = gain if first_gain is None else first_gain + gain
    own_end = plan.own(start_grad.own, result.own)
    result_far = plan.along(result.across.astype(BF), half, (1,))
    grad_far = plan.along(start_grad.across.astype(BF), half, (0,))
    far_end = plan.own(grad_far, result_far).astype(F32)
    lower = plan.batch == 0
    ends_out = jnp.stack([jnp.where(lower, own_end, far_end), jnp.where(lower, far_end, own_end)])
    ends_out = ends_out[None, :, None]

    def reduced(terms):
        came = plan.first_side(terms.away)
        kept_back = add(terms.keep[0], came[0])
        given = add(terms.keep[1], came[1])
        return add(kept_back, plan.second_side(given))

    share = D // (4 * seq)
    gate_rows = D // 4
    in_grads = []
    out_grads = []
    for layer in range(2):
        gates, rest = weight_terms[layer]
        gates = reduced(gates)
        rest = reduced(rest)
        outs = gates[gate_rows:]
        outs = add(plan.home(outs, 0, layer), plan.home(outs, 1, layer)).astype(F32)
        size = width // 4
        pieces = [outs[k * size : (k + 1) * size] for k in range(D // wide)]
        out_grads.append(jnp.concatenate(pieces, axis=1))

        def both(value):
            came = plan.swap(value, (1 - layer,))
            return (value, came) if layer == 0 else (came, value)

        gate_sides = both(plan.gather_chips(gates, share))
        rest_sides = both(plan.gather_chips(rest, share))
        gate_list = []
        inputs = []
        raws = []
        pair = None
        for place_at in range(half):
            for gate_side, rest_side in zip(gate_sides, rest_sides):
                gate_list.append(gate_side[place_at][:, :width].astype(F32))
                part = rest_side[place_at].astype(F32)
                pair = part[:, :PAIR] if pair is None else pair + part[:, :PAIR]
                inputs.append(part[:, PAIR : PAIR + width])
                raws.append(part[:, PAIR + wide : PAIR + wide + heads])
        in_grads.append(jnp.concatenate(gate_list + inputs + [pair] + raws, axis=1))
    g_in = plan.own(in_grads[0], in_grads[1])
    g_out = plan.own(out_grads[0], out_grads[1])

    gains = [first_gain, gain_terms]

    def flat_of(layer):
        gtaps, gheads, gskip, ggated = small_terms[layer]
        zeros = lambda *shape: jnp.zeros(shape, F32)
        inner = lax.dynamic_update_slice_in_dim(
            zeros(KCONV + 1, INNER), gtaps[: KCONV + 1, PAIR : PAIR + width], rank * width, 1
        )
        channels = jnp.concatenate([inner, gtaps[: KCONV + 1, :PAIR]], axis=1)

        def per_head(value):
            return lax.dynamic_update_slice_in_dim(zeros(HEADS), value, rank * heads, 0)

        return jnp.concatenate(
            [
                channels.reshape(-1),
                per_head(gheads[0, :heads]),
                per_head(gheads[1, :heads]),
                per_head(jnp.sum(gskip[0, :width].reshape(heads, HEADDIM), axis=1)),
                lax.dynamic_update_slice_in_dim(zeros(INNER), ggated[0, :width], rank * width, 0),
            ]
        )

    def spread_sum(values):
        sums = plan.own(values[0], values[1]) + plan.swap(plan.own(values[1], values[0]))
        sums = sums + plan.first_side(sums)
        sums = sums + plan.second_side(sums)
        hop = 1
        while hop < seq:
            sums = sums + plan.along(sums, hop)
            hop *= 2
        return sums

    mine = (rank == 0).astype(F32)
    g_norm = spread_sum([gains[0][0] * mine, gains[1][0] * mine])
    sums = spread_sum([flat_of(0), flat_of(1)])
    _, g_taps, g_dt, g_log, g_skip, g_gated = pieces_of(jnp.concatenate([g_norm, sums]))
    g_taps = g_taps.reshape(KCONV + 1, INNER + PAIR)
    return (
        ends_out,
        g_norm[None],
        g_in[None],
        g_taps[None, :KCONV],
        g_taps[KCONV][None],
        g_dt[None],
        g_log[None],
        g_skip[None],
        g_gated[None],
        g_out[None],
    )


def solution(mesh):
    placed = (
        P("section", None, "wshard", "seq", None),
        P(None, "wshard", None),
        P(None, "wshard", None),
        P("section", None),
        P("section", "wshard", None),
        P("section", None, None),
        P("section", None),
        P("section", None),
        P("section", None),
        P("section", None),
        P("section", None),
        P("section", "wshard", None),
    )
    return jax.shard_map(
        on_device,
        mesh=mesh,
        in_specs=placed,
        out_specs=(
            P("section", None, "wshard", "seq", None),
            P("section", None),
            P("section", ("seq", "wshard"), None),
            P("section", None, None),
            P("section", None),
            P("section", None),
            P("section", None),
            P("section", None),
            P("section", None),
            P("section", ("seq", "wshard"), None),
        ),
        check_vma=False,
    )
```

```python
import functools
import types

import jax
import jax.numpy as jnp
from jax import lax
from jax.experimental import pallas as pl
from jax.experimental.pallas import tpu as pltpu
from jax.sharding import PartitionSpec as P

D = 1024
HEADDIM = 64
STATE = 128
KCONV = 4
BLOCK = 256
INNER = 2048
HEADS = 32
PAIR = 2 * STATE
LANES = 128
EPS = 1e-05
NEG = -1e30
BF = jnp.bfloat16
F32 = jnp.float32
HIGH = lax.Precision.HIGHEST
AXES = ("section", "seq", "wshard")
VMEM_LIMIT = 58 << 20
MICRO = 1.15e9


def nn(a, b, precision=None):
    return lax.dot_general(
        a, b, (((1,), (0,)), ((), ())), preferred_element_type=F32, precision=precision
    )


def nt(a, b):
    return lax.dot_general(a, b, (((1,), (1,)), ((), ())), preferred_element_type=F32)


def tn(a, b):
    return lax.dot_general(a, b, (((0,), (0,)), ((), ())), preferred_element_type=F32)


def two(x):
    hi = x.astype(BF)
    lo = (x - hi.astype(F32)).astype(BF)
    return jnp.concatenate([hi, lo], axis=1)


def iota(shape, dim):
    return lax.broadcasted_iota(jnp.int32, shape, dim)


def column(row):
    return jnp.broadcast_to(row, (LANES, row.shape[1])).T[:, :1]


def as_row(col):
    return jnp.broadcast_to(col, (col.shape[0], LANES)).T[:1]


def sigmoid(x):
    return 1.0 / (1.0 + jnp.exp(-x))


def softplus(x):
    return jnp.maximum(x, 0.0) + jnp.log1p(jnp.exp(-jnp.abs(x)))


def full(shape):
    return pl.BlockSpec(shape, lambda i: (0,) * len(shape))


class Names:
    def __getattr__(self, name):
        return name


N = Names()


def launch(name, body, grid, ins, outs, scratch=(), micros=1, aliases=()):
    names = [item[0] for item in ins] + [item[0] for item in outs] + [item[0] for item in scratch]

    def kernel(*refs):
        body(types.SimpleNamespace(**dict(zip(names, refs))))

    results = pl.pallas_call(
        kernel,
        grid=grid,
        in_specs=[item[2] for item in ins],
        out_specs=[item[3] for item in outs],
        out_shape=[jax.ShapeDtypeStruct(item[1], item[2]) for item in outs],
        scratch_shapes=[item[1] for item in scratch],
        compiler_params=pltpu.CompilerParams(
            dimension_semantics=(N.arbitrary,) * len(grid), vmem_limit_bytes=VMEM_LIMIT
        ),
        input_output_aliases=dict(aliases),
        cost_estimate=pl.CostEstimate(
            flops=int(micros * MICRO), bytes_accessed=1, transcendentals=0
        ),
        name=name,
    )(*[item[1] for item in ins])
    return types.SimpleNamespace(**dict(zip([item[0] for item in outs], results)))


def small():
    return pl.BlockSpec(memory_space=pltpu.SMEM)


def rows_of(width, first=0):
    return pl.BlockSpec((BLOCK, width), lambda i: (first + i, 0))


def turned(width, last):
    return pl.BlockSpec((BLOCK, width), lambda i: (last - i, 0))


def place(orders, halves):
    mine, theirs = halves
    total = 2 * mine.shape[0]

    def body(r):
        at = pl.program_id(0) * BLOCK + iota((BLOCK, total // 2), 0)
        first = (r.mine_order[...] == at).astype(BF)
        second = (r.their_order[...] == at).astype(BF)
        r.out[...] = (nn(first, r.mine[...]) + nn(second, r.theirs[...])).astype(BF)

    return launch(
        N.place,
        body,
        (total // BLOCK,),
        [
            (N.mine_order, orders[0], full((1, total // 2))),
            (N.their_order, orders[1], full((1, total // 2))),
            (N.mine, mine, full((total // 2, D))),
            (N.theirs, theirs, full((total // 2, D))),
        ],
        [(N.out, (total, D), BF, rows_of(D))],
        micros=5.3,
    ).out


def prepare_in(spot, in_w, seq):
    depth = in_w.shape[2] // 2
    heads = HEADS // seq
    width = heads * HEADDIM
    wide = max(width, LANES)
    side = 2 * wide + LANES
    shape = (2 * side + PAIR, depth)

    def body(r):
        core = r.spot[0]
        for at in range(seq // 2):

            @pl.when(r.spot[3] == at)
            def _():
                for half, ref in ((core, r.keep), (1 - core, r.give)):
                    span = pl.ds(pl.multiple_of(half * depth, depth), depth)
                    edge = r.w[0, 2 * INNER + PAIR :, span].astype(F32)

                    def piece(start):
                        value = r.w[0, start : start + width, span]
                        if width < wide:
                            room = jnp.zeros((wide - width, depth), BF)
                            value = jnp.concatenate([value, room], axis=0)
                        return value

                    for index in range(2):
                        head = 2 * at + index
                        base = index * (side + PAIR)
                        ref[base : base + wide] = piece(width * head)
                        ref[base + wide : base + 2 * wide] = piece(INNER + width * head)
                        raw = edge[heads * head : heads * (head + 1)]
                        room = jnp.zeros((LANES - heads, depth), F32)
                        raw = jnp.concatenate([raw, room], axis=0).astype(BF)
                        ref[base + 2 * wide : base + side] = raw
                    ref[side : side + PAIR] = r.w[0, 2 * INNER : 2 * INNER + PAIR, span]

    return launch(
        N.prepare_in,
        body,
        (1,),
        [(N.spot, spot, small()), (N.w, in_w, full(in_w.shape))],
        [(N.keep, shape, BF, full(shape)), (N.give, shape, BF, full(shape))],
        micros=3,
    )


def prepare_rest(spot, out_w, ends):
    out_shape = (out_w.shape[1] // 2, D)
    end_shape = (2, ends.shape[3] // 2, D)

    def body(r):
        core = r.spot[0]
        for half, out, end in ((core, r.out_keep, r.end_keep), (1 - core, r.out_give, r.end_give)):
            size = out_shape[0]
            out[...] = r.out_w[0, pl.ds(pl.multiple_of(half * size, size), size)]
            size = end_shape[1]
            span = pl.ds(pl.multiple_of(half * size, size), size)
            for batch in range(2):
                end[batch] = r.ends[0, batch, 0, span]

    return launch(
        N.prepare_rest,
        body,
        (1,),
        [
            (N.spot, spot, small()),
            (N.out_w, out_w, full(out_w.shape)),
            (N.ends, ends, full(ends.shape)),
        ],
        [
            (N.out_keep, out_shape, BF, full(out_shape)),
            (N.out_give, out_shape, BF, full(out_shape)),
            (N.end_keep, end_shape, BF, full(end_shape)),
            (N.end_give, end_shape, BF, full(end_shape)),
        ],
        micros=3,
    )


def assemble(spot, mine, theirs, wide, by_distance):
    depth = mine[0].shape[-1]
    side = 2 * wide + LANES
    total = PAIR + side
    count = 4

    def body(r):
        w = r.spot[1]
        named = vars(r)

        def parts_of(name, arrays):
            found = []
            for index, array in enumerate(arrays):
                ref = named[name + str(index)]
                if array.ndim == 2:
                    found.append(ref)
                else:
                    found += [ref.at[k] for k in range(array.shape[0])]
            return found

        def move(source, start, base, pair):
            span = pl.ds(pl.multiple_of(start, depth), depth)
            r.out[:wide, span] = source[base : base + wide]
            r.out[wide : wide + PAIR, span] = source[pair : pair + PAIR]
            r.out[wide + PAIR :, span] = source[base + wide : base + side]

        for core in range(2):

            @pl.when(r.spot[0] == core)
            def _():
                own = core * (side + PAIR)
                shards = list(range(count))
                other = shards
                if by_distance:
                    shards = (w, w ^ (1 + core), w ^ (2 - core), w ^ 3)
                    other = (w, w ^ (2 - core), w ^ (1 + core), w ^ 3)
                for source, shard in zip(parts_of(N.mine, mine), shards):
                    move(source, (2 * shard + core) * depth, own, side)
                for source, shard in zip(parts_of(N.theirs, theirs), other):
                    move(source, (2 * shard + 1 - core) * depth, core * PAIR, (1 - core) * side)

    return launch(
        N.assemble,
        body,
        (1,),
        [(N.spot, spot, small())]
        + [(N.mine + str(k), value, full(value.shape)) for k, value in enumerate(mine)]
        + [(N.theirs + str(k), value, full(value.shape)) for k, value in enumerate(theirs)],
        [(N.out, (total, 2 * count * depth), BF, full((total, 2 * count * depth)))],
        micros=4.5,
    ).out


def block_terms(raw, dtb, rate_sign, offset):
    rate = softplus(raw + dtb)
    lower = (iota((BLOCK, BLOCK), 1) <= iota((BLOCK, BLOCK), 0)).astype(F32)
    level = nn(lower, rate * rate_sign, HIGH)
    local = iota((BLOCK, 1), 0)
    end = level[BLOCK - 1 :]
    end_offset = offset[BLOCK - 1 :]
    head = jnp.where(offset > local, jnp.exp(level), 0.0)
    fade = jnp.where(local >= BLOCK - 1 - end_offset, jnp.exp(end - level), 0.0)
    carry = jnp.where(end_offset > BLOCK - 1, jnp.exp(end), 0.0)
    return rate, level, head, fade, carry


def either(flag, first, second):
    chosen = flag.astype(F32)
    return chosen * first.astype(F32) + (1.0 - chosen) * second.astype(F32)


def keep_or_give(r, core, block, split, value):
    slot = pl.ds(pl.multiple_of(block % split * BLOCK, BLOCK), BLOCK)

    @pl.when(block // split == core)
    def _():
        r.keep[slot] = value

    @pl.when(block // split != core)
    def _():
        r.away[slot] = value


def forward_body(layer, begin, wide, split, r):
    heads = wide // HEADDIM
    conv = PAIR + wide
    step = pl.program_id(0)
    core = r.spot[0]

    @pl.when(step == 0)
    def _():
        if begin:
            r.state[...] = jnp.zeros_like(r.state)
            r.halo[...] = jnp.zeros_like(r.halo)
        else:
            r.state[...] = r.state_in[...]
            r.halo[...] = r.halo_in[...]

    tokens = r.tokens[...].astype(F32)
    if layer == 1:
        scale = lax.rsqrt(column(r.last_rows[0][0:1]) / INNER + EPS)
        summed = either(step // split == core, r.mine[...], r.theirs[...])
        low = (tokens + summed * scale).astype(BF)
        r.next[...] = low
        tokens = low.astype(F32)
    scale = lax.rsqrt(jnp.mean(tokens * tokens, axis=1, keepdims=True) + EPS)
    x = (tokens * scale * r.gain[...]).astype(BF)
    r.normed[...] = x
    projected = nt(x, r.w[...])
    gate = projected[:, :wide]
    r.gate[...] = gate
    cin_low = projected[:, wide : wide + conv].astype(BF)
    r.cin[...] = cin_low
    raw_low = projected[:, wide + conv :].astype(BF)
    r.raw[...] = raw_low
    pos = r.pos[...]
    label_col = pos[:, 0:1]
    offset = pos[:, 1:2]
    cin = cin_low.astype(F32)
    longer = jnp.concatenate([r.halo[...], cin], axis=0)
    r.halo[...] = cin[BLOCK - 8 :]
    taps = r.taps[...]
    pre = taps[KCONV : KCONV + 1] + taps[KCONV - 1 : KCONV] * cin
    for index in range(KCONV - 1):
        delay = KCONV - 1 - index
        moved = longer[8 - delay : 8 - delay + BLOCK]
        pre = pre + jnp.where(offset >= delay, taps[index : index + 1] * moved, 0.0)
    r.pre[...] = pre
    mixed_conv = (pre * sigmoid(pre)).astype(BF)
    write = mixed_conv[:, :STATE]
    read = mixed_conv[:, STATE:PAIR]
    xs = mixed_conv[:, PAIR:]
    xs_float = xs.astype(F32)
    terms = r.terms[...]
    rate, level, head, fade, carry = block_terms(
        raw_low.astype(F32), terms[0:1], terms[1:2], offset
    )
    level_rows = level.T
    rate_rows = rate.T
    spread = r.spread[...]
    state = r.state[...]
    r.states[0] = state
    wides = r.wides[...]
    mixed = nn(two(head), spread) * nn(read, state.astype(BF)) + wides[0:1] * xs_float
    gram = nt(read, write)
    inside = (label_col == r.label[0]) & (iota((BLOCK, BLOCK), 1) <= iota((BLOCK, BLOCK), 0))
    closed = jnp.where(inside, 0.0, NEG)
    parts = []
    for first in range(0, heads, 2):
        span = xs[:, first * HEADDIM : (first + 2) * HEADDIM]
        mixing = []
        values = []
        for h in range(first, first + 2):
            weight = jnp.exp(level[:, h : h + 1] - level_rows[h : h + 1] + closed)
            mixing.append((gram * (weight * rate_rows[h : h + 1])).astype(BF))
            own = iota(span.shape, 1) // HEADDIM == h - first
            values.append(jnp.where(own, span, jnp.zeros_like(span)))
        parts.append(nn(jnp.concatenate(mixing, axis=1), jnp.concatenate(values, axis=0)))
    mixed = mixed + jnp.concatenate(parts, axis=1)
    mixed_low = mixed.astype(BF)
    r.mixed[...] = mixed_low
    carry_wide = nn(two(jnp.broadcast_to(carry, (8, LANES))), spread)[:1]
    written = (nn(two(fade * rate), spread) * xs_float).astype(BF)
    r.state[...] = carry_wide * state + tn(write, written)
    gv = mixed_low.astype(F32) * (gate * sigmoid(gate))
    r.rows[0, 0:1] = as_row(jnp.sum(gv * gv, axis=1, keepdims=True))
    scaled = gv * wides[1:2]
    if layer == 1:
        dotted = nt(r.dout[...], r.w_out[...]) * scaled
        r.rows[0, 1:2] = as_row(jnp.sum(dotted, axis=1, keepdims=True))
    else:
        r.rows[0, 1:2] = jnp.zeros((1, BLOCK), F32)
    keep_or_give(r, core, step, split, nn(scaled.astype(BF), r.w_out[...]).astype(BF))


def forward(layer, part, spot, env, tokens, before, weights, vectors, carried, dout):
    w, w_out = weights
    wide = w_out.shape[0]
    conv = PAIR + wide
    count = tokens.shape[0] // BLOCK // 2
    split = count // 2
    first = part * count
    total = count * BLOCK
    row = pl.BlockSpec((1, 2, BLOCK), lambda i: (i, 0, 0))
    ins = [
        (N.spot, spot, small()),
        (N.tokens, tokens, rows_of(D, first)),
        (N.gain, vectors[N.gain], full((1, D))),
        (N.w, w, full(w.shape)),
        (N.w_out, w_out, full(w_out.shape)),
        (N.taps, vectors[N.taps], full((8, conv))),
        (N.terms, vectors[N.terms], full((8, LANES))),
        (N.wides, vectors[N.wides], full((8, wide))),
        (N.spread, env.spread, full(env.spread.shape)),
        (N.pos, env.pos, rows_of(3, first)),
        (N.label, env.label_row, pl.BlockSpec((1, 1, BLOCK), lambda i: (first + i, 0, 0))),
    ]
    outs = [
        (N.normed, (total, D), BF, rows_of(D)),
        (N.gate, (total, wide), F32, rows_of(wide)),
        (N.pre, (total, conv), F32, rows_of(conv)),
        (N.cin, (total, conv), BF, rows_of(conv)),
        (N.raw, (total, LANES), BF, rows_of(LANES)),
        (N.mixed, (total, wide), BF, rows_of(wide)),
        (N.states, (count, STATE, wide), F32, pl.BlockSpec((1, STATE, wide), lambda i: (i, 0, 0))),
        (N.rows, (count, 2, BLOCK), F32, row),
        (N.state, (STATE, wide), F32, full((STATE, wide))),
        (N.halo, (8, conv), F32, full((8, conv))),
    ]
    joint = layer * total // 2
    side = pl.BlockSpec((total // 2, D), lambda i: (part * layer, 0))
    outs += [
        (N.keep, (total // 2 + joint, D), BF, side),
        (N.away, (total // 2 + joint, D), BF, side),
    ]
    aliases = []
    if part == 1:
        ins += [
            (N.state_in, carried.state, full((STATE, wide))),
            (N.halo_in, carried.halo, full((8, conv))),
        ]
        if layer == 1:
            anywhere = pl.BlockSpec(memory_space=pl.ANY)
            aliases = [(len(ins), len(outs) - 2), (len(ins) + 1, len(outs) - 1)]
            ins += [(N.keep_in, carried.keep, anywhere), (N.away_in, carried.away, anywhere)]
    if layer == 1:
        block = pl.BlockSpec((BLOCK, D), lambda i: (i % split, 0))
        mine, theirs, last_rows = before
        ins += [
            (N.mine, mine, block),
            (N.theirs, theirs, block),
            (N.last_rows, last_rows, row),
            (N.dout, dout, rows_of(D, first)),
        ]
        outs.append((N.next, (total, D), BF, rows_of(D)))
    return launch(
        N.forward,
        functools.partial(forward_body, layer, part == 0, wide, split),
        (count,),
        ins,
        outs,
        micros=12.5,
        aliases=aliases,
    )


def ungate_body(layer, wide, count, split, r):
    step = pl.program_id(0)
    block = count - 1 - step
    core = r.spot[0]

    @pl.when(step == 0)
    def _():
        r.ggated[...] = jnp.zeros_like(r.ggated)

    scale = lax.rsqrt(column(r.rows[0][0:1]) / INNER + EPS)
    if layer == 1:
        dout = r.dout[...]
        dots = column(r.rows[0][1:2])
    else:
        flag = block // split == core
        grad = either(flag, r.grad_mine[...], r.grad_theirs[...])
        dtokens = unnorm(r.tokens[...].astype(F32), r.gain[...], grad)
        dout = (r.dlater[...].astype(F32) + dtokens).astype(BF)
        r.dout[...] = dout
        summed = either(flag, r.mine[...], r.theirs[...])
        dots = jnp.sum(dout.astype(F32) * summed, axis=1, keepdims=True)
    gate = r.gate[...]
    gain = r.wides[1:2]
    mixed = r.mixed[...].astype(F32)
    sig = sigmoid(gate)
    act = gate * sig
    normal = mixed * act * scale
    grad_out = nt(dout, r.w_out[...])
    shared = dots * scale / INNER
    grad_gv = scale * (grad_out * gain - normal * shared)
    r.dmixed[...] = (grad_gv * act).astype(BF)
    r.dgate[...] = (grad_gv * mixed * (sig * (1.0 + gate * (1.0 - sig)))).astype(BF)
    r.ggated[...] += jnp.sum(grad_out * normal, axis=0, keepdims=True)
    r.normed_out[...] = (normal * gain).astype(BF)


def unnorm(tokens, gain, grad):
    scale = lax.rsqrt(jnp.mean(tokens * tokens, axis=1, keepdims=True) + EPS)
    normal = tokens * scale
    inner = grad * gain
    return scale * (inner - normal * jnp.mean(inner * normal, axis=1, keepdims=True))


def ungate(layer, part, spot, kept, rows, w_out, vectors, above):
    total, wide = kept.mixed.shape
    count = total // BLOCK
    split = count // 2
    last = count - 1
    row = pl.BlockSpec((1, 2, BLOCK), lambda i: (last - i, 0, 0))
    ins = [
        (N.spot, spot, small()),
        (N.rows, rows, row),
        (N.gate, kept.gate, turned(wide, last)),
        (N.mixed, kept.mixed, turned(wide, last)),
        (N.wides, vectors[N.wides], full((8, wide))),
        (N.w_out, w_out, full((wide, D))),
    ]
    outs = [
        (N.dmixed, (total, wide), BF, turned(wide, last)),
        (N.dgate, (total, wide), BF, turned(wide, last)),
        (N.normed_out, (total, wide), BF, turned(wide, last)),
        (N.ggated, (1, wide), F32, full((1, wide))),
    ]
    if layer == 1:
        ins.append((N.dout, above.dout, turned(D, part * count + last)))
    else:
        block = pl.BlockSpec((BLOCK, D), lambda i: ((last - i) % split, 0))
        ins += [
            (N.grad_mine, above.grad[0], block),
            (N.grad_theirs, above.grad[1], block),
            (N.mine, above.summed[0], block),
            (N.theirs, above.summed[1], block),
            (N.tokens, above.tokens, turned(D, last)),
            (N.gain, above.gain, full((1, D))),
            (N.dlater, above.dout, turned(D, part * count + last)),
        ]
        outs.append((N.dout, (total, D), BF, turned(D, last)))
    return launch(
        N.ungate,
        functools.partial(ungate_body, layer, wide, count, split),
        (count,),
        ins,
        outs,
        micros=5.5,
    )


def backward_body(begin, wide, count, split, r):
    heads = wide // HEADDIM
    conv = PAIR + wide
    step = pl.program_id(0)
    block = count - 1 - step
    core = r.spot[0]

    @pl.when(step == 0)
    def _():
        if begin:
            r.dstate[...] = jnp.zeros_like(r.dstate)
            r.halo[...] = jnp.zeros_like(r.halo)
        else:
            r.dstate[...] = r.dstate_in[...]
            r.halo[...] = r.halo_in[...]
        r.gtaps[...] = jnp.zeros_like(r.gtaps)
        r.gheads[...] = jnp.zeros_like(r.gheads)
        r.gskip[...] = jnp.zeros_like(r.gskip)
        r.ggain[...] = jnp.zeros_like(r.ggain)

    pos = r.pos[...]
    label_col = pos[:, 0:1]
    offset = pos[:, 1:2]
    remain = pos[:, 2:3]
    pre = r.pre[...]
    sig = sigmoid(pre)
    mixed_conv = (pre * sig).astype(BF)
    write = mixed_conv[:, :STATE]
    read = mixed_conv[:, STATE:PAIR]
    xs = mixed_conv[:, PAIR:]
    xs_float = xs.astype(F32)
    raw = r.raw[...].astype(F32)
    terms = r.terms[...]
    dtb = terms[0:1]
    sign = terms[1:2]
    rate, level, head, fade, carry = block_terms(raw, dtb, sign, offset)
    tail = fade * rate
    level_rows = level.T
    spread = r.spread[...]
    fold = r.fold[...]
    dy = r.dmixed[...]
    dy_float = dy.astype(F32)
    state = r.states[0]
    state_low = state.astype(BF)
    dstate = r.dstate[...]
    dstate_low = dstate.astype(BF)
    dhead = nn(two(dy_float * nn(read, state_low)), fold)
    tail_wide = nn(two(tail), spread)
    scaled = (nn(two(head), spread) * dy_float).astype(BF)
    written = (tail_wide * xs_float).astype(BF)
    through = nn(write, dstate_low)
    dtail = nn(two(xs_float * through), fold)
    r.gskip[...] += jnp.sum(dy_float * xs_float, axis=0, keepdims=True)
    carry_wide = nn(two(jnp.broadcast_to(carry, (8, LANES))), spread)[:1]
    held = jnp.broadcast_to(jnp.sum(state * dstate, axis=0, keepdims=True), (8, wide))
    dcarry = nn(two(held), fold)[:1]

    gram = nt(write, read)
    inside = (label_col == r.label[0]) & (iota((BLOCK, BLOCK), 0) <= iota((BLOCK, BLOCK), 1))
    closed = jnp.where(inside, 0.0, NEG)
    lane = iota((1, LANES), 1)
    drate = jnp.zeros((BLOCK, LANES), F32)
    level_sums = []
    parts = []
    dgram = jnp.zeros((BLOCK, BLOCK), F32)
    for first in range(0, heads, 2):
        cut_at = slice(first * HEADDIM, (first + 2) * HEADDIM)
        xs_span = xs[:, cut_at]
        dy_span = dy[:, cut_at]
        mixing = []
        values = []
        for h in range(first, first + 2):
            own = iota(xs_span.shape, 1) // HEADDIM == h - first
            xs_own = jnp.where(own, xs_span, jnp.zeros_like(xs_span))
            values.append(jnp.where(own, dy_span, jnp.zeros_like(dy_span)))
            decay = jnp.exp(level_rows[h : h + 1] - level[:, h : h + 1] + closed)
            rate_col = rate[:, h : h + 1]
            weight = decay * rate_col
            mixing.append((gram * weight).astype(BF))
            dmix = nt(xs_own, dy_span)
            dgram = dgram + dmix * weight
            bare = dmix * gram * decay
            drate = drate + jnp.sum(bare, axis=1, keepdims=True) * (lane == h).astype(F32)
            level_sums.append(jnp.sum(bare * rate_col, axis=0, keepdims=True))
        parts.append(nn(jnp.concatenate(mixing, axis=1), jnp.concatenate(values, axis=0)))
    dxs = jnp.concatenate(parts, axis=1) + r.wides[0:1] * dy_float + tail_wide * through
    dgram_low = dgram.astype(BF)
    dread = tn(dgram_low, write) + nt(scaled, state_low)
    dwrite = nn(dgram_low, read) + nt(written, dstate_low)
    r.dstate[...] = carry_wide * dstate + tn(read, scaled)

    level_sums.append(jnp.zeros((LANES - heads, BLOCK), F32))
    tail_flow = dtail * tail
    local = iota((BLOCK, 1), 0)
    last = jnp.sum(tail_flow, axis=0, keepdims=True) + dcarry * carry
    dlevel = jnp.concatenate(level_sums, axis=0).T - rate * drate + dhead * head - tail_flow
    dlevel = dlevel + jnp.where(local == BLOCK - 1, last, 0.0)
    upper = (iota((BLOCK, BLOCK), 0) <= iota((BLOCK, BLOCK), 1)).astype(F32)
    dsum = nn(upper, dlevel, HIGH)
    drate = drate + dtail * fade + sign * dsum
    draw = drate * sigmoid(raw + dtb)
    r.gheads[0:1] += jnp.sum(draw, axis=0, keepdims=True)
    r.gheads[1:2] += jnp.sum(rate * dsum, axis=0, keepdims=True) * sign

    dpre = jnp.concatenate([dwrite, dread, dxs], axis=1) * (sig * (1.0 + pre * (1.0 - sig)))
    longer = jnp.concatenate([dpre, r.halo[...]], axis=0)
    r.halo[...] = dpre[:8]
    cin = r.cin[...].astype(F32)
    taps = r.taps[...]
    r.gtaps[KCONV : KCONV + 1] += jnp.sum(dpre, axis=0, keepdims=True)
    r.gtaps[KCONV - 1 : KCONV] += jnp.sum(dpre * cin, axis=0, keepdims=True)
    dcin = taps[KCONV - 1 : KCONV] * dpre
    for index in range(KCONV - 1):
        delay = KCONV - 1 - index
        moved = jnp.where(remain >= delay, longer[delay : delay + BLOCK], 0.0)
        dcin = dcin + taps[index : index + 1] * moved
        r.gtaps[index : index + 1] += jnp.sum(moved * cin, axis=0, keepdims=True)
    rest = jnp.concatenate([dcin, draw], axis=1).astype(BF)
    r.rest[...] = rest
    w = r.w[...]
    dnormed = nn(r.dgate[...], w[:wide]) + nn(rest, w[wide:])
    r.ggain[...] += jnp.sum(dnormed * r.normed[...].astype(F32), axis=0, keepdims=True)
    keep_or_give(r, core, block, split, dnormed.astype(BF))


def backward(part, spot, env, kept, grads, w, vectors, carried):
    total, wide = kept.mixed.shape
    conv = PAIR + wide
    count = total // BLOCK
    split = count // 2
    last = count - 1
    top = part * count + last
    ins = [
        (N.spot, spot, small()),
        (N.w, w, full(w.shape)),
        (N.taps, vectors[N.taps], full((8, conv))),
        (N.terms, vectors[N.terms], full((8, LANES))),
        (N.wides, vectors[N.wides], full((8, wide))),
        (N.spread, env.spread, full(env.spread.shape)),
        (N.fold, env.fold, full(env.fold.shape)),
        (N.pos, env.pos, turned(3, top)),
        (N.label, env.label_row, pl.BlockSpec((1, 1, BLOCK), lambda i: (top - i, 0, 0))),
        (N.pre, kept.pre, turned(conv, last)),
        (N.cin, kept.cin, turned(conv, last)),
        (N.raw, kept.raw, turned(LANES, last)),
        (N.states, kept.states, pl.BlockSpec((1, STATE, wide), lambda i: (last - i, 0, 0))),
        (N.normed, kept.normed, turned(D, last)),
        (N.dmixed, grads.dmixed, turned(wide, last)),
        (N.dgate, grads.dgate, turned(wide, last)),
    ]
    if part == 0:
        ins += [
            (N.dstate_in, carried.dstate, full((STATE, wide))),
            (N.halo_in, carried.halo, full((8, conv))),
        ]
    outs = [
        (N.keep, (total // 2, D), BF, full((total // 2, D))),
        (N.away, (total // 2, D), BF, full((total // 2, D))),
        (N.rest, (total, conv + LANES), BF, turned(conv + LANES, last)),
        (N.gtaps, (8, conv), F32, full((8, conv))),
        (N.gheads, (8, LANES), F32, full((8, LANES))),
        (N.gskip, (1, wide), F32, full((1, wide))),
        (N.ggain, (1, D), F32, full((1, D))),
        (N.dstate, (STATE, wide), F32, full((STATE, wide))),
        (N.halo, (8, conv), F32, full((8, conv))),
    ]
    return launch(
        N.backward,
        functools.partial(backward_body, part == 1, wide, count, split),
        (count,),
        ins,
        outs,
        micros=14.5,
    )


def weight_grads(spot, lefts, rights, seq, outer=None, size=0):
    depth = lefts[0].shape[1]
    spans = []
    wide = 0
    for pair in rights:
        spans.append((wide, pair[0].shape[1]))
        wide += pair[0].shape[1]
    share = depth // (4 * seq)
    rows = depth // 4
    room = 0 if outer is None else outer[0][0].shape[1]

    def body(r):
        w = r.spot[1]
        z = r.spot[2]
        named = vars(r)
        sides = ((r.keep, (0, r.spot[5])), (r.away, (r.spot[4], 3)))
        for index, (base, width) in enumerate(spans):
            right = [named[N.right + str(index) + str(part)] for part in range(2)]
            r.total[:, base : base + width] = tn(r.left0[...], right[0][...]) + tn(
                r.left1[...], right[1][...]
            )
        for ref, shards in sides:
            for index, shard in enumerate(shards):
                for turn in range(seq):
                    start = ((z ^ turn) * 4 + (w ^ shard)) * share
                    piece = r.total[pl.ds(pl.multiple_of(start, share), share)]
                    ref[index, turn * share : (turn + 1) * share, :wide] = piece.astype(BF)
        if outer is None:
            return
        for part in range(D // room):
            cols = slice(part * room, (part + 1) * room)
            r.outer[...] = tn(r.out0[...], r.dout0[...][:, cols]) + tn(
                r.out1[...], r.dout1[...][:, cols]
            )
            for ref, shards in sides:
                for index, shard in enumerate(shards):
                    start = pl.multiple_of((w ^ shard) * size, size)
                    ref[index, part * size : (part + 1) * size, wide:] = r.outer[
                        pl.ds(start, size)
                    ].astype(BF)
        if size * (D // room) < rows:
            for ref, _ in sides:
                ref[:, size * (D // room) :, wide:] = jnp.zeros(
                    (2, rows - size * (D // room), room), BF
                )

    ins = [(N.spot, spot, small())]
    for index in range(2):
        ins.append((N.left + str(index), lefts[index], full(lefts[index].shape)))
    for index, pair in enumerate(rights):
        for part in range(2):
            ins.append((N.right + str(index) + str(part), pair[part], full(pair[part].shape)))
    scratch = [(N.total, pltpu.VMEM((depth, wide), F32))]
    if outer is not None:
        outs, douts = outer
        height = outs[0].shape[0]
        for index in range(2):
            ins.append((N.out + str(index), outs[index], full(outs[index].shape)))
            array, at = douts[index]
            spec = pl.BlockSpec((height, D), functools.partial(lambda at, i: (at, 0), at))
            ins.append((N.dout + str(index), array, spec))
        scratch.append((N.outer, pltpu.VMEM((room, room), F32)))
    shape = (2, rows, wide + room)
    return launch(
        N.weight_grads,
        body,
        (1,),
        ins,
        [(N.keep, shape, BF, full(shape)), (N.away, shape, BF, full(shape))],
        scratch=scratch,
        micros=6 if len(rights) == 1 else 11,
    )


def finish(kind, part, spot, orders, values, before):
    count = values.count
    split = count // 2
    total = count * BLOCK

    def body(r):
        step = pl.program_id(0)
        core = r.spot[0]

        @pl.when(step == 0)
        def _():
            if before is None:
                r.own[...] = jnp.zeros_like(r.own)
                r.across[...] = jnp.zeros_like(r.across)
            else:
                r.own[...] = r.own_in[...]
                r.across[...] = r.across_in[...]

        summed = either(step // split == core, r.mine[...], r.theirs[...])
        if kind == N.grad:
            dtokens = unnorm(r.tokens[...].astype(F32), r.gain[...], summed)
            value = r.rest[...].astype(F32) + dtokens
        else:
            scale = lax.rsqrt(column(r.rows[0][0:1]) / INNER + EPS)
            value = r.rest[...].astype(F32) + summed * scale
        low = value.astype(BF)
        at = (part * count + step) * BLOCK + iota((BLOCK, BLOCK), 1)
        r.own[...] += nn((r.own_order[...] == at).astype(BF), low).astype(BF)
        r.across[...] += nn((r.far_order[...] == at).astype(BF), low).astype(BF)

    block = pl.BlockSpec((BLOCK, D), lambda i: (values.first + i % split, 0))
    ins = [
        (N.spot, spot, small()),
        (N.own_order, orders[0], full((BLOCK, 1))),
        (N.far_order, orders[1], full((BLOCK, 1))),
        (N.mine, values.summed[0], block),
        (N.theirs, values.summed[1], block),
        (N.rest, values.rest, rows_of(D)),
    ]
    outs = [
        (N.own, (BLOCK, D), BF, full((BLOCK, D))),
        (N.across, (BLOCK, D), BF, full((BLOCK, D))),
    ]
    if kind == N.grad:
        ins += [
            (N.tokens, values.tokens, rows_of(D, part * count)),
            (N.gain, values.gain, full((1, D))),
        ]
    else:
        ins.append((N.rows, values.rows, pl.BlockSpec((1, 2, BLOCK), lambda i: (i, 0, 0))))
    if before is not None:
        ins += [
            (N.own_in, before.own, full((BLOCK, D))),
            (N.across_in, before.across, full((BLOCK, D))),
        ]
    return launch(
        N.finish, body, (count,), ins, outs, micros=5,
    )


def settle(spot, ends):
    rows = ends[0].shape[0]

    def body(r):
        core = r.spot[0]
        batch = r.spot[7]
        for layer, own, far in ((0, r.own0, r.far0), (1, r.own1, r.far1)):
            for at in range(2):

                @pl.when((core == layer) & (batch == at))
                def _():
                    r.out[0, at, 0] = own[...].astype(F32)
                    r.out[0, 1 - at, 0] = far[...].astype(F32)

    names = (N.own0, N.far0, N.own1, N.far1)
    shape = (1, 2, 1, rows, D)
    return launch(
        N.settle,
        body,
        (1,),
        [(N.spot, spot, small())]
        + [(name, value, full(value.shape)) for name, value in zip(names, ends)],
        [(N.out, shape, F32, full(shape))],
        micros=2,
    ).out


def gather_columns(spot, sides, seq):
    half = seq // 2
    heads = HEADS // seq
    width = heads * HEADDIM
    wide = max(width, LANES)
    share = sides[0][0].shape[1]
    shape = (1, share, 2 * INNER + PAIR + HEADS)

    def body(r):
        named = vars(r)
        for layer in range(2):

            @pl.when(r.spot[0] == layer)
            def _():
                raws = []
                pair = jnp.zeros((share, PAIR), F32)
                for place_at in range(half):
                    for side in range(2):
                        rank = 2 * place_at + side
                        part = named[N.side + str(layer) + str(side)][place_at].astype(F32)
                        r.out[0, :, width * rank : width * (rank + 1)] = part[:, :width]
                        start = wide + PAIR
                        r.out[0, :, INNER + width * rank : INNER + width * (rank + 1)] = part[
                            :, start : start + width
                        ]
                        pair = pair + part[:, wide : wide + PAIR]
                        raws.append(part[:, start + wide : start + wide + heads])
                r.out[0, :, 2 * INNER : 2 * INNER + PAIR] = pair
                r.out[0, :, 2 * INNER + PAIR :] = jnp.concatenate(raws, axis=1)

    ins = [(N.spot, spot, small())]
    for layer in range(2):
        for side in range(2):
            value = sides[layer][side]
            ins.append((N.side + str(layer) + str(side), value, full(value.shape)))
    return launch(
        N.gather_columns, body, (1,), ins, [(N.out, shape, F32, full(shape))], micros=2
    ).out


def pack(spot, fold, gains, scans, gated, seq):
    heads = HEADS // seq
    width = heads * HEADDIM
    wide = max(width, LANES)
    conv = PAIR + wide
    shape = (KCONV + 3, INNER + PAIR)
    ins = [(N.spot, spot, small()), (N.fold, fold, full(fold.shape))]
    for layer in range(2):
        ins.append((N.gain + str(layer), gains[layer], full((1, D))))
        for part in range(2):
            scan = scans[layer][part]
            for name, value in (
                (N.gtaps, scan.gtaps),
                (N.gheads, scan.gheads),
                (N.gskip, scan.gskip),
                (N.ggain, scan.ggain),
                (N.ggated, gated[layer][part].ggated),
            ):
                ins.append((name + str(layer) + str(part), value, full(value.shape)))

    def body(r):
        named = vars(r)

        def both(name, layer):
            return named[name + str(layer) + "0"][...] + named[name + str(layer) + "1"][...]

        for layer in range(2):
            taps = both(N.gtaps, layer)
            by_head = both(N.gheads, layer)
            skips = jnp.broadcast_to(both(N.gskip, layer), (8, wide))
            skips = nn(two(skips), r.fold[...])[:1]
            gated_row = both(N.ggated, layer)
            gain_row = both(N.ggain, layer) / named[N.gain + str(layer)][...]

            def fill(ref):
                ref[...] = jnp.zeros(shape, F32)
                ref[: KCONV + 1, INNER:] = taps[: KCONV + 1, :PAIR]
                ref[KCONV + 2 :, :D] = gain_row
                for rank in range(seq):

                    @pl.when(r.spot[6] == rank)
                    def _():
                        cols = slice(rank * width, (rank + 1) * width)
                        ref[: KCONV + 1, cols] = taps[: KCONV + 1, PAIR : PAIR + width]
                        ref[KCONV + 1 : KCONV + 2, cols] = gated_row[:, :width]
                        row = []
                        for value in (by_head[0:1], by_head[1:2], skips):
                            if rank:
                                row.append(jnp.zeros((1, rank * heads), F32))
                            row.append(value[:, :heads])
                            if rank < seq - 1:
                                row.append(jnp.zeros((1, HEADS - (rank + 1) * heads), F32))
                        row.append(jnp.zeros((1, PAIR - 3 * HEADS), F32))
                        ref[KCONV + 1 : KCONV + 2, INNER:] = jnp.concatenate(row, axis=1)

            @pl.when(r.spot[0] == layer)
            def _():
                fill(r.mine)

            @pl.when(r.spot[0] != layer)
            def _():
                fill(r.give)

    return launch(
        N.pack,
        body,
        (1,),
        ins,
        [(N.mine, shape, F32, full(shape)), (N.give, shape, F32, full(shape))],
        micros=2,
    )


class Plan:
    def __init__(self):
        self.seq = lax.axis_size(N.seq)
        self.shards = lax.axis_size(N.wshard)
        self.half = self.seq // 2
        self.core = lax.axis_index(N.section)
        self.z = lax.axis_index(N.seq)
        self.w = lax.axis_index(N.wshard)
        self.batch = self.z // self.half
        self.place = self.z % self.half
        self.rank = 2 * self.place + self.core

    def send(self, value, route, cores=(0, 1)):
        pairs = []
        for c in range(2):
            for z in range(self.seq):
                for w in range(self.shards):
                    target = route(c, z, w)
                    if c in cores and target is not None:
                        source = (c * self.seq + z) * self.shards + w
                        tc, tz, tw = target
                        pairs.append((source, (tc * self.seq + tz) * self.shards + tw))
        return lax.ppermute(value, AXES, pairs)

    def swap(self, value, cores=(0, 1)):
        return self.send(value, lambda c, z, w: (1 - c, z, w), cores)

    def along(self, value, k, cores=(0, 1)):
        return self.send(value, lambda c, z, w: (c, z ^ k, w), cores)

    def first_side(self, value):
        return self.send(value, lambda c, z, w: (c, z, w ^ (1 + c)))

    def second_side(self, value):
        return self.send(value, lambda c, z, w: (c, z, w ^ (2 - c)))

    def own(self, first, second):
        return jnp.where(self.core == 0, first, second)

    def reach(self, near, far):
        pieces = [self.along(near, k) for k in range(1, self.half)]
        return near, pieces, self.along(far, self.half)

    def collect(self, reached, mark, late):
        near, pieces, came = reached
        came = after(came, mark)
        more = [self.along(came, k) for k in range(1, self.half)]
        mine = jnp.concatenate([near] + pieces + [came] + [after(piece, late) for piece in more], axis=0)
        return mine, self.swap(mine)

    def fold(self, terms):
        return add(terms.keep, self.swap(terms.away))

    def reduce(self, total, *marks):
        hop = 1
        while hop < self.half:
            total = add(total, after(self.along(total, hop), *marks))
            hop *= 2
        return total, self.swap(total)

    def chip_total(self, value):
        return value + self.swap(value)

    def total(self, value, *marks):
        hop = 1
        while hop < self.half:
            value = value + after(self.along(value, hop), *marks)
            hop *= 2
        return value

    def home(self, value, batch, layer):
        half = self.half

        def route(c, z, w):
            if z // half != batch:
                return None
            return (layer, 2 * (z % half) + c, w)

        return self.send(value, route)

    def gather_chips(self, value, share):
        pieces = [value[:share]]
        for k in range(1, self.seq):
            pieces.append(self.along(value[k * share : (k + 1) * share], k))
        half = self.half
        terms = [add(pieces[k], pieces[k + half]) for k in range(half)]
        if half == 2:
            even = self.place == 0
            ordered = [jnp.where(even, terms[0], terms[1]), jnp.where(even, terms[1], terms[0])]
            return jnp.stack(ordered)
        stacked = jnp.stack(terms)
        return stacked[self.place ^ jnp.arange(half)]


def add(first, second):
    return (first.astype(F32) + second.astype(F32)).astype(BF)


def after(value, *others):
    return lax.optimization_barrier((value,) + others)[0]


def pick(value, index, axis=0):
    return lax.dynamic_index_in_dim(value, index, axis, keepdims=False)


def cut(value, start, size, axis):
    return lax.dynamic_slice_in_dim(value, start, size, axis)


def on_device(
    ends_in,
    seq_lengths,
    deal_order,
    norm_w,
    in_w,
    conv_w,
    conv_b,
    dt_bias,
    a_log,
    d_skip,
    gnorm_w,
    out_w,
):
    plan = Plan()
    core = plan.core
    half = plan.half
    rank = plan.rank
    seq = plan.seq
    rows = ends_in.shape[3]
    total = rows * seq
    count = total // BLOCK
    heads = HEADS // seq
    width = heads * HEADDIM
    wide = max(width, LANES)
    side = 2 * wide + LANES
    first = 1 + core
    second = 2 - core
    spot = jnp.stack([core, plan.w, plan.z, plan.place, first, second, rank, plan.batch])
    spot = spot.astype(jnp.int32)

    def padded(value, size):
        return jnp.pad(value, ((0, 0), (0, size - value.shape[1])))

    held = prepare_in(spot, jnp.swapaxes(in_w, 1, 2), seq)
    came = plan.swap(held.give)
    chunk_parts = [plan.own(held.keep, came), plan.own(came, held.keep)]
    held = prepare_rest(after(spot, held.give), out_w, ends_in)
    came = plan.swap(held.end_give)
    end_parts = [plan.own(held.end_keep, came), plan.own(came, held.end_keep)]
    came = plan.swap(held.out_give)
    out_parts = [plan.own(held.out_keep, came), plan.own(came, held.out_keep)]
    half_rows = rows // 2

    order = pick(deal_order[:, 0], plan.batch)
    by_chip = order.reshape(seq, 2, half_rows)[plan.z ^ jnp.arange(seq)]
    orders = (
        pick(by_chip, core, 1).reshape(1, total // 2),
        pick(by_chip, 1 - core, 1).reshape(1, total // 2),
    )
    end_orders = (
        cut(order, rows * plan.z, rows, 0).reshape(rows, 1),
        cut(order, rows * (plan.z ^ half), rows, 0).reshape(rows, 1),
    )

    def give(value):
        return plan.swap(cut(value, (1 - core) * side, side + PAIR, value.ndim - 2))

    def in_weights(part):
        near = plan.first_side(part)
        beyond = plan.second_side(part)
        far = plan.second_side(near)
        theirs = (give(jnp.stack([part, near, beyond])), give(far))
        return assemble(spot, (part, near, beyond, far), theirs, wide, True), near, far

    def later_in_weights(part):
        every = lax.all_gather(part, N.wshard)
        return assemble(spot, (every,), (give(every),), wide, False)

    def chosen_rows(every):
        half_part = every.shape[1]
        if half == 2:
            mine = pick(every, rank)
            theirs = plan.swap(pick(every, rank ^ 1))
            return jnp.concatenate([plan.own(mine, theirs), plan.own(theirs, mine)], axis=0)
        other = plan.swap(every)
        whole = jnp.stack([plan.own(every, other), plan.own(other, every)], axis=1)
        whole = whole.reshape(8 * half_part, D)
        return jnp.pad(cut(whole, width * rank, width, 0), ((0, wide - width), (0, 0)))

    def out_weights(part):
        if half == 2:
            low_shard = plan.w // 2

            def route(c, z, w):
                return (c, z, w ^ 2) if w // 2 == z % half else None

            came = plan.send(part, route)
            here = jnp.where(low_shard == plan.place, part, came)
            beside = plan.send(here, lambda c, z, w: (c, z, w ^ 1))
            same = plan.w % 2 == core
            mine = jnp.where(same, here, beside)
            theirs = plan.swap(jnp.where(same, beside, here))
            return jnp.concatenate([plan.own(mine, theirs), plan.own(theirs, mine)], axis=0)
        return chosen_rows(lax.all_gather(part, N.wshard))

    def reach(part):
        return plan.reach(pick(part, plan.batch), pick(part, 1 - plan.batch))

    w_first, in_near, in_far = in_weights(chunk_parts[0])
    started = plan.collect(reach(end_parts[0]), in_far, in_far)
    w_out_first = out_weights(after(out_parts[0], in_near))
    w_second = later_in_weights(after(chunk_parts[1], in_far))
    w_out_second = out_weights(after(out_parts[1], w_out_first))
    weights = [(w_first, w_out_first), (w_second, w_out_second)]

    tokens = place(orders, started)

    lengths = pick(seq_lengths[:, 0], plan.batch)
    ends = jnp.cumsum(lengths)
    at = iota((total,), 0)
    passed = at[:, None] >= ends[None, :]
    label = jnp.sum(passed.astype(jnp.int32), axis=1)
    begin = jnp.max(jnp.where(passed, ends[None, :], 0), axis=1)
    finished = jnp.min(jnp.where(passed, total, ends[None, :]), axis=1)
    channel_head = iota((LANES, wide), 1) // HEADDIM
    hot = (channel_head == iota((LANES, wide), 0)).astype(BF)
    env = types.SimpleNamespace(
        pos=jnp.stack([label, at - begin, finished - 1 - at], axis=1),
        label_row=label.reshape(count, 1, BLOCK),
        spread=jnp.concatenate([hot, hot], axis=0),
        fold=jnp.concatenate([hot.T, hot.T], axis=0),
    )

    own_small = jnp.concatenate(
        [
            norm_w[0],
            conv_w[0].reshape(-1),
            conv_b[0],
            dt_bias[0],
            a_log[0],
            d_skip[0],
            gnorm_w[0],
        ]
    )
    other_small = plan.swap(own_small)
    sizes = (D, (KCONV + 1) * (INNER + PAIR), HEADS, HEADS, HEADS, INNER)

    def pieces_of(flat):
        pieces = []
        begin = 0
        for size in sizes:
            pieces.append(flat[begin : begin + size])
            begin += size
        return pieces

    def vectors_of(layer):
        flat = jnp.where(core == layer, own_small, other_small)
        gain, taps, dtb, log_rate, skip, gated = pieces_of(flat)
        taps = taps.reshape(KCONV + 1, INNER + PAIR)
        channels = jnp.concatenate(
            [taps[:, INNER:], padded(cut(taps, rank * width, width, 1), wide)], axis=1
        )

        def lanes(value):
            return padded(cut(value, rank * heads, heads, 0)[None], LANES)

        terms = jnp.concatenate([lanes(dtb), lanes(-jnp.exp(log_rate))], axis=0)
        skips = jnp.repeat(cut(skip, rank * heads, heads, 0), HEADDIM)[None]
        wides = jnp.concatenate([skips, cut(gated, rank * width, width, 0)[None]], axis=0)
        return {
            N.gain: gain[None],
            N.taps: jnp.pad(channels, ((0, 8 - KCONV - 1), (0, 0))),
            N.terms: jnp.pad(terms, ((0, 6), (0, 0))),
            N.wides: jnp.pad(wides, ((0, 6), (0, wide - width))),
        }

    vectors = [vectors_of(0), vectors_of(1)]

    kept = [[], []]
    rows_summed = [[], []]
    summed = [[], []]
    def pass_on(layer, part, turn, before, dout):
        carried = kept[layer][0] if part == 1 else None
        done = forward(
            layer, part, turn, env, tokens, before, weights[layer], vectors[layer], carried, dout
        )
        kept[layer].append(done)
        return done

    reached = reach(after(end_parts[1], *started))
    done = pass_on(0, 0, spot, None, None)
    mark = done.rows
    rows_low = plan.chip_total(done.rows)
    folded = plan.fold(done)
    done = pass_on(0, 1, after(spot, folded, rows_low), None, None)
    rows_summed[0].append(plan.total(rows_low, done.rows))
    summed[0].append(plan.reduce(folded, done.rows))
    cotangent = place(orders, plan.collect(reached, mark, done.rows))
    folded = plan.fold(done)
    rows_summed[0].append(plan.total(plan.chip_total(done.rows)))
    turn = after(spot, folded, rows_summed[0][1])
    done = pass_on(1, 0, turn, summed[0][0] + (rows_summed[0][0],), cotangent)
    summed[0].append(plan.reduce(folded, done.rows))
    rows_low = plan.chip_total(done.rows)
    turn = after(spot, rows_low)
    done = pass_on(1, 1, turn, summed[0][1] + (rows_summed[0][1],), cotangent)
    rows_summed[1].append(plan.total(rows_low, done.rows))
    rows_summed[1].append(plan.total(plan.chip_total(done.rows)))
    last_fold = after(plan.fold(done), *rows_summed[1])

    grads_summed = [[None, None], [None, None]]
    gated = [[None, None], [None, None]]
    scans = [[None, None], [None, None]]
    grad_parts = [[None, None], [None, None]]

    def ungate_part(layer, part, turn):
        above = types.SimpleNamespace(dout=cotangent)
        if layer == 0:
            above.grad = grads_summed[1][part]
            above.summed = summed[0][part]
            above.tokens = kept[1][part].next
            above.gain = vectors[1][N.gain]
        gated[layer][part] = ungate(
            layer,
            part,
            turn,
            kept[layer][part],
            rows_summed[layer][part],
            weights[layer][1],
            vectors[layer],
            above,
        )

    def scan_part(layer, part, turn):
        carried = scans[layer][1] if part == 0 else None
        scan = backward(
            part, turn, env, kept[layer][part], gated[layer][part], weights[layer][0], vectors[layer], carried
        )
        scans[layer][part] = scan
        return plan.fold(scan)

    def outer_of(layer):
        douts = [(cotangent, 0), (cotangent, 1)]
        if layer == 0:
            douts = [(item.dout, 0) for item in gated[0]]
        return [item.normed_out for item in gated[layer]], douts

    def normed_of(layer):
        return [item.normed for item in kept[layer]]

    def gates_of(layer):
        return [item.dgate for item in gated[layer]]

    def rests_of(layer):
        return [item.rest for item in scans[layer]]

    def first_hop(terms):
        return plan.first_side(terms.away)

    def first_add(terms, came):
        return add(terms.keep[0], came[0]), add(terms.keep[1], came[1])

    def finish_part(kind, part, turn, before):
        if kind == N.result:
            values = types.SimpleNamespace(
                summed=last_sums,
                rest=kept[1][part].next,
                rows=rows_summed[1][part],
                first=part * (count // 4),
            )
        else:
            values = types.SimpleNamespace(
                summed=grads_summed[0][part],
                rest=gated[0][part].dout,
                tokens=tokens,
                gain=vectors[0][N.gain],
                first=0,
            )
        values.count = count // 2
        return finish(kind, part, turn, end_orders, values, before)

    share = D // (4 * seq)
    gate_span = wide
    rest_span = side + PAIR - wide
    def homed(outs, layer, *marks):
        return add(
            after(plan.home(outs, 0, layer), *marks), after(plan.home(outs, 1, layer), *marks)
        )

    ungate_part(1, 0, spot)
    ungate_part(1, 1, spot)
    folded = scan_part(1, 1, spot)
    last_sums = plan.reduce(last_fold, scans[1][1].gskip)
    upper = folded
    folded = scan_part(1, 0, after(spot, folded, *last_sums))
    mark = scans[1][0].gskip
    grads_summed[1][1] = plan.reduce(upper, mark)
    result = finish_part(N.result, 0, after(spot, mark), None)
    result = finish_part(N.result, 1, spot, result)
    terms = weight_grads(
        after(spot, result.own, folded),
        normed_of(1),
        (gates_of(1), rests_of(1)),
        seq,
        outer_of(1),
        width // 4,
    )
    came = first_hop(terms)
    grads_summed[1][0] = plan.reduce(folded, terms.away)
    ungate_part(0, 1, after(spot, terms.away))
    result_far = plan.along(result.across, half, (1,))
    folded = scan_part(0, 1, after(spot, gated[0][1].ggated, *grads_summed[1][0]))
    pair = first_add(terms, after(came, scans[0][1].gskip))
    given = plan.second_side(pair[1])
    ungate_part(0, 0, after(spot, folded, pair[1]))
    gate_terms = weight_grads(
        after(spot, gated[0][0].ggated), normed_of(0), (gates_of(0),), seq, outer_of(0), width // 4
    )
    gate_came = first_hop(gate_terms)
    grads_summed[0][1] = plan.reduce(folded, gate_terms.away)
    later_last = add(pair[0], after(given, gate_terms.away))
    start_grad = finish_part(N.grad, 1, after(spot, later_last), None)
    folded = scan_part(0, 0, after(spot, start_grad.own, result_far))
    mark = scans[0][0].gskip
    chips_later = plan.gather_chips(later_last[:, : gate_span + rest_span], share)
    came_later = plan.swap(chips_later, (0,))
    outs_later = homed(later_last[:, gate_span + rest_span :], 1)
    rest_terms = weight_grads(
        after(spot, mark, chips_later, outs_later, folded), normed_of(0), (rests_of(0),), seq
    )
    rest_came = first_hop(rest_terms)
    grads_summed[0][0] = plan.reduce(folded, rest_terms.away)
    gate_pair = first_add(gate_terms, after(gate_came, mark))
    gate_given = plan.second_side(gate_pair[1])
    rest_pair = first_add(rest_terms, rest_came)
    rest_given = plan.second_side(rest_pair[1])
    gate_last = add(gate_pair[0], after(gate_given, rest_terms.away))
    start_grad = finish_part(N.grad, 0, after(spot, rest_pair[1]), start_grad)
    rest_last = add(rest_pair[0], rest_given)
    joined = jnp.concatenate([gate_last[:, :gate_span], rest_last], axis=1)
    chips_first = plan.gather_chips(joined, share)
    weight_sums = [
        (homed(gate_last[:, gate_span:], 0, rest_last), chips_first, plan.swap(chips_first, (1,))),
        (outs_later, chips_later, came_later),
    ]

    grad_far = plan.along(start_grad.across, half, (0,))
    ends_out = settle(spot, (start_grad.own, grad_far, result.own, result_far))

    both_sides = []
    out_grads = []
    for layer in range(2):
        outs, chips, came = weight_sums[layer]
        size = width // 4
        pieces = [outs[k * size : (k + 1) * size] for k in range(D // wide)]
        out_grads.append(jnp.concatenate(pieces, axis=1).astype(F32))
        both_sides.append((chips, came) if layer == 0 else (came, chips))
    g_in = gather_columns(spot, both_sides, seq)
    g_out = plan.own(out_grads[0], out_grads[1])

    packed = pack(after(spot, folded), env.fold, [item[N.gain] for item in vectors], scans, gated, seq)
    sums = packed.mine + plan.swap(packed.give)
    sums = sums + after(plan.first_side(after(sums, rest_terms.away)), rest_pair[1])
    sums = sums + plan.second_side(after(sums, rest_last))
    hop = 1
    while hop < seq:
        sums = sums + after(plan.along(sums, hop), grad_far)
        hop *= 2
    heads_at = INNER + HEADS
    return (
        ends_out,
        sums[KCONV + 2 :, :D],
        g_in,
        sums[None, :KCONV],
        sums[KCONV][None],
        sums[KCONV + 1 : KCONV + 2, INNER:heads_at],
        sums[KCONV + 1 : KCONV + 2, heads_at : heads_at + HEADS],
        sums[KCONV + 1 : KCONV + 2, heads_at + HEADS : heads_at + 2 * HEADS],
        sums[KCONV + 1 : KCONV + 2, :INNER],
        g_out[None],
    )


def solution(mesh):
    placed = (
        P("section", None, "wshard", "seq", None),
        P(None, "wshard", None),
        P(None, "wshard", None),
        P("section", None),
        P("section", "wshard", None),
        P("section", None, None),
        P("section", None),
        P("section", None),
        P("section", None),
        P("section", None),
        P("section", None),
        P("section", "wshard", None),
    )
    return jax.shard_map(
        on_device,
        mesh=mesh,
        in_specs=placed,
        out_specs=(
            P("section", None, "wshard", "seq", None),
            P("section", None),
            P("section", ("seq", "wshard"), None),
            P("section", None, None),
            P("section", None),
            P("section", None),
            P("section", None),
            P("section", None),
            P("section", None),
            P("section", ("seq", "wshard"), None),
        ),
        check_vma=False,
    )
```

```python
import functools
import types

import jax
import jax.numpy as jnp
from jax import lax
from jax.experimental import pallas as pl
from jax.experimental.pallas import tpu as pltpu
from jax.sharding import PartitionSpec as P

D = 1024
HEADDIM = 64
STATE = 128
KCONV = 4
BLOCK = 256
INNER = 2048
HEADS = 32
PAIR = 2 * STATE
LANES = 128
EPS = 1e-05
NEG = -1e30
BF = jnp.bfloat16
F32 = jnp.float32
HIGH = lax.Precision.HIGHEST
AXES = ("section", "seq", "wshard")
VMEM_LIMIT = 58 << 20
MICRO = 1.15e9


def nn(a, b, precision=None):
    return lax.dot_general(
        a, b, (((1,), (0,)), ((), ())), preferred_element_type=F32, precision=precision
    )


def nt(a, b):
    return lax.dot_general(a, b, (((1,), (1,)), ((), ())), preferred_element_type=F32)


def tn(a, b):
    return lax.dot_general(a, b, (((0,), (0,)), ((), ())), preferred_element_type=F32)


def two(x):
    hi = x.astype(BF)
    lo = (x - hi.astype(F32)).astype(BF)
    return jnp.concatenate([hi, lo], axis=1)


def sums(choice, x):
    first = x.astype(BF)
    rest = x - first.astype(F32)
    second = rest.astype(BF)
    third = (rest - second.astype(F32)).astype(BF)
    return nn(choice, first) + nn(choice, second) + nn(choice, third)


def iota(shape, dim):
    return lax.broadcasted_iota(jnp.int32, shape, dim)


def column(row):
    return jnp.broadcast_to(row, (LANES, row.shape[1])).T[:, :1]


def as_row(col):
    return jnp.broadcast_to(col, (col.shape[0], LANES)).T[:1]


def sigmoid(x):
    return 0.5 * jnp.tanh(0.5 * x) + 0.5


def softplus(x):
    return jnp.maximum(x, 0.0) + jnp.log1p(jnp.exp(-jnp.abs(x)))


def full(shape):
    return pl.BlockSpec(shape, lambda i: (0,) * len(shape))


class Names:
    def __getattr__(self, name):
        return name


N = Names()


def launch(name, body, grid, ins, outs, scratch=(), micros=1, aliases=()):
    names = [item[0] for item in ins] + [item[0] for item in outs] + [item[0] for item in scratch]

    def kernel(*refs):
        body(types.SimpleNamespace(**dict(zip(names, refs))))

    results = pl.pallas_call(
        kernel,
        grid=grid,
        in_specs=[item[2] for item in ins],
        out_specs=[item[3] for item in outs],
        out_shape=[jax.ShapeDtypeStruct(item[1], item[2]) for item in outs],
        scratch_shapes=[item[1] for item in scratch],
        compiler_params=pltpu.CompilerParams(
            dimension_semantics=(N.arbitrary,) * len(grid), vmem_limit_bytes=VMEM_LIMIT
        ),
        input_output_aliases=dict(aliases),
        cost_estimate=pl.CostEstimate(
            flops=int(micros * MICRO), bytes_accessed=1, transcendentals=0
        ),
        name=name,
    )(*[item[1] for item in ins])
    return types.SimpleNamespace(**dict(zip([item[0] for item in outs], results)))


def small():
    return pl.BlockSpec(memory_space=pltpu.SMEM)


def rows_of(width, first=0):
    return pl.BlockSpec((BLOCK, width), lambda i: (first + i, 0))


def turned(width, last):
    return pl.BlockSpec((BLOCK, width), lambda i: (last - i, 0))


def place(orders, halves):
    mine, theirs = halves
    total = 2 * mine.shape[0]

    def body(r):
        at = pl.program_id(0) * BLOCK + iota((BLOCK, total // 2), 0)
        first = (r.mine_order[...] == at).astype(BF)
        second = (r.their_order[...] == at).astype(BF)
        r.out[...] = (nn(first, r.mine[...]) + nn(second, r.theirs[...])).astype(BF)

    return launch(
        N.place,
        body,
        (total // BLOCK,),
        [
            (N.mine_order, orders[0], full((1, total // 2))),
            (N.their_order, orders[1], full((1, total // 2))),
            (N.mine, mine, full((total // 2, D))),
            (N.theirs, theirs, full((total // 2, D))),
        ],
        [(N.out, (total, D), BF, rows_of(D))],
        micros=5.3,
    ).out


def prepare_in(spot, in_w, seq):
    depth = in_w.shape[2] // 2
    heads = HEADS // seq
    width = heads * HEADDIM
    wide = max(width, LANES)
    side = 2 * wide + LANES
    shape = (2 * side + PAIR, depth)

    def body(r):
        core = r.spot[0]
        for at in range(seq // 2):

            @pl.when(r.spot[3] == at)
            def _():
                for half, ref in ((core, r.keep), (1 - core, r.give)):
                    span = pl.ds(pl.multiple_of(half * depth, depth), depth)
                    edge = r.w[0, 2 * INNER + PAIR :, span].astype(F32)

                    def piece(start):
                        value = r.w[0, start : start + width, span]
                        if width < wide:
                            room = jnp.zeros((wide - width, depth), BF)
                            value = jnp.concatenate([value, room], axis=0)
                        return value

                    for index in range(2):
                        head = 2 * at + index
                        base = index * (side + PAIR)
                        ref[base : base + wide] = piece(width * head)
                        ref[base + wide : base + 2 * wide] = piece(INNER + width * head)
                        raw = edge[heads * head : heads * (head + 1)]
                        room = jnp.zeros((LANES - heads, depth), F32)
                        raw = jnp.concatenate([raw, room], axis=0).astype(BF)
                        ref[base + 2 * wide : base + side] = raw
                    ref[side : side + PAIR] = r.w[0, 2 * INNER : 2 * INNER + PAIR, span]

    return launch(
        N.prepare_in,
        body,
        (1,),
        [(N.spot, spot, small()), (N.w, in_w, full(in_w.shape))],
        [(N.keep, shape, BF, full(shape)), (N.give, shape, BF, full(shape))],
        micros=3,
    )


def prepare_rest(spot, out_w, ends):
    out_shape = (out_w.shape[1] // 2, D)
    end_shape = (2, ends.shape[3] // 2, D)

    def body(r):
        core = r.spot[0]
        for half, out, end in ((core, r.out_keep, r.end_keep), (1 - core, r.out_give, r.end_give)):
            size = out_shape[0]
            out[...] = r.out_w[0, pl.ds(pl.multiple_of(half * size, size), size)]
            size = end_shape[1]
            span = pl.ds(pl.multiple_of(half * size, size), size)
            for batch in range(2):
                end[batch] = r.ends[0, batch, 0, span]

    return launch(
        N.prepare_rest,
        body,
        (1,),
        [
            (N.spot, spot, small()),
            (N.out_w, out_w, full(out_w.shape)),
            (N.ends, ends, full(ends.shape)),
        ],
        [
            (N.out_keep, out_shape, BF, full(out_shape)),
            (N.out_give, out_shape, BF, full(out_shape)),
            (N.end_keep, end_shape, BF, full(end_shape)),
            (N.end_give, end_shape, BF, full(end_shape)),
        ],
        micros=3,
    )


def assemble(spot, mine, theirs, wide, by_distance):
    depth = mine[0].shape[-1]
    side = 2 * wide + LANES
    total = PAIR + side
    count = 4

    def body(r):
        w = r.spot[1]
        named = vars(r)

        def parts_of(name, arrays):
            found = []
            for index, array in enumerate(arrays):
                ref = named[name + str(index)]
                if array.ndim == 2:
                    found.append(ref)
                else:
                    found += [ref.at[k] for k in range(array.shape[0])]
            return found

        def move(source, start, base, pair):
            span = pl.ds(pl.multiple_of(start, depth), depth)
            r.out[:wide, span] = source[base : base + wide]
            r.out[wide : wide + PAIR, span] = source[pair : pair + PAIR]
            r.out[wide + PAIR :, span] = source[base + wide : base + side]

        for core in range(2):

            @pl.when(r.spot[0] == core)
            def _():
                own = core * (side + PAIR)
                shards = list(range(count))
                other = shards
                if by_distance:
                    shards = (w, w ^ (1 + core), w ^ (2 - core), w ^ 3)
                    other = (w, w ^ (2 - core), w ^ (1 + core), w ^ 3)
                for source, shard in zip(parts_of(N.mine, mine), shards):
                    move(source, (2 * shard + core) * depth, own, side)
                for source, shard in zip(parts_of(N.theirs, theirs), other):
                    move(source, (2 * shard + 1 - core) * depth, core * PAIR, (1 - core) * side)

    return launch(
        N.assemble,
        body,
        (1,),
        [(N.spot, spot, small())]
        + [(N.mine + str(k), value, full(value.shape)) for k, value in enumerate(mine)]
        + [(N.theirs + str(k), value, full(value.shape)) for k, value in enumerate(theirs)],
        [(N.out, (total, 2 * count * depth), BF, full((total, 2 * count * depth)))],
        micros=4.5,
    ).out


def block_terms(raw, dtb, rate_sign, offset):
    rate = softplus(raw + dtb)
    lower = (iota((BLOCK, BLOCK), 1) <= iota((BLOCK, BLOCK), 0)).astype(BF)
    level = sums(lower, rate * rate_sign)
    local = iota((BLOCK, 1), 0)
    end = level[BLOCK - 1 :]
    end_offset = offset[BLOCK - 1 :]
    head = jnp.where(offset > local, jnp.exp(level), 0.0)
    fade = jnp.where(local >= BLOCK - 1 - end_offset, jnp.exp(end - level), 0.0)
    carry = jnp.where(end_offset > BLOCK - 1, jnp.exp(end), 0.0)
    return rate, level, head, fade, carry


def either(flag, first, second):
    chosen = flag.astype(F32)
    return chosen * first.astype(F32) + (1.0 - chosen) * second.astype(F32)


def keep_or_give(r, core, block, split, value):
    slot = pl.ds(pl.multiple_of(block % split * BLOCK, BLOCK), BLOCK)

    @pl.when(block // split == core)
    def _():
        r.keep[slot] = value

    @pl.when(block // split != core)
    def _():
        r.away[slot] = value


def forward_body(layer, begin, wide, split, r):
    heads = wide // HEADDIM
    conv = PAIR + wide
    step = pl.program_id(0)
    core = r.spot[0]

    @pl.when(step == 0)
    def _():
        if begin:
            r.state[...] = jnp.zeros_like(r.state)
            r.halo[...] = jnp.zeros_like(r.halo)
        else:
            r.state[...] = r.state_in[...]
            r.halo[...] = r.halo_in[...]

    tokens = r.tokens[...].astype(F32)
    if layer == 1:
        scale = lax.rsqrt(column(r.last_rows[0][0:1]) / INNER + EPS)
        summed = either(step // split == core, r.mine[...], r.theirs[...])
        low = (tokens + summed * scale).astype(BF)
        r.next[...] = low
        tokens = low.astype(F32)
    scale = lax.rsqrt(jnp.mean(tokens * tokens, axis=1, keepdims=True) + EPS)
    x = (tokens * scale * r.gain[...]).astype(BF)
    r.normed[...] = x
    projected = nt(x, r.w[...])
    gate = projected[:, :wide]
    r.gate[...] = gate
    cin_low = projected[:, wide : wide + conv].astype(BF)
    r.cin[...] = cin_low
    raw_low = projected[:, wide + conv :].astype(BF)
    r.raw[...] = raw_low
    pos = r.pos[...]
    label_col = pos[:, 0:1]
    offset = pos[:, 1:2]
    cin = cin_low.astype(F32)
    longer = jnp.concatenate([r.halo[...], cin], axis=0)
    r.halo[...] = cin[BLOCK - 8 :]
    taps = r.taps[...]
    pre = taps[KCONV : KCONV + 1] + taps[KCONV - 1 : KCONV] * cin
    for index in range(KCONV - 1):
        delay = KCONV - 1 - index
        moved = longer[8 - delay : 8 - delay + BLOCK]
        pre = pre + jnp.where(offset >= delay, taps[index : index + 1] * moved, 0.0)
    r.pre[...] = pre
    mixed_conv = (pre * sigmoid(pre)).astype(BF)
    write = mixed_conv[:, :STATE]
    read = mixed_conv[:, STATE:PAIR]
    xs = mixed_conv[:, PAIR:]
    xs_float = xs.astype(F32)
    terms = r.terms[...]
    rate, level, head, fade, carry = block_terms(
        raw_low.astype(F32), terms[0:1], terms[1:2], offset
    )
    level_rows = level.T
    rate_rows = rate.T
    spread = r.spread[...]
    state = r.state[...]
    r.states[0] = state
    wides = r.wides[...]
    mixed = nn(two(head), spread) * nn(read, state.astype(BF)) + wides[0:1] * xs_float
    gram = nt(read, write)
    inside = (label_col == r.label[0]) & (iota((BLOCK, BLOCK), 1) <= iota((BLOCK, BLOCK), 0))
    closed = jnp.where(inside, 0.0, NEG)
    parts = []
    for first in range(0, heads, 2):
        span = xs[:, first * HEADDIM : (first + 2) * HEADDIM]
        mixing = []
        values = []
        for h in range(first, first + 2):
            weight = jnp.exp(level[:, h : h + 1] - level_rows[h : h + 1] + closed)
            mixing.append((gram * (weight * rate_rows[h : h + 1])).astype(BF))
            own = iota(span.shape, 1) // HEADDIM == h - first
            values.append(jnp.where(own, span, jnp.zeros_like(span)))
        parts.append(nn(jnp.concatenate(mixing, axis=1), jnp.concatenate(values, axis=0)))
    mixed = mixed + jnp.concatenate(parts, axis=1)
    mixed_low = mixed.astype(BF)
    r.mixed[...] = mixed_low
    carry_wide = nn(two(jnp.broadcast_to(carry, (8, LANES))), spread)[:1]
    written = (nn(two(fade * rate), spread) * xs_float).astype(BF)
    r.state[...] = carry_wide * state + tn(write, written)
    gv = mixed_low.astype(F32) * (gate * sigmoid(gate))
    r.rows[0, 0:1] = as_row(jnp.sum(gv * gv, axis=1, keepdims=True))
    scaled = gv * wides[1:2]
    if layer == 1:
        dotted = nt(r.dout[...], r.w_out[...]) * scaled
        r.rows[0, 1:2] = as_row(jnp.sum(dotted, axis=1, keepdims=True))
    else:
        r.rows[0, 1:2] = jnp.zeros((1, BLOCK), F32)
    keep_or_give(r, core, step, split, nn(scaled.astype(BF), r.w_out[...]).astype(BF))


def forward(layer, part, spot, env, tokens, before, weights, vectors, carried, dout):
    w, w_out = weights
    wide = w_out.shape[0]
    conv = PAIR + wide
    count = tokens.shape[0] // BLOCK // 2
    split = count // 2
    first = part * count
    total = count * BLOCK
    row = pl.BlockSpec((1, 2, BLOCK), lambda i: (i, 0, 0))
    ins = [
        (N.spot, spot, small()),
        (N.tokens, tokens, rows_of(D, first)),
        (N.gain, vectors[N.gain], full((1, D))),
        (N.w, w, full(w.shape)),
        (N.w_out, w_out, full(w_out.shape)),
        (N.taps, vectors[N.taps], full((8, conv))),
        (N.terms, vectors[N.terms], full((8, LANES))),
        (N.wides, vectors[N.wides], full((8, wide))),
        (N.spread, env.spread, full(env.spread.shape)),
        (N.pos, env.pos, rows_of(3, first)),
        (N.label, env.label_row, pl.BlockSpec((1, 1, BLOCK), lambda i: (first + i, 0, 0))),
    ]
    outs = [
        (N.normed, (total, D), BF, rows_of(D)),
        (N.gate, (total, wide), F32, rows_of(wide)),
        (N.pre, (total, conv), F32, rows_of(conv)),
        (N.cin, (total, conv), BF, rows_of(conv)),
        (N.raw, (total, LANES), BF, rows_of(LANES)),
        (N.mixed, (total, wide), BF, rows_of(wide)),
        (N.states, (count, STATE, wide), F32, pl.BlockSpec((1, STATE, wide), lambda i: (i, 0, 0))),
        (N.rows, (count, 2, BLOCK), F32, row),
        (N.state, (STATE, wide), F32, full((STATE, wide))),
        (N.halo, (8, conv), F32, full((8, conv))),
    ]
    joint = layer * total // 2
    side = pl.BlockSpec((total // 2, D), lambda i: (part * layer, 0))
    outs += [
        (N.keep, (total // 2 + joint, D), BF, side),
        (N.away, (total // 2 + joint, D), BF, side),
    ]
    aliases = []
    if part == 1:
        ins += [
            (N.state_in, carried.state, full((STATE, wide))),
            (N.halo_in, carried.halo, full((8, conv))),
        ]
        if layer == 1:
            anywhere = pl.BlockSpec(memory_space=pl.ANY)
            aliases = [(len(ins), len(outs) - 2), (len(ins) + 1, len(outs) - 1)]
            ins += [(N.keep_in, carried.keep, anywhere), (N.away_in, carried.away, anywhere)]
    if layer == 1:
        block = pl.BlockSpec((BLOCK, D), lambda i: (i % split, 0))
        mine, theirs, last_rows = before
        ins += [
            (N.mine, mine, block),
            (N.theirs, theirs, block),
            (N.last_rows, last_rows, row),
            (N.dout, dout, rows_of(D, first)),
        ]
        outs.append((N.next, (total, D), BF, rows_of(D)))
    return launch(
        N.forward,
        functools.partial(forward_body, layer, part == 0, wide, split),
        (count,),
        ins,
        outs,
        micros=12.5,
        aliases=aliases,
    )


def ungate_body(layer, wide, count, split, r):
    step = pl.program_id(0)
    block = count - 1 - step
    core = r.spot[0]

    @pl.when(step == 0)
    def _():
        r.ggated[...] = jnp.zeros_like(r.ggated)

    scale = lax.rsqrt(column(r.rows[0][0:1]) / INNER + EPS)
    if layer == 1:
        dout = r.dout[...]
        dots = column(r.rows[0][1:2])
    else:
        flag = block // split == core
        grad = either(flag, r.grad_mine[...], r.grad_theirs[...])
        dtokens = unnorm(r.tokens[...].astype(F32), r.gain[...], grad)
        dout = (r.dlater[...].astype(F32) + dtokens).astype(BF)
        r.dout[...] = dout
        summed = either(flag, r.mine[...], r.theirs[...])
        dots = jnp.sum(dout.astype(F32) * summed, axis=1, keepdims=True)
    gate = r.gate[...]
    gain = r.wides[1:2]
    mixed = r.mixed[...].astype(F32)
    sig = sigmoid(gate)
    act = gate * sig
    normal = mixed * act * scale
    grad_out = nt(dout, r.w_out[...])
    shared = dots * scale / INNER
    grad_gv = scale * (grad_out * gain - normal * shared)
    r.dmixed[...] = (grad_gv * act).astype(BF)
    r.dgate[...] = (grad_gv * mixed * (sig * (1.0 + gate * (1.0 - sig)))).astype(BF)
    r.ggated[...] += jnp.sum(grad_out * normal, axis=0, keepdims=True)
    r.normed_out[...] = (normal * gain).astype(BF)


def unnorm(tokens, gain, grad):
    scale = lax.rsqrt(jnp.mean(tokens * tokens, axis=1, keepdims=True) + EPS)
    normal = tokens * scale
    inner = grad * gain
    return scale * (inner - normal * jnp.mean(inner * normal, axis=1, keepdims=True))


def ungate(layer, part, spot, kept, rows, w_out, vectors, above):
    total, wide = kept.mixed.shape
    count = total // BLOCK
    split = count // 2
    last = count - 1
    row = pl.BlockSpec((1, 2, BLOCK), lambda i: (last - i, 0, 0))
    ins = [
        (N.spot, spot, small()),
        (N.rows, rows, row),
        (N.gate, kept.gate, turned(wide, last)),
        (N.mixed, kept.mixed, turned(wide, last)),
        (N.wides, vectors[N.wides], full((8, wide))),
        (N.w_out, w_out, full((wide, D))),
    ]
    outs = [
        (N.dmixed, (total, wide), BF, turned(wide, last)),
        (N.dgate, (total, wide), BF, turned(wide, last)),
        (N.normed_out, (total, wide), BF, turned(wide, last)),
        (N.ggated, (1, wide), F32, full((1, wide))),
    ]
    if layer == 1:
        ins.append((N.dout, above.dout, turned(D, part * count + last)))
    else:
        block = pl.BlockSpec((BLOCK, D), lambda i: ((last - i) % split, 0))
        ins += [
            (N.grad_mine, above.grad[0], block),
            (N.grad_theirs, above.grad[1], block),
            (N.mine, above.summed[0], block),
            (N.theirs, above.summed[1], block),
            (N.tokens, above.tokens, turned(D, last)),
            (N.gain, above.gain, full((1, D))),
            (N.dlater, above.dout, turned(D, part * count + last)),
        ]
        outs.append((N.dout, (total, D), BF, turned(D, last)))
    return launch(
        N.ungate,
        functools.partial(ungate_body, layer, wide, count, split),
        (count,),
        ins,
        outs,
        micros=5.5,
    )


def backward_body(begin, wide, count, split, r):
    heads = wide // HEADDIM
    conv = PAIR + wide
    step = pl.program_id(0)
    block = count - 1 - step
    core = r.spot[0]

    @pl.when(step == 0)
    def _():
        if begin:
            r.dstate[...] = jnp.zeros_like(r.dstate)
            r.halo[...] = jnp.zeros_like(r.halo)
        else:
            r.dstate[...] = r.dstate_in[...]
            r.halo[...] = r.halo_in[...]
        r.gtaps[...] = jnp.zeros_like(r.gtaps)
        r.gheads[...] = jnp.zeros_like(r.gheads)
        r.gskip[...] = jnp.zeros_like(r.gskip)
        r.ggain[...] = jnp.zeros_like(r.ggain)

    pos = r.pos[...]
    label_col = pos[:, 0:1]
    offset = pos[:, 1:2]
    remain = pos[:, 2:3]
    pre = r.pre[...]
    sig = sigmoid(pre)
    mixed_conv = (pre * sig).astype(BF)
    write = mixed_conv[:, :STATE]
    read = mixed_conv[:, STATE:PAIR]
    xs = mixed_conv[:, PAIR:]
    xs_float = xs.astype(F32)
    raw = r.raw[...].astype(F32)
    terms = r.terms[...]
    dtb = terms[0:1]
    sign = terms[1:2]
    rate, level, head, fade, carry = block_terms(raw, dtb, sign, offset)
    tail = fade * rate
    level_rows = level.T
    spread = r.spread[...]
    fold = r.fold[...]
    dy = r.dmixed[...]
    dy_float = dy.astype(F32)
    state = r.states[0]
    state_low = state.astype(BF)
    dstate = r.dstate[...]
    dstate_low = dstate.astype(BF)
    dhead = nn(two(dy_float * nn(read, state_low)), fold)
    tail_wide = nn(two(tail), spread)
    scaled = (nn(two(head), spread) * dy_float).astype(BF)
    written = (tail_wide * xs_float).astype(BF)
    through = nn(write, dstate_low)
    dtail = nn(two(xs_float * through), fold)
    r.gskip[...] += jnp.sum(dy_float * xs_float, axis=0, keepdims=True)
    carry_wide = nn(two(jnp.broadcast_to(carry, (8, LANES))), spread)[:1]
    held = jnp.broadcast_to(jnp.sum(state * dstate, axis=0, keepdims=True), (8, wide))
    dcarry = nn(two(held), fold)[:1]

    gram = nt(write, read)
    inside = (label_col == r.label[0]) & (iota((BLOCK, BLOCK), 0) <= iota((BLOCK, BLOCK), 1))
    closed = jnp.where(inside, 0.0, NEG)
    lane = iota((1, LANES), 1)
    drate = jnp.zeros((BLOCK, LANES), F32)
    level_sums = []
    parts = []
    dgram = jnp.zeros((BLOCK, BLOCK), F32)
    for first in range(0, heads, 2):
        cut_at = slice(first * HEADDIM, (first + 2) * HEADDIM)
        xs_span = xs[:, cut_at]
        dy_span = dy[:, cut_at]
        mixing = []
        values = []
        for h in range(first, first + 2):
            own = iota(xs_span.shape, 1) // HEADDIM == h - first
            xs_own = jnp.where(own, xs_span, jnp.zeros_like(xs_span))
            values.append(jnp.where(own, dy_span, jnp.zeros_like(dy_span)))
            decay = jnp.exp(level_rows[h : h + 1] - level[:, h : h + 1] + closed)
            rate_col = rate[:, h : h + 1]
            weight = decay * rate_col
            mixing.append((gram * weight).astype(BF))
            dmix = nt(xs_own, dy_span)
            dgram = dgram + dmix * weight
            bare = dmix * gram * decay
            drate = drate + jnp.sum(bare, axis=1, keepdims=True) * (lane == h).astype(F32)
            level_sums.append(jnp.sum(bare * rate_col, axis=0, keepdims=True))
        parts.append(nn(jnp.concatenate(mixing, axis=1), jnp.concatenate(values, axis=0)))
    dxs = jnp.concatenate(parts, axis=1) + r.wides[0:1] * dy_float + tail_wide * through
    dgram_low = dgram.astype(BF)
    dread = tn(dgram_low, write) + nt(scaled, state_low)
    dwrite = nn(dgram_low, read) + nt(written, dstate_low)
    r.dstate[...] = carry_wide * dstate + tn(read, scaled)

    level_sums.append(jnp.zeros((LANES - heads, BLOCK), F32))
    tail_flow = dtail * tail
    local = iota((BLOCK, 1), 0)
    last = jnp.sum(tail_flow, axis=0, keepdims=True) + dcarry * carry
    dlevel = jnp.concatenate(level_sums, axis=0).T - rate * drate + dhead * head - tail_flow
    dlevel = dlevel + jnp.where(local == BLOCK - 1, last, 0.0)
    upper = (iota((BLOCK, BLOCK), 0) <= iota((BLOCK, BLOCK), 1)).astype(BF)
    dsum = sums(upper, dlevel)
    drate = drate + dtail * fade + sign * dsum
    draw = drate * sigmoid(raw + dtb)
    r.gheads[0:1] += jnp.sum(draw, axis=0, keepdims=True)
    r.gheads[1:2] += jnp.sum(rate * dsum, axis=0, keepdims=True) * sign

    dpre = jnp.concatenate([dwrite, dread, dxs], axis=1) * (sig * (1.0 + pre * (1.0 - sig)))
    longer = jnp.concatenate([dpre, r.halo[...]], axis=0)
    r.halo[...] = dpre[:8]
    cin = r.cin[...].astype(F32)
    taps = r.taps[...]
    r.gtaps[KCONV : KCONV + 1] += jnp.sum(dpre, axis=0, keepdims=True)
    r.gtaps[KCONV - 1 : KCONV] += jnp.sum(dpre * cin, axis=0, keepdims=True)
    dcin = taps[KCONV - 1 : KCONV] * dpre
    for index in range(KCONV - 1):
        delay = KCONV - 1 - index
        moved = jnp.where(remain >= delay, longer[delay : delay + BLOCK], 0.0)
        dcin = dcin + taps[index : index + 1] * moved
        r.gtaps[index : index + 1] += jnp.sum(moved * cin, axis=0, keepdims=True)
    rest = jnp.concatenate([dcin, draw], axis=1).astype(BF)
    r.rest[...] = rest
    w = r.w[...]
    dnormed = nn(r.dgate[...], w[:wide]) + nn(rest, w[wide:])
    r.ggain[...] += jnp.sum(dnormed * r.normed[...].astype(F32), axis=0, keepdims=True)
    keep_or_give(r, core, block, split, dnormed.astype(BF))


def backward(part, spot, env, kept, grads, w, vectors, carried):
    total, wide = kept.mixed.shape
    conv = PAIR + wide
    count = total // BLOCK
    split = count // 2
    last = count - 1
    top = part * count + last
    ins = [
        (N.spot, spot, small()),
        (N.w, w, full(w.shape)),
        (N.taps, vectors[N.taps], full((8, conv))),
        (N.terms, vectors[N.terms], full((8, LANES))),
        (N.wides, vectors[N.wides], full((8, wide))),
        (N.spread, env.spread, full(env.spread.shape)),
        (N.fold, env.fold, full(env.fold.shape)),
        (N.pos, env.pos, turned(3, top)),
        (N.label, env.label_row, pl.BlockSpec((1, 1, BLOCK), lambda i: (top - i, 0, 0))),
        (N.pre, kept.pre, turned(conv, last)),
        (N.cin, kept.cin, turned(conv, last)),
        (N.raw, kept.raw, turned(LANES, last)),
        (N.states, kept.states, pl.BlockSpec((1, STATE, wide), lambda i: (last - i, 0, 0))),
        (N.normed, kept.normed, turned(D, last)),
        (N.dmixed, grads.dmixed, turned(wide, last)),
        (N.dgate, grads.dgate, turned(wide, last)),
    ]
    if part == 0:
        ins += [
            (N.dstate_in, carried.dstate, full((STATE, wide))),
            (N.halo_in, carried.halo, full((8, conv))),
        ]
    outs = [
        (N.keep, (total // 2, D), BF, full((total // 2, D))),
        (N.away, (total // 2, D), BF, full((total // 2, D))),
        (N.rest, (total, conv + LANES), BF, turned(conv + LANES, last)),
        (N.gtaps, (8, conv), F32, full((8, conv))),
        (N.gheads, (8, LANES), F32, full((8, LANES))),
        (N.gskip, (1, wide), F32, full((1, wide))),
        (N.ggain, (1, D), F32, full((1, D))),
        (N.dstate, (STATE, wide), F32, full((STATE, wide))),
        (N.halo, (8, conv), F32, full((8, conv))),
    ]
    return launch(
        N.backward,
        functools.partial(backward_body, part == 1, wide, count, split),
        (count,),
        ins,
        outs,
        micros=14.5,
    )


def weight_grads(spot, lefts, rights, seq, outer=None, size=0):
    depth = lefts[0].shape[1]
    spans = []
    wide = 0
    for pair in rights:
        spans.append((wide, pair[0].shape[1]))
        wide += pair[0].shape[1]
    share = depth // (4 * seq)
    rows = depth // 4
    room = 0 if outer is None else outer[0][0].shape[1]

    def body(r):
        w = r.spot[1]
        z = r.spot[2]
        named = vars(r)
        sides = ((r.keep, (0, r.spot[5])), (r.away, (r.spot[4], 3)))
        for index, (base, width) in enumerate(spans):
            right = [named[N.right + str(index) + str(part)] for part in range(2)]
            r.total[:, base : base + width] = tn(r.left0[...], right[0][...]) + tn(
                r.left1[...], right[1][...]
            )
        for ref, shards in sides:
            for index, shard in enumerate(shards):
                for turn in range(seq):
                    start = ((z ^ turn) * 4 + (w ^ shard)) * share
                    piece = r.total[pl.ds(pl.multiple_of(start, share), share)]
                    ref[index, turn * share : (turn + 1) * share, :wide] = piece.astype(BF)
        if outer is None:
            return
        for part in range(D // room):
            cols = slice(part * room, (part + 1) * room)
            r.outer[...] = tn(r.out0[...], r.dout0[...][:, cols]) + tn(
                r.out1[...], r.dout1[...][:, cols]
            )
            for ref, shards in sides:
                for index, shard in enumerate(shards):
                    start = pl.multiple_of((w ^ shard) * size, size)
                    ref[index, part * size : (part + 1) * size, wide:] = r.outer[
                        pl.ds(start, size)
                    ].astype(BF)
        if size * (D // room) < rows:
            for ref, _ in sides:
                ref[:, size * (D // room) :, wide:] = jnp.zeros(
                    (2, rows - size * (D // room), room), BF
                )

    ins = [(N.spot, spot, small())]
    for index in range(2):
        ins.append((N.left + str(index), lefts[index], full(lefts[index].shape)))
    for index, pair in enumerate(rights):
        for part in range(2):
            ins.append((N.right + str(index) + str(part), pair[part], full(pair[part].shape)))
    scratch = [(N.total, pltpu.VMEM((depth, wide), F32))]
    if outer is not None:
        outs, douts = outer
        height = outs[0].shape[0]
        for index in range(2):
            ins.append((N.out + str(index), outs[index], full(outs[index].shape)))
            array, at = douts[index]
            spec = pl.BlockSpec((height, D), functools.partial(lambda at, i: (at, 0), at))
            ins.append((N.dout + str(index), array, spec))
        scratch.append((N.outer, pltpu.VMEM((room, room), F32)))
    shape = (2, rows, wide + room)
    return launch(
        N.weight_grads,
        body,
        (1,),
        ins,
        [(N.keep, shape, BF, full(shape)), (N.away, shape, BF, full(shape))],
        scratch=scratch,
        micros=6 if len(rights) == 1 else 11,
    )


def finish(kind, part, spot, orders, values, before):
    count = values.count
    split = count // 2
    total = count * BLOCK

    def body(r):
        step = pl.program_id(0)
        core = r.spot[0]

        @pl.when(step == 0)
        def _():
            if before is None:
                r.own[...] = jnp.zeros_like(r.own)
                r.across[...] = jnp.zeros_like(r.across)
            else:
                r.own[...] = r.own_in[...]
                r.across[...] = r.across_in[...]

        summed = either(step // split == core, r.mine[...], r.theirs[...])
        if kind == N.grad:
            dtokens = unnorm(r.tokens[...].astype(F32), r.gain[...], summed)
            value = r.rest[...].astype(F32) + dtokens
        else:
            scale = lax.rsqrt(column(r.rows[0][0:1]) / INNER + EPS)
            value = r.rest[...].astype(F32) + summed * scale
        low = value.astype(BF)
        at = (part * count + step) * BLOCK + iota((BLOCK, BLOCK), 1)
        r.own[...] += nn((r.own_order[...] == at).astype(BF), low).astype(BF)
        r.across[...] += nn((r.far_order[...] == at).astype(BF), low).astype(BF)

    block = pl.BlockSpec((BLOCK, D), lambda i: (values.first + i % split, 0))
    ins = [
        (N.spot, spot, small()),
        (N.own_order, orders[0], full((BLOCK, 1))),
        (N.far_order, orders[1], full((BLOCK, 1))),
        (N.mine, values.summed[0], block),
        (N.theirs, values.summed[1], block),
        (N.rest, values.rest, rows_of(D)),
    ]
    outs = [
        (N.own, (BLOCK, D), BF, full((BLOCK, D))),
        (N.across, (BLOCK, D), BF, full((BLOCK, D))),
    ]
    if kind == N.grad:
        ins += [
            (N.tokens, values.tokens, rows_of(D, part * count)),
            (N.gain, values.gain, full((1, D))),
        ]
    else:
        ins.append((N.rows, values.rows, pl.BlockSpec((1, 2, BLOCK), lambda i: (i, 0, 0))))
    if before is not None:
        ins += [
            (N.own_in, before.own, full((BLOCK, D))),
            (N.across_in, before.across, full((BLOCK, D))),
        ]
    return launch(
        N.finish, body, (count,), ins, outs, micros=5,
    )


def settle(spot, ends):
    rows = ends[0].shape[0]

    def body(r):
        core = r.spot[0]
        batch = r.spot[7]
        for layer, own, far in ((0, r.own0, r.far0), (1, r.own1, r.far1)):
            for at in range(2):

                @pl.when((core == layer) & (batch == at))
                def _():
                    r.out[0, at, 0] = own[...].astype(F32)
                    r.out[0, 1 - at, 0] = far[...].astype(F32)

    names = (N.own0, N.far0, N.own1, N.far1)
    shape = (1, 2, 1, rows, D)
    return launch(
        N.settle,
        body,
        (1,),
        [(N.spot, spot, small())]
        + [(name, value, full(value.shape)) for name, value in zip(names, ends)],
        [(N.out, shape, F32, full(shape))],
        micros=2,
    ).out


def gather_columns(spot, sides, seq):
    half = seq // 2
    heads = HEADS // seq
    width = heads * HEADDIM
    wide = max(width, LANES)
    share = sides[0][0].shape[1]
    shape = (1, share, 2 * INNER + PAIR + HEADS)

    def body(r):
        named = vars(r)
        for layer in range(2):

            @pl.when(r.spot[0] == layer)
            def _():
                raws = []
                pair = jnp.zeros((share, PAIR), F32)
                for place_at in range(half):
                    for side in range(2):
                        rank = 2 * place_at + side
                        part = named[N.side + str(layer) + str(side)][place_at].astype(F32)
                        r.out[0, :, width * rank : width * (rank + 1)] = part[:, :width]
                        start = wide + PAIR
                        r.out[0, :, INNER + width * rank : INNER + width * (rank + 1)] = part[
                            :, start : start + width
                        ]
                        pair = pair + part[:, wide : wide + PAIR]
                        raws.append(part[:, start + wide : start + wide + heads])
                r.out[0, :, 2 * INNER : 2 * INNER + PAIR] = pair
                r.out[0, :, 2 * INNER + PAIR :] = jnp.concatenate(raws, axis=1)

    ins = [(N.spot, spot, small())]
    for layer in range(2):
        for side in range(2):
            value = sides[layer][side]
            ins.append((N.side + str(layer) + str(side), value, full(value.shape)))
    return launch(
        N.gather_columns, body, (1,), ins, [(N.out, shape, F32, full(shape))], micros=2
    ).out


def pack(spot, fold, gains, scans, gated, seq):
    heads = HEADS // seq
    width = heads * HEADDIM
    wide = max(width, LANES)
    conv = PAIR + wide
    shape = (KCONV + 3, INNER + PAIR)
    ins = [(N.spot, spot, small()), (N.fold, fold, full(fold.shape))]
    for layer in range(2):
        ins.append((N.gain + str(layer), gains[layer], full((1, D))))
        for part in range(2):
            scan = scans[layer][part]
            for name, value in (
                (N.gtaps, scan.gtaps),
                (N.gheads, scan.gheads),
                (N.gskip, scan.gskip),
                (N.ggain, scan.ggain),
                (N.ggated, gated[layer][part].ggated),
            ):
                ins.append((name + str(layer) + str(part), value, full(value.shape)))

    def body(r):
        named = vars(r)

        def both(name, layer):
            return named[name + str(layer) + "0"][...] + named[name + str(layer) + "1"][...]

        for layer in range(2):
            taps = both(N.gtaps, layer)
            by_head = both(N.gheads, layer)
            skips = jnp.broadcast_to(both(N.gskip, layer), (8, wide))
            skips = nn(two(skips), r.fold[...])[:1]
            gated_row = both(N.ggated, layer)
            gain_row = both(N.ggain, layer) / named[N.gain + str(layer)][...]

            def fill(ref):
                ref[...] = jnp.zeros(shape, F32)
                ref[: KCONV + 1, INNER:] = taps[: KCONV + 1, :PAIR]
                ref[KCONV + 2 :, :D] = gain_row
                for rank in range(seq):

                    @pl.when(r.spot[6] == rank)
                    def _():
                        cols = slice(rank * width, (rank + 1) * width)
                        ref[: KCONV + 1, cols] = taps[: KCONV + 1, PAIR : PAIR + width]
                        ref[KCONV + 1 : KCONV + 2, cols] = gated_row[:, :width]
                        row = []
                        for value in (by_head[0:1], by_head[1:2], skips):
                            if rank:
                                row.append(jnp.zeros((1, rank * heads), F32))
                            row.append(value[:, :heads])
                            if rank < seq - 1:
                                row.append(jnp.zeros((1, HEADS - (rank + 1) * heads), F32))
                        row.append(jnp.zeros((1, PAIR - 3 * HEADS), F32))
                        ref[KCONV + 1 : KCONV + 2, INNER:] = jnp.concatenate(row, axis=1)

            @pl.when(r.spot[0] == layer)
            def _():
                fill(r.mine)

            @pl.when(r.spot[0] != layer)
            def _():
                fill(r.give)

    return launch(
        N.pack,
        body,
        (1,),
        ins,
        [(N.mine, shape, F32, full(shape)), (N.give, shape, F32, full(shape))],
        micros=2,
    )


class Plan:
    def __init__(self):
        self.seq = lax.axis_size(N.seq)
        self.shards = lax.axis_size(N.wshard)
        self.half = self.seq // 2
        self.core = lax.axis_index(N.section)
        self.z = lax.axis_index(N.seq)
        self.w = lax.axis_index(N.wshard)
        self.batch = self.z // self.half
        self.place = self.z % self.half
        self.rank = 2 * self.place + self.core

    def send(self, value, route, cores=(0, 1)):
        pairs = []
        for c in range(2):
            for z in range(self.seq):
                for w in range(self.shards):
                    target = route(c, z, w)
                    if c in cores and target is not None:
                        source = (c * self.seq + z) * self.shards + w
                        tc, tz, tw = target
                        pairs.append((source, (tc * self.seq + tz) * self.shards + tw))
        return lax.ppermute(value, AXES, pairs)

    def swap(self, value, cores=(0, 1)):
        return self.send(value, lambda c, z, w: (1 - c, z, w), cores)

    def along(self, value, k, cores=(0, 1)):
        return self.send(value, lambda c, z, w: (c, z ^ k, w), cores)

    def first_side(self, value):
        return self.send(value, lambda c, z, w: (c, z, w ^ (1 + c)))

    def second_side(self, value):
        return self.send(value, lambda c, z, w: (c, z, w ^ (2 - c)))

    def own(self, first, second):
        return jnp.where(self.core == 0, first, second)

    def reach(self, near, far):
        pieces = [self.along(near, k) for k in range(1, self.half)]
        return near, pieces, self.along(far, self.half)

    def collect(self, reached, late):
        near, pieces, came = reached
        more = [self.along(came, k) for k in range(1, self.half)]
        mine = jnp.concatenate([near] + pieces + [came] + [after(piece, late) for piece in more], axis=0)
        return mine, self.swap(mine)

    def fold(self, terms):
        return add(terms.keep, self.swap(terms.away))

    def reduce(self, total, *marks):
        hop = 1
        while hop < self.half:
            total = add(total, after(self.along(total, hop), *marks))
            hop *= 2
        return total, self.swap(total)

    def chip_total(self, value):
        return value + self.swap(value)

    def total(self, value, *marks):
        hop = 1
        while hop < self.half:
            value = value + after(self.along(value, hop), *marks)
            hop *= 2
        return value

    def home(self, value, batch, layer):
        half = self.half

        def route(c, z, w):
            if z // half != batch:
                return None
            return (layer, 2 * (z % half) + c, w)

        return self.send(value, route)

    def gather_chips(self, value, share, *marks):
        pieces = [value[:share]]
        for k in range(1, self.seq):
            piece = self.along(value[k * share : (k + 1) * share], k)
            pieces.append(after(piece, *marks))
        half = self.half
        terms = [add(pieces[k], pieces[k + half]) for k in range(half)]
        if half == 2:
            even = self.place == 0
            ordered = [jnp.where(even, terms[0], terms[1]), jnp.where(even, terms[1], terms[0])]
            return jnp.stack(ordered)
        stacked = jnp.stack(terms)
        return stacked[self.place ^ jnp.arange(half)]


def add(first, second):
    return (first.astype(F32) + second.astype(F32)).astype(BF)


def after(value, *others):
    return lax.optimization_barrier((value,) + others)[0]


def pick(value, index, axis=0):
    return lax.dynamic_index_in_dim(value, index, axis, keepdims=False)


def cut(value, start, size, axis):
    return lax.dynamic_slice_in_dim(value, start, size, axis)


def on_device(
    ends_in,
    seq_lengths,
    deal_order,
    norm_w,
    in_w,
    conv_w,
    conv_b,
    dt_bias,
    a_log,
    d_skip,
    gnorm_w,
    out_w,
):
    plan = Plan()
    core = plan.core
    half = plan.half
    rank = plan.rank
    seq = plan.seq
    rows = ends_in.shape[3]
    total = rows * seq
    count = total // BLOCK
    heads = HEADS // seq
    width = heads * HEADDIM
    wide = max(width, LANES)
    side = 2 * wide + LANES
    first = 1 + core
    second = 2 - core
    spot = jnp.stack([core, plan.w, plan.z, plan.place, first, second, rank, plan.batch])
    spot = spot.astype(jnp.int32)

    def padded(value, size):
        return jnp.pad(value, ((0, 0), (0, size - value.shape[1])))

    held = prepare_in(spot, jnp.swapaxes(in_w, 1, 2), seq)
    came = plan.swap(held.give)
    chunk_parts = [plan.own(held.keep, came), plan.own(came, held.keep)]
    held = prepare_rest(after(spot, held.give), out_w, ends_in)
    came = plan.swap(held.end_give)
    end_parts = [plan.own(held.end_keep, came), plan.own(came, held.end_keep)]
    came = plan.swap(held.out_give)
    out_parts = [plan.own(held.out_keep, came), plan.own(came, held.out_keep)]
    half_rows = rows // 2

    order = pick(deal_order[:, 0], plan.batch)
    by_chip = order.reshape(seq, 2, half_rows)[plan.z ^ jnp.arange(seq)]
    orders = (
        pick(by_chip, core, 1).reshape(1, total // 2),
        pick(by_chip, 1 - core, 1).reshape(1, total // 2),
    )
    end_orders = (
        cut(order, rows * plan.z, rows, 0).reshape(rows, 1),
        cut(order, rows * (plan.z ^ half), rows, 0).reshape(rows, 1),
    )

    def give(value):
        return plan.swap(cut(value, (1 - core) * side, side + PAIR, value.ndim - 2))

    def in_weights(part):
        near = plan.first_side(part)
        beyond = plan.second_side(part)
        far = plan.second_side(near)
        theirs = (give(jnp.stack([part, near, beyond])), give(far))
        return assemble(spot, (part, near, beyond, far), theirs, wide, True), near, far

    def later_in_weights(part):
        every = lax.all_gather(part, N.wshard)
        return assemble(spot, (every,), (give(every),), wide, False)

    def chosen_rows(every):
        half_part = every.shape[1]
        if half == 2:
            mine = pick(every, rank)
            theirs = plan.swap(pick(every, rank ^ 1))
            return jnp.concatenate([plan.own(mine, theirs), plan.own(theirs, mine)], axis=0)
        other = plan.swap(every)
        whole = jnp.stack([plan.own(every, other), plan.own(other, every)], axis=1)
        whole = whole.reshape(8 * half_part, D)
        return jnp.pad(cut(whole, width * rank, width, 0), ((0, wide - width), (0, 0)))

    def out_weights(part, *marks):
        if half == 2:
            low_shard = plan.w // 2

            def route(c, z, w):
                return (c, z, w ^ 2) if w // 2 == z % half else None

            came = after(plan.send(part, route), *marks[:1])
            here = jnp.where(low_shard == plan.place, part, came)
            beside = after(plan.send(here, lambda c, z, w: (c, z, w ^ 1)), *marks[1:])
            same = plan.w % 2 == core
            mine = jnp.where(same, here, beside)
            theirs = plan.swap(jnp.where(same, beside, here))
            return jnp.concatenate([plan.own(mine, theirs), plan.own(theirs, mine)], axis=0)
        return chosen_rows(lax.all_gather(part, N.wshard))

    def reach(part):
        return plan.reach(pick(part, plan.batch), pick(part, 1 - plan.batch))

    w_first, in_near, in_far = in_weights(chunk_parts[0])
    near, pieces, came = reach(end_parts[0])
    started = plan.collect((near, pieces, after(came, in_far)), in_far)
    w_out_first = out_weights(after(out_parts[0], in_near))
    w_second = later_in_weights(after(chunk_parts[1], in_far))
    weights = [(w_first, w_out_first)]

    tokens = place(orders, started)

    lengths = pick(seq_lengths[:, 0], plan.batch)
    ends = jnp.cumsum(lengths)
    at = iota((total,), 0)
    passed = at[:, None] >= ends[None, :]
    label = jnp.sum(passed.astype(jnp.int32), axis=1)
    begin = jnp.max(jnp.where(passed, ends[None, :], 0), axis=1)
    finished = jnp.min(jnp.where(passed, total, ends[None, :]), axis=1)
    channel_head = iota((LANES, wide), 1) // HEADDIM
    hot = (channel_head == iota((LANES, wide), 0)).astype(BF)
    env = types.SimpleNamespace(
        pos=jnp.stack([label, at - begin, finished - 1 - at], axis=1),
        label_row=label.reshape(count, 1, BLOCK),
        spread=jnp.concatenate([hot, hot], axis=0),
        fold=jnp.concatenate([hot.T, hot.T], axis=0),
    )

    own_small = jnp.concatenate(
        [
            norm_w[0],
            conv_w[0].reshape(-1),
            conv_b[0],
            dt_bias[0],
            a_log[0],
            d_skip[0],
            gnorm_w[0],
        ]
    )
    other_small = plan.swap(own_small)
    sizes = (D, (KCONV + 1) * (INNER + PAIR), HEADS, HEADS, HEADS, INNER)

    def pieces_of(flat):
        pieces = []
        begin = 0
        for size in sizes:
            pieces.append(flat[begin : begin + size])
            begin += size
        return pieces

    def vectors_of(layer):
        flat = jnp.where(core == layer, own_small, other_small)
        gain, taps, dtb, log_rate, skip, gated = pieces_of(flat)
        taps = taps.reshape(KCONV + 1, INNER + PAIR)
        channels = jnp.concatenate(
            [taps[:, INNER:], padded(cut(taps, rank * width, width, 1), wide)], axis=1
        )

        def lanes(value):
            return padded(cut(value, rank * heads, heads, 0)[None], LANES)

        terms = jnp.concatenate([lanes(dtb), lanes(-jnp.exp(log_rate))], axis=0)
        skips = jnp.repeat(cut(skip, rank * heads, heads, 0), HEADDIM)[None]
        wides = jnp.concatenate([skips, cut(gated, rank * width, width, 0)[None]], axis=0)
        return {
            N.gain: gain[None],
            N.taps: jnp.pad(channels, ((0, 8 - KCONV - 1), (0, 0))),
            N.terms: jnp.pad(terms, ((0, 6), (0, 0))),
            N.wides: jnp.pad(wides, ((0, 6), (0, wide - width))),
        }

    vectors = [vectors_of(0), vectors_of(1)]

    kept = [[], []]
    rows_summed = [[], []]
    summed = [[], []]
    def pass_on(layer, part, turn, before, dout):
        carried = kept[layer][0] if part == 1 else None
        done = forward(
            layer, part, turn, env, tokens, before, weights[layer], vectors[layer], carried, dout
        )
        kept[layer].append(done)
        return done

    reached = reach(after(end_parts[1], *started))
    done = pass_on(0, 0, spot, None, None)
    near, pieces, came = reached
    came = after(came, done.rows)
    done.away = after(done.away, came)
    rows_low = plan.chip_total(done.rows)
    folded = plan.fold(done)
    mark = done.rows
    done = pass_on(0, 1, after(spot, folded, rows_low), None, None)
    w_out_second = out_weights(after(out_parts[1], w_out_first), mark, done.rows)
    weights.append((w_second, w_out_second))
    rows_summed[0].append(plan.total(rows_low, done.rows))
    summed[0].append(plan.reduce(folded, done.rows))
    cotangent = place(orders, plan.collect((near, pieces, came), done.rows))
    folded = plan.fold(done)
    rows_summed[0].append(plan.total(plan.chip_total(done.rows)))
    turn = after(spot, folded, rows_summed[0][1])
    done = pass_on(1, 0, turn, summed[0][0] + (rows_summed[0][0],), cotangent)
    summed[0].append(plan.reduce(folded, done.rows))
    rows_low = plan.chip_total(done.rows)
    turn = after(spot, rows_low)
    done = pass_on(1, 1, turn, summed[0][1] + (rows_summed[0][1],), cotangent)
    rows_summed[1].append(plan.total(rows_low, done.rows))
    rows_summed[1].append(plan.total(plan.chip_total(done.rows)))
    last_fold = after(plan.fold(done), *rows_summed[1])

    grads_summed = [[None, None], [None, None]]
    gated = [[None, None], [None, None]]
    scans = [[None, None], [None, None]]
    grad_parts = [[None, None], [None, None]]

    def ungate_part(layer, part, turn):
        above = types.SimpleNamespace(dout=cotangent)
        if layer == 0:
            above.grad = grads_summed[1][part]
            above.summed = summed[0][part]
            above.tokens = kept[1][part].next
            above.gain = vectors[1][N.gain]
        gated[layer][part] = ungate(
            layer,
            part,
            turn,
            kept[layer][part],
            rows_summed[layer][part],
            weights[layer][1],
            vectors[layer],
            above,
        )

    def scan_part(layer, part, turn):
        carried = scans[layer][1] if part == 0 else None
        scan = backward(
            part, turn, env, kept[layer][part], gated[layer][part], weights[layer][0], vectors[layer], carried
        )
        scans[layer][part] = scan
        return plan.fold(scan)

    def outer_of(layer):
        douts = [(cotangent, 0), (cotangent, 1)]
        if layer == 0:
            douts = [(item.dout, 0) for item in gated[0]]
        return [item.normed_out for item in gated[layer]], douts

    def normed_of(layer):
        return [item.normed for item in kept[layer]]

    def gates_of(layer):
        return [item.dgate for item in gated[layer]]

    def rests_of(layer):
        return [item.rest for item in scans[layer]]

    def first_hop(terms):
        return plan.first_side(terms.away)

    def first_add(terms, came):
        return add(terms.keep[0], came[0]), add(terms.keep[1], came[1])

    def finish_part(kind, part, turn, before):
        if kind == N.result:
            values = types.SimpleNamespace(
                summed=last_sums,
                rest=kept[1][part].next,
                rows=rows_summed[1][part],
                first=part * (count // 4),
            )
        else:
            values = types.SimpleNamespace(
                summed=grads_summed[0][part],
                rest=gated[0][part].dout,
                tokens=tokens,
                gain=vectors[0][N.gain],
                first=0,
            )
        values.count = count // 2
        return finish(kind, part, turn, end_orders, values, before)

    share = D // (4 * seq)
    gate_span = wide
    rest_span = side + PAIR - wide
    def homed(outs, layer, *marks):
        return add(
            after(plan.home(outs, 0, layer), *marks), after(plan.home(outs, 1, layer), *marks)
        )

    ungate_part(1, 0, spot)
    ungate_part(1, 1, spot)
    folded = scan_part(1, 1, spot)
    last_sums = plan.reduce(last_fold, scans[1][1].gskip, gated[1][0].ggated)
    upper = folded
    folded = scan_part(1, 0, after(spot, folded, *last_sums))
    mark = scans[1][0].gskip
    grads_summed[1][1] = plan.reduce(upper, mark)
    result = finish_part(N.result, 0, after(spot, mark), None)
    result = finish_part(N.result, 1, spot, result)
    terms = weight_grads(
        after(spot, result.own, folded),
        normed_of(1),
        (gates_of(1), rests_of(1)),
        seq,
        outer_of(1),
        width // 4,
    )
    came = first_hop(terms)
    grads_summed[1][0] = plan.reduce(folded, terms.away)
    ungate_part(0, 1, after(spot, terms.away))
    result_far = plan.along(result.across, half, (1,))
    folded = scan_part(0, 1, after(spot, gated[0][1].ggated, *grads_summed[1][0]))
    pair = first_add(terms, after(came, scans[0][1].gskip))
    given = plan.second_side(pair[1])
    ungate_part(0, 0, after(spot, folded, pair[1]))
    gate_terms = weight_grads(
        after(spot, gated[0][0].ggated), normed_of(0), (gates_of(0),), seq, outer_of(0), width // 4
    )
    gate_came = first_hop(gate_terms)
    grads_summed[0][1] = plan.reduce(folded, gate_terms.away)
    later_last = add(pair[0], after(given, gate_terms.away))
    start_grad = finish_part(N.grad, 1, after(spot, later_last), None)
    folded = scan_part(0, 0, after(spot, start_grad.own, result_far))
    mark = scans[0][0].gskip
    outs_later = homed(later_last[:, gate_span + rest_span :], 1)
    rest_terms = weight_grads(after(spot, mark, folded), normed_of(0), (rests_of(0),), seq)
    chips_later = plan.gather_chips(
        later_last[:, : gate_span + rest_span], share, rest_terms.away
    )
    came_later = plan.swap(chips_later, (0,))
    rest_came = first_hop(rest_terms)
    grads_summed[0][0] = plan.reduce(folded, rest_terms.away)
    gate_pair = first_add(gate_terms, after(gate_came, mark))
    gate_given = plan.second_side(gate_pair[1])
    rest_pair = first_add(rest_terms, rest_came)
    rest_given = plan.second_side(rest_pair[1])
    gate_last = add(gate_pair[0], after(gate_given, rest_terms.away))
    start_grad = finish_part(N.grad, 0, after(spot, rest_pair[1]), start_grad)
    rest_last = add(rest_pair[0], rest_given)
    joined = jnp.concatenate([gate_last[:, :gate_span], rest_last], axis=1)
    chips_first = plan.gather_chips(joined, share)
    weight_sums = [
        (homed(gate_last[:, gate_span:], 0, rest_last), chips_first, plan.swap(chips_first, (1,))),
        (outs_later, chips_later, came_later),
    ]

    grad_far = plan.along(start_grad.across, half, (0,))
    ends_out = settle(spot, (start_grad.own, grad_far, result.own, result_far))

    both_sides = []
    out_grads = []
    for layer in range(2):
        outs, chips, came = weight_sums[layer]
        size = width // 4
        pieces = [outs[k * size : (k + 1) * size] for k in range(D // wide)]
        out_grads.append(jnp.concatenate(pieces, axis=1).astype(F32))
        both_sides.append((chips, came) if layer == 0 else (came, chips))
    g_in = gather_columns(spot, both_sides, seq)
    g_out = plan.own(out_grads[0], out_grads[1])

    packed = pack(after(spot, folded), env.fold, [item[N.gain] for item in vectors], scans, gated, seq)
    sums = packed.mine + plan.swap(packed.give)
    sums = sums + after(plan.first_side(after(sums, rest_terms.away)), rest_pair[1])
    sums = sums + plan.second_side(after(sums, rest_last))
    hop = 1
    while hop < seq:
        sums = sums + after(plan.along(sums, hop), grad_far)
        hop *= 2
    heads_at = INNER + HEADS
    return (
        ends_out,
        sums[KCONV + 2 :, :D],
        g_in,
        sums[None, :KCONV],
        sums[KCONV][None],
        sums[KCONV + 1 : KCONV + 2, INNER:heads_at],
        sums[KCONV + 1 : KCONV + 2, heads_at : heads_at + HEADS],
        sums[KCONV + 1 : KCONV + 2, heads_at + HEADS : heads_at + 2 * HEADS],
        sums[KCONV + 1 : KCONV + 2, :INNER],
        g_out[None],
    )


def solution(mesh):
    placed = (
        P("section", None, "wshard", "seq", None),
        P(None, "wshard", None),
        P(None, "wshard", None),
        P("section", None),
        P("section", "wshard", None),
        P("section", None, None),
        P("section", None),
        P("section", None),
        P("section", None),
        P("section", None),
        P("section", None),
        P("section", "wshard", None),
    )
    return jax.shard_map(
        on_device,
        mesh=mesh,
        in_specs=placed,
        out_specs=(
            P("section", None, "wshard", "seq", None),
            P("section", None),
            P("section", ("seq", "wshard"), None),
            P("section", None, None),
            P("section", None),
            P("section", None),
            P("section", None),
            P("section", None),
            P("section", None),
            P("section", ("seq", "wshard"), None),
        ),
        check_vma=False,
    )
```
